32 devices in a mesh: dp: 16 (over z, x, core), tensor: 2 (over y).
Axes of the slice: x: 2, y: 2, z: 4, core: 2. Of those that a mesh axis runs over, the one named last changes fastest.
Arguments:
- inputs: bfloat16 [16, 1500, 1536], P('dp', 'tensor'), may hold values from -16 to 16
- text_states: bfloat16 [16, 64, 1536], P('dp'), may hold values from -4 to 4
- teacher: bfloat16 [16, 1500, 1536], P('dp', 'tensor'), may hold values from -16 to 16
- valid_frames: int32 [16, 1500], P('dp', 'tensor'), may hold values from 0 to 1, as said below
- self_norm_gain: bfloat16 [1536], P('dp'), may hold values from 0.5 to 1.5
- self_norm_bias: bfloat16 [1536], P('dp'), may hold values from -0.25 to 0.25
- self_query: bfloat16 [1536, 1536], P('dp', 'tensor'), may hold values from -0.15625 to 0.15625
- self_key: bfloat16 [1536, 1536], P('dp', 'tensor'), may hold values from -0.15625 to 0.15625
- self_value: bfloat16 [1536, 1536], P('dp', 'tensor'), may hold values from -0.15625 to 0.15625
- self_out: bfloat16 [1536, 1536], P('tensor', 'dp'), may hold values from -0.875 to 0.875
- cross_norm_gain: bfloat16 [1536], P('dp'), may hold values from 0.5 to 1.5
- cross_norm_bias: bfloat16 [1536], P('dp'), may hold values from -0.25 to 0.25
- cross_query: bfloat16 [1536, 1536], P('dp', 'tensor'), may hold values from -0.15625 to 0.15625
- cross_key: bfloat16 [1536, 1536], P('dp', 'tensor'), may hold values from -0.15625 to 0.15625
- cross_value: bfloat16 [1536, 1536], P('dp', 'tensor'), may hold values from -0.15625 to 0.15625
- cross_out: bfloat16 [1536, 1536], P('tensor', 'dp'), may hold values from -1.25 to 1.25
- feed_norm_gain: bfloat16 [1536], P('dp'), may hold values from 0.5 to 1.5
- feed_norm_bias: bfloat16 [1536], P('dp'), may hold values from -0.25 to 0.25
- feed_in: bfloat16 [1536, 6144], P('dp', 'tensor'), may hold values from -0.15625 to 0.15625
- feed_out: bfloat16 [6144, 1536], P('tensor', 'dp'), may hold values from -0.15625 to 0.15625
Outputs:
- distill_loss: float32 [], replicated
- layer_out: bfloat16 [16, 1500, 1536], P('dp', 'tensor')
- inputs_grad: float32 [16, 1500, 1536], P('dp', 'tensor')
- text_grad: float32 [16, 64, 1536], P('dp', None, 'tensor')
- self_norm_gain_grad: float32 [1536], P(('dp', 'tensor'))
- self_norm_bias_grad: float32 [1536], P(('dp', 'tensor'))
- self_query_grad: float32 [1536, 1536], P('dp', 'tensor')
- self_key_grad: float32 [1536, 1536], P('dp', 'tensor')
- self_value_grad: float32 [1536, 1536], P('dp', 'tensor')
- self_out_grad: float32 [1536, 1536], P('tensor', 'dp')
- cross_norm_gain_grad: float32 [1536], P(('dp', 'tensor'))
- cross_norm_bias_grad: float32 [1536], P(('dp', 'tensor'))
- cross_query_grad: float32 [1536, 1536], P('dp', 'tensor')
- cross_key_grad: float32 [1536, 1536], P('dp', 'tensor')
- cross_value_grad: float32 [1536, 1536], P('dp', 'tensor')
- cross_out_grad: float32 [1536, 1536], P('tensor', 'dp')
- feed_norm_gain_grad: float32 [1536], P(('dp', 'tensor'))
- feed_norm_bias_grad: float32 [1536], P(('dp', 'tensor'))
- feed_in_grad: float32 [1536, 6144], P('dp', 'tensor')
- feed_out_grad: float32 [6144, 1536], P('tensor', 'dp')
The draws below stay inside these ranges and needn't reach their ends.
Inputs may be any that keep to these rules, and one draw needn't show every extreme that they name: `valid_frames`: in each clip the valid frames form a prefix of at least 250 frames; the last clip is valid throughout.
All inputs are finite; a program needn't handle non-finite values.
Results may differ from the reference program's by a relative error of at most 0.02.
Values may be sent and summed in bfloat16 or wider, within the bound.
A program may use at most 512 MiB of HBM per device.

```python
import jax
import jax.numpy as jnp
from jax import lax

D = 1536
HEADS = 24
HEAD_DIM = 64
FF = 6144
TEXT = 64
FRAMES = 1500
CLIPS = 16
TOKENS = 24000


def draw_valid_frames(key, part):
    clip_index = jnp.arange(CLIPS, dtype=jnp.int32)
    lowest = FRAMES // 3
    base_length = lowest + clip_index * (FRAMES - lowest) // max(CLIPS - 1, 1)
    jitter = jax.random.randint(key, (CLIPS,), 0, max(FRAMES // 12, 3), dtype=jnp.int32)
    jitter = jitter * (clip_index < CLIPS - 1).astype(jnp.int32)
    length = jnp.maximum(base_length - jitter, 1)
    frame_index = jnp.arange(FRAMES, dtype=jnp.int32)
    return (frame_index[None, :] < length[:, None]).astype(jnp.int32)


def feature_spike(spike_key):
    clip_order = jax.random.permutation(spike_key, CLIPS)
    feature_block = jnp.arange(D, dtype=jnp.int32) * CLIPS // D
    return jnp.where(feature_block[None, :] == clip_order[:, None], 4.0, 1.0).astype(jnp.float32)


def draw_inputs(key, part):
    key = jax.random.fold_in(key, 11)
    spike_key, value_key = jax.random.split(key, 2)
    spike_table = feature_spike(spike_key)
    entries = jnp.clip(jax.random.normal(value_key, (CLIPS, FRAMES, D), jnp.float32), -4.0, 4.0)
    return (entries * spike_table[:, None, :]).astype(jnp.bfloat16)


def draw_text_states(key, part):
    key = jax.random.fold_in(key, 23)
    entries = jnp.clip(jax.random.normal(key, (CLIPS, TEXT, D), jnp.float32), -4.0, 4.0)
    return entries.astype(jnp.bfloat16)


def draw_teacher(key, part):
    key = jax.random.fold_in(key, 37)
    spike_key, value_key = jax.random.split(key, 2)
    spike_table = feature_spike(spike_key)
    entries = jnp.clip(jax.random.normal(value_key, (CLIPS, FRAMES, D), jnp.float32), -4.0, 4.0)
    return (entries * spike_table[:, None, :]).astype(jnp.bfloat16)


def shard_levels(rng, shape, pieces, least, largest):
    loudness = 1.0
    for axis_at, blocks in pieces:
        draws = jax.random.uniform(jax.random.fold_in(jax.random.fold_in(rng, 6), axis_at), (blocks,), jnp.float32, least / len(pieces), largest / len(pieces))
        loudness = loudness * jnp.repeat(jnp.exp(draws), shape[axis_at] // blocks).reshape((-1,) + (1,) * (len(shape) - 1 - axis_at))
    return loudness


def gaussian(stream_key, dims, deviation, reach, cuts=(), kind=jnp.bfloat16):
    loudness = shard_levels(stream_key, dims, cuts, -0.22, 0.18) if cuts else 1.0
    drawn = jax.random.normal(stream_key, dims, jnp.float32) * deviation * loudness
    return jnp.minimum(jnp.maximum(drawn, -reach), reach).astype(kind)


def setup_inputs(seed: int = 0) -> dict:
    splits = jax.random.split(jax.random.key(seed), 21)
    inputs = draw_inputs(jax.random.fold_in(splits[20], 71), 0)
    text_states = draw_text_states(jax.random.fold_in(splits[20], 71), 0)
    teacher = draw_teacher(jax.random.fold_in(splits[20], 71), 0)
    valid_frames = draw_valid_frames(jax.random.fold_in(splits[20], 71), 0)
    self_norm_gain = jnp.clip(1.0 + 0.1 * jax.random.normal(splits[4], (D,), jnp.float32), 0.5, 1.5).astype(jnp.bfloat16)
    self_norm_bias = gaussian(splits[5], (D,), 0.05, 0.25, ((0, 16),))
    self_query = gaussian(splits[6], (D, D), D ** -0.5, 0.15625, ((0, 16), (1, 2)))
    self_key = gaussian(splits[7], (D, D), D ** -0.5, 0.15625, ((0, 16), (1, 2)))
    self_value = gaussian(splits[8], (D, D), D ** -0.5, 0.15625, ((0, 16), (1, 2)))
    self_out = gaussian(splits[9], (D, D), (max(1, D // 32)) ** -0.5, 0.875, ((0, 2), (1, 16)))
    cross_norm_gain = jnp.clip(1.0 + 0.1 * jax.random.normal(splits[10], (D,), jnp.float32), 0.5, 1.5).astype(jnp.bfloat16)
    cross_norm_bias = gaussian(splits[11], (D,), 0.05, 0.25, ((0, 16),))
    cross_query = gaussian(splits[12], (D, D), D ** -0.5, 0.15625, ((0, 16), (1, 2)))
    cross_key = gaussian(splits[13], (D, D), D ** -0.5, 0.15625, ((0, 16), (1, 2)))
    cross_value = gaussian(splits[14], (D, D), D ** -0.5, 0.15625, ((0, 16), (1, 2)))
    cross_out = gaussian(splits[15], (D, D), (max(1, D // TEXT)) ** -0.5, 1.25, ((0, 2), (1, 16)))
    feed_norm_gain = jnp.clip(1.0 + 0.1 * jax.random.normal(splits[16], (D,), jnp.float32), 0.5, 1.5).astype(jnp.bfloat16)
    feed_norm_bias = gaussian(splits[17], (D,), 0.05, 0.25, ((0, 16),))
    feed_in = gaussian(splits[18], (D, FF), D ** -0.5, 0.15625, ((0, 16), (1, 2)))
    feed_out = gaussian(splits[19], (FF, D), (FF // 4) ** -0.5, 0.15625, ((0, 2), (1, 16)))
    return dict(inputs=inputs, text_states=text_states, teacher=teacher, valid_frames=valid_frames, self_norm_gain=self_norm_gain, self_norm_bias=self_norm_bias, self_query=self_query, self_key=self_key, self_value=self_value, self_out=self_out, cross_norm_gain=cross_norm_gain, cross_norm_bias=cross_norm_bias, cross_query=cross_query, cross_key=cross_key, cross_value=cross_value, cross_out=cross_out, feed_norm_gain=feed_norm_gain, feed_norm_bias=feed_norm_bias, feed_in=feed_in, feed_out=feed_out)


HIGHEST = lax.Precision.HIGHEST
NEGATIVE = -1e+30
EPSILON = 1e-05

@jax.custom_vjp
def low(v):
    return lax.optimization_barrier(v.astype(jnp.bfloat16)).astype(jnp.float32)

@jax.custom_vjp
def low_back(v):
    return v

def low_keep(v):
    return (low(v), None)

def low_pass(kept, grad):
    return (grad,)

def back_keep(v):
    return (v, None)

def back_low(kept, grad):
    return (low(grad),)
low.defvjp(low_keep, low_pass)
low_back.defvjp(back_keep, back_low)

def normalize(values, gain_vec, bias_vec):
    center = values - lax.optimization_barrier(jnp.mean(values, -1, keepdims=True))
    spread = lax.optimization_barrier(jnp.mean(center * center, -1, keepdims=True))
    return center * lax.rsqrt(spread + EPSILON) * gain_vec + bias_vec

def project(left, weight):
    return jnp.dot(left, weight, precision=HIGHEST)

def split_heads(values):
    return values.reshape(values.shape[0], HEADS, HEAD_DIM)

def self_attention(queries, keys_in, values_in):
    rows_block = FRAMES // 2
    score_scale = HEAD_DIM ** (-0.5)
    key_index = jnp.arange(FRAMES, dtype=jnp.int32)[None, :]

    def one_block(block_pair):
        block_queries, start_row = block_pair
        scores = jnp.einsum('qhd,khd->hqk', block_queries, keys_in, precision=HIGHEST) * score_scale
        row_index = start_row + jnp.arange(rows_block, dtype=jnp.int32)[:, None]
        scores = low_back(jnp.where(key_index <= row_index, scores, NEGATIVE))
        probs = low(jax.nn.softmax(scores, axis=-1))
        return jnp.einsum('hqk,khd->qhd', probs, values_in, precision=HIGHEST)
    starts = jnp.arange(2, dtype=jnp.int32) * rows_block
    blocks = lax.map(jax.checkpoint(one_block), (queries.reshape(2, rows_block, HEADS, HEAD_DIM), starts))
    return blocks.reshape(FRAMES, HEADS * HEAD_DIM)

def cross_attention(queries, keys_in, values_in):
    score_scale = HEAD_DIM ** (-0.5)
    scores = low_back(jnp.einsum('qhd,khd->hqk', queries, keys_in, precision=HIGHEST) * score_scale)
    probs = low(jax.nn.softmax(scores, axis=-1))
    return jnp.einsum('hqk,khd->qhd', probs, values_in, precision=HIGHEST).reshape(FRAMES, HEADS * HEAD_DIM)

def clip_layer(frames_in, text_in, params):
    self_norm_gain, self_norm_bias, self_query, self_key, self_value, self_out, cross_norm_gain, cross_norm_bias, cross_query, cross_key, cross_value, cross_out, feed_norm_gain, feed_norm_bias, feed_in, feed_out = params
    normed = low(normalize(frames_in, self_norm_gain, self_norm_bias))
    queries = low_back(low(project(normed, self_query)))
    keys_self = low_back(low(project(normed, self_key)))
    values_self = low_back(low(project(normed, self_value)))
    mixed = low_back(low(self_attention(split_heads(queries), split_heads(keys_self), split_heads(values_self))))
    after_self = frames_in + low_back(project(mixed, self_out))
    normed_cross = low(normalize(after_self, cross_norm_gain, cross_norm_bias))
    cross_queries = low_back(low(project(normed_cross, cross_query)))
    cross_keys = low_back(low(project(text_in, cross_key)))
    cross_values = low_back(low(project(text_in, cross_value)))
    mixed_cross = low_back(low(cross_attention(split_heads(cross_queries), split_heads(cross_keys), split_heads(cross_values))))
    after_cross = after_self + low_back(project(mixed_cross, cross_out))
    normed_feed = low(normalize(after_cross, feed_norm_gain, feed_norm_bias))
    hidden_pre = low_back(project(normed_feed, feed_in))
    hidden_act = low(jax.nn.gelu(hidden_pre, approximate=False))
    return after_cross + low_back(project(hidden_act, feed_out))

def reference(inputs, text_states, teacher, valid_frames, self_norm_gain, self_norm_bias, self_query, self_key, self_value, self_out, cross_norm_gain, cross_norm_bias, cross_query, cross_key, cross_value, cross_out, feed_norm_gain, feed_norm_bias, feed_in, feed_out):
    params = tuple((weight_arg.astype(jnp.float32) for weight_arg in (self_norm_gain, self_norm_bias, self_query, self_key, self_value, self_out, cross_norm_gain, cross_norm_bias, cross_query, cross_key, cross_value, cross_out, feed_norm_gain, feed_norm_bias, feed_in, feed_out)))
    inputs_float = inputs.astype(jnp.float32)
    text_float = text_states.astype(jnp.float32)
    teacher_float = teacher.astype(jnp.float32)
    valid_mask = valid_frames.astype(jnp.float32)[..., None]
    token_count = jnp.sum(valid_frames).astype(jnp.float32)

    def objective(frames_all, text_all, params_in):

        def one_clip(clip_pair):
            return clip_layer(clip_pair[0], clip_pair[1], params_in)
        outputs = lax.map(jax.checkpoint(one_clip), (frames_all, text_all))
        residual = outputs - teacher_float
        loss_value = jnp.sum(valid_mask * residual * residual) / (D * token_count)
        return (loss_value, outputs)
    (loss_value, outputs), pullback = jax.vjp(objective, inputs_float, text_float, params)
    loss_scale = float(D * TOKENS)
    grad_inputs, grad_text, grad_params = pullback((jnp.ones_like(loss_value) * loss_scale, jnp.zeros_like(outputs)))
    return (loss_value, outputs.astype(jnp.bfloat16), grad_inputs, grad_text, grad_params[0], grad_params[1], grad_params[2], grad_params[3], grad_params[4], grad_params[5], grad_params[6], grad_params[7], grad_params[8], grad_params[9], grad_params[10], grad_params[11], grad_params[12], grad_params[13], grad_params[14], grad_params[15])
```

```python
import functools

import jax
import jax.numpy as jnp
import numpy as np
from jax import lax
from jax.experimental import pallas as pl
from jax.experimental.pallas import tpu as pltpu
from jax.sharding import Mesh
from jax.sharding import PartitionSpec as P

HEAD_DIM = 64
LANES = 128
ROWS = 256
FLOAT = jnp.float32
BRAIN = jnp.bfloat16
NEGATIVE = -1e30
EPSILON = 1e-05
SCALE = HEAD_DIM ** (-0.5)
CHIPS = ("z", "x", "y")
MESH = pl.DeviceIdType.MESH


def swap_core(v):
    return lax.ppermute(v, "c", [(0, 1), (1, 0)])


def swap_clip(v):
    return lax.ppermute(v, ("c", "y"), [(0, 0), (1, 2), (2, 1), (3, 3)])


def ring_fit():
    return lax.axis_size("z") == 4 and lax.axis_size("x") == 2 and lax.axis_size("y") == 2


def by_chip(v):
    return v.reshape(4, 2, 2, v.shape[0] // 16, v.shape[1])


def joined(v):
    return v.reshape(-1, v.shape[-1])


def dot_nt(a, b, **kw):
    return lax.dot_general(a, b, (((1,), (1,)), ((), ())), preferred_element_type=FLOAT, **kw)


def dot_nn(a, b):
    return lax.dot_general(a, b, (((1,), (0,)), ((), ())), preferred_element_type=FLOAT)


def dot_tn(a, b):
    return lax.dot_general(a, b, (((0,), (0,)), ((), ())), preferred_element_type=FLOAT)


def attend_kernel(half, real, q_ref, k_ref, v_ref, o_ref, lse_ref):
    core = lax.axis_index("c")
    per_half = half // ROWS
    blocks = 2 * per_half
    lane = lax.broadcasted_iota(jnp.int32, (ROWS, LANES), 1)
    first = lane < HEAD_DIM
    rows_at = lax.broadcasted_iota(jnp.int32, (ROWS, ROWS), 0)
    cols_at = lax.broadcasted_iota(jnp.int32, (ROWS, ROWS), 1)

    def place(i):
        start = jnp.where(core == i // per_half, 0, half) + (i % per_half) * ROWS
        return pl.ds(pl.multiple_of(start, ROWS), ROWS)

    for i in range(blocks):
        queries = q_ref[place(i), :].astype(FLOAT) * SCALE
        outs = []
        logs = []
        for head in range(2):
            mine = first if head == 0 else jnp.logical_not(first)
            masked = jnp.where(mine, queries, 0.0).astype(BRAIN)
            scores = []
            for j in range(i + 1):
                s = dot_nt(masked, k_ref[place(j), :])
                if j == i:
                    s = jnp.where(cols_at <= rows_at, s, NEGATIVE)
                elif j == per_half - 1:
                    s = jnp.where(cols_at < real - (per_half - 1) * ROWS, s, NEGATIVE)
                scores.append(s)
            top = scores[0]
            for s in scores[1:]:
                top = jnp.maximum(top, s)
            top = jnp.max(top, 1, keepdims=True)
            total = None
            out = None
            for j in range(i + 1):
                e = jnp.exp(scores[j] - top)
                total = e if total is None else total + e
                term = dot_nn(e.astype(BRAIN), v_ref[place(j), :])
                out = term if out is None else out + term
            total = jnp.sum(total, 1, keepdims=True)
            outs.append(out / total)
            logs.append(top + jnp.log(total))
        o_ref[place(i), :] = jnp.where(first, outs[0], outs[1]).astype(BRAIN)
        both = jnp.where(lane == 0, logs[0], logs[1])
        lse_ref[0, :, i * ROWS : (i + 1) * ROWS] = both.T[:8, :]


def attend_self(q, k, v, real):
    rows, width = q.shape
    pairs = width // LANES
    spec = pl.BlockSpec((rows, LANES), lambda p: (0, p))
    return pl.pallas_call(
        functools.partial(attend_kernel, rows // 2, real),
        grid=(pairs,),
        in_specs=[spec, spec, spec],
        out_specs=[spec, pl.BlockSpec((1, 8, rows), lambda p: (p, 0, 0))],
        out_shape=[
            jax.ShapeDtypeStruct((rows, width), BRAIN),
            jax.ShapeDtypeStruct((pairs, 8, rows), FLOAT),
        ],
        compiler_params=pltpu.CompilerParams(vmem_limit_bytes=48 * 2**20),
        cost_estimate=pl.CostEstimate(
            flops=10 * rows * rows * width, bytes_accessed=8 * rows * width, transcendentals=0
        ),
        name="attend",
    )(q, k, v)


def attend_back_kernel(
    half, real, q_ref, k_ref, v_ref, do_ref, o_ref, lse_ref, dq_ref, dk_ref, dv_ref,
    dq_sum, dk_sum, dv_sum, inner, hook=None,
):
    core = lax.axis_index("c")
    per_half = half // ROWS
    blocks = 2 * per_half
    first = lax.broadcasted_iota(jnp.int32, (ROWS, LANES), 1) < HEAD_DIM
    key_at = lax.broadcasted_iota(jnp.int32, (ROWS, ROWS), 0)
    query_at = lax.broadcasted_iota(jnp.int32, (ROWS, ROWS), 1)
    pick = lax.broadcasted_iota(jnp.int32, (8, LANES), 1) // HEAD_DIM
    pick = (pick == lax.broadcasted_iota(jnp.int32, (8, LANES), 0)).astype(FLOAT)

    def place(i):
        start = jnp.where(core == i // per_half, 0, half) + (i % per_half) * ROWS
        return pl.ds(pl.multiple_of(start, ROWS), ROWS)

    for i in range(blocks):
        product = do_ref[place(i), :].astype(FLOAT) * o_ref[place(i), :].astype(FLOAT)
        inner[:, i * ROWS : (i + 1) * ROWS] = dot_nt(pick, product, precision=lax.Precision.HIGHEST)
    dq_sum[...] = jnp.zeros_like(dq_sum)

    for j in range(blocks):
        if hook is not None:
            hook(j)
        keys = k_ref[place(j), :]
        values = v_ref[place(j), :]
        dk_sum[...] = jnp.zeros_like(dk_sum)
        dv_sum[...] = jnp.zeros_like(dv_sum)

        def query_step(i, carry, j=j, keys=keys, values=values):
            rows = pl.ds(pl.multiple_of(i * ROWS, ROWS), ROWS)
            queries = q_ref[place(i), :].astype(FLOAT) * SCALE
            grads = do_ref[place(i), :].astype(FLOAT)
            dead = jnp.logical_and(key_at + j * ROWS >= real, key_at + j * ROWS < half)
            keep = jnp.logical_and(key_at + j * ROWS <= query_at + i * ROWS, jnp.logical_not(dead))
            dqs = []
            dk = dk_sum[...]
            dv = dv_sum[...]
            for head in range(2):
                mine = first if head == 0 else jnp.logical_not(first)
                q_m = jnp.where(mine, queries, 0.0).astype(BRAIN)
                do_m = jnp.where(mine, grads, 0.0).astype(BRAIN)
                s = dot_nt(keys, q_m)
                p = jnp.where(keep, jnp.exp(s - lse_ref[0, head : head + 1, rows]), 0.0)
                dp = dot_nt(values, do_m)
                ds = (p * (dp - inner[head : head + 1, rows])).astype(BRAIN)
                dv = dv + dot_nn(p.astype(BRAIN), do_m)
                dk = dk + dot_nn(ds, q_m)
                dqs.append(dot_tn(ds, keys))
            dk_sum[...] = dk
            dv_sum[...] = dv
            dq_sum[rows, :] += jnp.where(first, dqs[0], dqs[1])
            return carry

        lax.fori_loop(j, blocks, query_step, 0)
        dk_ref[place(j), :] = dk_sum[...].astype(BRAIN)
        dv_ref[place(j), :] = dv_sum[...].astype(BRAIN)

    for i in range(blocks):
        dq_ref[place(i), :] = (dq_sum[i * ROWS : (i + 1) * ROWS, :] * SCALE).astype(BRAIN)


def attend_self_back(q, k, v, do, o, lse, real):
    rows, width = q.shape
    pairs = width // LANES
    spec = pl.BlockSpec((rows, LANES), lambda p: (0, p))
    return pl.pallas_call(
        functools.partial(attend_back_kernel, rows // 2, real),
        grid=(pairs,),
        in_specs=[spec] * 5 + [pl.BlockSpec((1, 8, rows), lambda p: (p, 0, 0))],
        out_specs=[spec] * 3,
        scratch_shapes=[
            pltpu.VMEM((rows, LANES), FLOAT),
            pltpu.VMEM((ROWS, LANES), FLOAT),
            pltpu.VMEM((ROWS, LANES), FLOAT),
            pltpu.VMEM((8, rows), FLOAT),
        ],
        out_shape=[jax.ShapeDtypeStruct((rows, width), BRAIN)] * 3,
        compiler_params=pltpu.CompilerParams(vmem_limit_bytes=48 * 2**20),
        cost_estimate=pl.CostEstimate(
            flops=25 * rows * rows * width, bytes_accessed=16 * rows * width, transcendentals=0
        ),
        name="attend_back",
    )(q, k, v, do, o, lse)


ORDERS = ("zxy", "zyx", "xyz")
TICKS = 5


def whereabouts():
    z, x, c, y = (lax.axis_index(name) for name in ("z", "x", "c", "y"))
    return z, x, c, y, lax.rem(z + 1, 4), lax.rem(z + 3, 4), lax.rem(z + 2, 4)


def greet(c, y, up, down, x, cores):
    barrier = pltpu.get_barrier_semaphore()
    partners = [{"z": up}, {"z": down}, {"x": 1 - x}, {"y": 1 - y}]
    if cores:
        partners.append({"c": 1 - c})
    for partner in partners:
        pl.semaphore_signal(barrier, inc=1, device_id=partner, device_id_type=MESH)

    @pl.when(c != y)
    def _():
        pl.semaphore_signal(barrier, inc=1, device_id={"c": y, "y": c}, device_id_type=MESH)
        pl.semaphore_wait(barrier, len(partners) + 1)

    @pl.when(c == y)
    def _():
        pl.semaphore_wait(barrier, len(partners))


def one(i):
    return pl.ds(i, 1)


class Crossing:
    def __init__(self, c, y, send, recv, local):
        self.c, self.y, self.send, self.recv, self.local = c, y, send, recv, local
        self.used = 0

    def begin(self, src, dst):
        start, finish = self.prepare(src, dst)
        start()
        return finish

    def prepare(self, src, dst):
        at = self.used
        self.used += 1
        far = pltpu.make_async_remote_copy(
            src_ref=src, dst_ref=dst, send_sem=self.send.at[at], recv_sem=self.recv.at[at],
            device_id={"c": self.y, "y": self.c}, device_id_type=MESH,
        )
        near = pltpu.make_async_copy(src, dst, self.local.at[at])

        def start():
            @pl.when(self.c != self.y)
            def _():
                far.start()

            @pl.when(self.c == self.y)
            def _():
                near.start()

        def finish():
            @pl.when(self.c != self.y)
            def _():
                far.wait()

            @pl.when(self.c == self.y)
            def _():
                near.wait()

        return start, finish


def gather_events(where, slots, weights, send, recv):
    z, x, c, y, up, down, across = where
    every = slice(None)
    chains = []
    for number, (which, start, sizes) in enumerate(slots):
        ref = weights[which]
        ticks = [[] for _ in range(TICKS)]
        for kind, order in enumerate(ORDERS):
            size = sizes[kind]
            if size == 0:
                continue
            columns = pl.ds(start, size)
            start += size

            def copy(at, region, partner, ref=ref, columns=columns, kind=kind, number=number):
                view = ref.at[(*region, every, columns)]
                return pltpu.make_async_remote_copy(
                    src_ref=view, dst_ref=view, send_sem=send.at[number, kind, at],
                    recv_sem=recv.at[number, kind, at], device_id=partner, device_id_type=MESH,
                )

            if order == "xyz":
                by_x = copy(0, (one(z), one(x), one(y)), {"x": 1 - x})
                by_y = copy(1, (one(z), every, one(y)), {"y": 1 - y})
                rest = (every, every)
            else:
                rest = (one(x), one(y))
            z_up = copy(2, (one(z), *rest), {"z": up})
            z_down = copy(3, (one(z), *rest), {"z": down})
            z_more = copy(4, (one(down), *rest), {"z": up})
            if order == "xyz":
                ticks[0] += [by_x.start]
                ticks[1] += [by_x.wait, by_y.start]
                ticks[2] += [by_y.wait, z_up.start, z_down.start]
                ticks[3] += [z_up.wait, z_more.start]
                ticks[4] += [z_down.wait, z_more.wait]
            else:
                if order == "zxy":
                    near = copy(0, (every, one(x), one(y)), {"x": 1 - x})
                    far = copy(1, (every, every, one(y)), {"y": 1 - y})
                else:
                    near = copy(0, (every, one(x), one(y)), {"y": 1 - y})
                    far = copy(1, (every, one(x), every), {"x": 1 - x})
                ticks[0] += [z_up.start, z_down.start]
                ticks[1] += [z_up.wait, z_more.start]
                ticks[2] += [z_down.wait, z_more.wait, near.start]
                ticks[3] += [near.wait, far.start]
                ticks[4] += [far.wait]
        chains.append(ticks)
    return chains


def run_tick(chains, at):
    for number, ticks in enumerate(chains):
        if 0 <= at - number < TICKS:
            for event in ticks[at - number]:
                event()


def total_ticks(slots):
    return len(slots) + TICKS - 1


def gather_first_kernel(slots, count, *refs):
    blocks, (frames, target, text) = refs[:count], refs[count : count + 3]
    refs = refs[count + 3 :]
    weights, (frames_out, target_out, text_out) = refs[:count], refs[count : count + 3]
    send, recv, cross_send, cross_recv, cross_local, core_send, core_recv = refs[count + 3 :]
    where = whereabouts()
    z, x, c, y, up, down, across = where
    greet(c, y, up, down, x, True)
    crossing = Crossing(c, y, cross_send, cross_recv, cross_local)
    own = [crossing.begin(b, w.at[z, x, c]) for b, w in zip(blocks, weights)]
    frames_in = crossing.begin(frames, frames_out.at[0])
    text_in = crossing.begin(text, text_out)
    target_in = crossing.begin(target, target_out)
    chains = gather_events(where, slots, weights, send, recv)
    sibling = pltpu.make_async_remote_copy(
        src_ref=frames_out.at[0], dst_ref=frames_out.at[1], send_sem=core_send, recv_sem=core_recv,
        device_id={"c": 1 - c}, device_id_type=MESH,
    )
    seen = set()
    for at in range(total_ticks(slots)):
        if at < len(slots) and slots[at][0] not in seen:
            seen.add(slots[at][0])
            own[slots[at][0]]()
        run_tick(chains, at)
        if at == 3:
            frames_in()
            sibling.start()
    sibling.wait()
    text_in()
    target_in()


ANY = pl.BlockSpec(memory_space=pl.ANY)


def gather_first(blocks, frames, target, text, slots):
    count = len(blocks)
    rows = blocks[0].shape[0]
    crossings = count + 3
    shapes = [jax.ShapeDtypeStruct((4, 2, 2, rows, b.shape[1]), BRAIN) for b in blocks]
    shapes += [
        jax.ShapeDtypeStruct((2, *frames.shape), BRAIN),
        jax.ShapeDtypeStruct(target.shape, BRAIN),
        jax.ShapeDtypeStruct(text.shape, BRAIN),
    ]
    dma = pltpu.SemaphoreType.DMA
    return pl.pallas_call(
        functools.partial(gather_first_kernel, slots, count),
        out_shape=shapes,
        in_specs=[ANY] * (count + 3),
        out_specs=[ANY] * (count + 3),
        scratch_shapes=[
            dma((len(slots), 3, 5)), dma((len(slots), 3, 5)),
            dma((crossings,)), dma((crossings,)), dma((crossings,)), dma, dma,
        ],
        compiler_params=pltpu.CompilerParams(collective_id=1, has_side_effects=True),
        name="gather_first",
    )(*blocks, frames, target, text)


def gather_attend_kernel(slots, count, pairs, half, real, q_ref, k_ref, v_ref, *refs):
    blocks, o_ref, lse_ref = refs[:count], refs[count], refs[count + 1]
    weights = refs[count + 2 : 2 * count + 2]
    send, recv, cross_send, cross_recv, cross_local = refs[2 * count + 2 :]
    where = whereabouts()
    z, x, c, y, up, down, across = where
    crossing = Crossing(c, y, cross_send, cross_recv, cross_local)
    chains = gather_events(where, slots, weights, send, recv)
    ticks = total_ticks(slots)
    step = pl.program_id(0)

    @pl.when(step == 0)
    def _():
        greet(c, y, up, down, x, False)
        own = [crossing.begin(b, w.at[z, x, c]) for b, w in zip(blocks, weights)]
        for finish in own:
            finish()
        run_tick(chains, 0)
        run_tick(chains, 1)

    for turn in range(1, pairs):
        @pl.when(step == turn)
        def _(turn=turn):
            for at in range(2 + (turn - 1) * (ticks - 2) // (pairs - 1), 2 + turn * (ticks - 2) // (pairs - 1)):
                if at < ticks - 1:
                    run_tick(chains, at)

    attend_kernel(half, real, q_ref, k_ref, v_ref, o_ref, lse_ref)

    @pl.when(step == pairs - 1)
    def _():
        run_tick(chains, ticks - 1)


def gather_attend(q, k, v, real, blocks, slots):
    rows, width = q.shape
    pairs = width // LANES
    count = len(blocks)
    spec = pl.BlockSpec((rows, LANES), lambda p: (0, p))
    dma = pltpu.SemaphoreType.DMA
    return pl.pallas_call(
        functools.partial(gather_attend_kernel, slots, count, pairs, rows // 2, real),
        grid=(pairs,),
        in_specs=[spec, spec, spec] + [ANY] * count,
        out_specs=[spec, pl.BlockSpec((1, 8, rows), lambda p: (p, 0, 0))] + [ANY] * count,
        out_shape=[
            jax.ShapeDtypeStruct((rows, width), BRAIN),
            jax.ShapeDtypeStruct((pairs, 8, rows), FLOAT),
            *[jax.ShapeDtypeStruct((4, 2, 2, *b.shape), BRAIN) for b in blocks],
        ],
        scratch_shapes=[
            dma((len(slots), 3, 5)), dma((len(slots), 3, 5)), dma((count,)), dma((count,)), dma((count,)),
        ],
        compiler_params=pltpu.CompilerParams(
            collective_id=2, has_side_effects=True, vmem_limit_bytes=48 * 2**20
        ),
        name="gather_attend",
    )(q, k, v, *blocks)


def plus(*terms):
    total = terms[0].astype(FLOAT)
    for term in terms[1:]:
        total = total + term.astype(FLOAT)
    return total.astype(BRAIN)


def sum_scratch(slots, rows):
    shapes = []
    for _, _, sizes in slots:
        for kind, order in enumerate(ORDERS):
            size = sizes[kind]
            if size == 0:
                continue
            if order == "xyz":
                leads = [(2, 2, 2), (2, 2), (2, 2), (2, 2), (2,), ()]
            else:
                leads = [(4, 2), (4, 2), (4,), (), (), (), ()]
            shapes += [pltpu.VMEM((*lead, rows, size), BRAIN) for lead in leads]
    return shapes


def sum_events(where, slots, terms, outs, buffers, crossing, send, recv, local):
    z, x, c, y, up, down, across = where
    every = slice(None)
    chains = []
    taken = 0
    for number, (which, start, sizes) in enumerate(slots):
        ref, out = terms[which], outs[which]
        ticks = [[] for _ in range(TICKS + 1)]
        for kind, order in enumerate(ORDERS):
            size = sizes[kind]
            if size == 0:
                continue
            columns = pl.ds(start, size)
            start += size
            need = 6 if order == "xyz" else 7
            held = buffers[taken : taken + need]
            taken += need

            def copy(at, src, dst, partner, kind=kind, number=number):
                return pltpu.make_async_remote_copy(
                    src_ref=src, dst_ref=dst, send_sem=send.at[number, kind, at],
                    recv_sem=recv.at[number, kind, at], device_id=partner, device_id_type=MESH,
                )

            def view(*region, ref=ref, columns=columns):
                return ref.at[(*region, every, columns)]

            if order == "xyz":
                own, from_two, from_down, from_up, from_y, from_x = held
                load_a = pltpu.make_async_copy(view(z, every, every), own.at[0], local.at[number, kind, 0])
                load_b = pltpu.make_async_copy(view(down, every, every), own.at[1], local.at[number, kind, 1])
                s_three = copy(0, view(up, every, every), from_down, {"z": up})
                s_two = copy(1, view(across, every, every), from_two, {"z": down})
                s_one = copy(2, own.at[1], from_up, {"z": down})
                s_y = copy(3, own.at[0, every, 1 - y], from_y, {"y": 1 - y})
                s_x = copy(4, from_y.at[1 - x], from_x, {"x": 1 - x})

                def add_two(own=own, from_two=from_two):
                    for i in range(2):
                        for j in range(2):
                            own[1, i, j] = plus(own[1, i, j], from_two[i, j])

                def add_z(own=own, a=from_down, b=from_up):
                    for i in range(2):
                        for j in range(2):
                            own[0, i, j] = plus(own[0, i, j], a[i, j], b[i, j])

                def add_y(own=own, from_y=from_y):
                    for i in range(2):
                        from_y[i] = plus(own[0, i, y], from_y[i])

                def add_x(from_y=from_y, from_x=from_x):
                    from_x[...] = plus(from_y[x], from_x[...])

                ticks[0] += [load_a.start, load_b.start, s_three.start, s_two.start]
                ticks[1] += [s_two.wait, load_b.wait, add_two, s_one.start]
                ticks[2] += [s_three.wait, load_a.wait, s_one.wait, add_z, s_y.start]
                ticks[3] += [s_y.wait, add_y, s_x.start]
                ticks[4] += [s_x.wait, add_x]
                final = from_x
            else:
                own, from_first, from_second, from_two, from_down, from_up, total = held
                if order == "zxy":
                    mine, theirs = view(every, every, y), view(every, every, 1 - y)
                    first, second = {"y": 1 - y}, {"x": 1 - x}
                    side = x
                else:
                    mine, theirs = view(every, x, every), view(every, 1 - x, every)
                    first, second = {"x": 1 - x}, {"y": 1 - y}
                    side = y
                load = pltpu.make_async_copy(mine, own, local.at[number, kind, 0])
                s_first = copy(0, theirs, from_first, first)
                s_second = copy(1, own.at[every, 1 - side], from_second, second)
                s_three = copy(2, from_second.at[up], from_down, {"z": up})
                s_two = copy(3, from_second.at[across], from_two, {"z": down})
                s_one = copy(4, from_second.at[down], from_up, {"z": down})

                def add_first(own=own, got=from_first, side=side):
                    for i in range(4):
                        own[i, 1 - side] = plus(own[i, 1 - side], got[i, 1 - side])

                def add_second(own=own, got=from_first, more=from_second, side=side):
                    for i in range(4):
                        more[i] = plus(own[i, side], got[i, side], more[i])

                def add_two(more=from_second, two=from_two):
                    more[down] = plus(more[down], two[...])

                def add_z(more=from_second, a=from_down, b=from_up, total=total):
                    total[...] = plus(more[z], a[...], b[...])

                ticks[0] += [load.start, s_first.start]
                ticks[1] += [s_first.wait, load.wait, add_first, s_second.start]
                ticks[2] += [s_second.wait, add_second, s_three.start, s_two.start]
                ticks[3] += [s_two.wait, add_two, s_one.start]
                ticks[4] += [s_three.wait, s_one.wait, add_z]
                final = total

            leave, left = crossing.prepare(final, out.at[every, columns])
            ticks[4] += [leave]
            ticks[5] += [left]
        chains.append(ticks)
    return chains


def run_sum_tick(chains, at):
    for number, ticks in enumerate(chains):
        if 0 <= at - number < TICKS + 1:
            for event in ticks[at - number]:
                event()


def sum_attend_kernel(slots, count, pairs, half, real, q_ref, k_ref, v_ref, do_ref, o_ref, lse_ref, *refs):
    terms, frames = refs[:count], refs[count]
    refs = refs[count + 1 :]
    dq_ref, dk_ref, dv_ref = refs[:3]
    outs, frames_out = refs[3 : 3 + count], refs[3 + count]
    refs = refs[4 + count :]
    work, refs = refs[:4], refs[4:]
    send, recv, local, cross_send, cross_recv, cross_local = refs[:6]
    where = whereabouts()
    z, x, c, y, up, down, across = where
    crossing = Crossing(c, y, cross_send, cross_recv, cross_local)
    chains = sum_events(where, slots, terms, outs, refs[6:], crossing, send, recv, local)
    frames_start, frames_finish = crossing.prepare(frames, frames_out)
    ticks = len(slots) + TICKS
    step = pl.program_id(0)
    blocks = 2 * half // ROWS
    spots = {}
    for at in range(ticks - 1):
        spot = at * pairs * blocks // ticks
        spots.setdefault(spot, []).append(at)

    def hook(j):
        for turn in range(pairs):
            here = spots.get(turn * blocks + j, [])
            if here:
                @pl.when(step == turn)
                def _(here=here):
                    for at in here:
                        if at == 0:
                            greet(c, y, up, down, x, False)
                            frames_start()
                        run_sum_tick(chains, at)

    attend_back_kernel(
        half, real, q_ref, k_ref, v_ref, do_ref, o_ref, lse_ref, dq_ref, dk_ref, dv_ref, *work, hook=hook
    )

    @pl.when(step == pairs - 1)
    def _():
        run_sum_tick(chains, ticks - 1)
        frames_finish()


def sum_attend(q, k, v, do, o, lse, real, terms, frames, slots):
    rows, width = q.shape
    pairs = width // LANES
    count = len(terms)
    block = terms[0].shape[3]
    spec = pl.BlockSpec((rows, LANES), lambda p: (0, p))
    dma = pltpu.SemaphoreType.DMA
    crossings = 3 * len(slots) + 1
    return pl.pallas_call(
        functools.partial(sum_attend_kernel, slots, count, pairs, rows // 2, real),
        grid=(pairs,),
        in_specs=[spec] * 5
        + [pl.BlockSpec((1, 8, rows), lambda p: (p, 0, 0))] + [ANY] * (count + 1),
        out_specs=[spec] * 3 + [ANY] * (count + 1),
        out_shape=[jax.ShapeDtypeStruct((rows, width), BRAIN)] * 3
        + [jax.ShapeDtypeStruct((block, t.shape[4]), BRAIN) for t in terms]
        + [jax.ShapeDtypeStruct(frames.shape, BRAIN)],
        scratch_shapes=[
            pltpu.VMEM((rows, LANES), FLOAT), pltpu.VMEM((ROWS, LANES), FLOAT),
            pltpu.VMEM((ROWS, LANES), FLOAT), pltpu.VMEM((8, rows), FLOAT),
            dma((len(slots), 3, 5)), dma((len(slots), 3, 5)), dma((len(slots), 3, 2)),
            dma((crossings,)), dma((crossings,)), dma((crossings,)),
            *sum_scratch(slots, block),
        ],
        compiler_params=pltpu.CompilerParams(
            collective_id=3, has_side_effects=True, vmem_limit_bytes=58 * 2**20
        ),
        name="sum_attend",
    )(q, k, v, do, o, lse, *terms, frames)


def sum_last_kernel(slots, count, *refs):
    terms, (frames, vectors) = refs[:count], refs[count : count + 2]
    refs = refs[count + 2 :]
    outs, (frames_out, vectors_out) = refs[:count], refs[count : count + 2]
    refs = refs[count + 2 :]
    send, recv, local, cross_send, cross_recv, cross_local, v_send, v_recv, held, four = refs[:10]
    where = whereabouts()
    z, x, c, y, up, down, across = where
    greet(c, y, up, down, x, True)
    crossing = Crossing(c, y, cross_send, cross_recv, cross_local)
    chains = sum_events(where, slots, terms, outs, refs[10:], crossing, send, recv, local)
    frames_finish = crossing.begin(frames, frames_out)

    def copy(at, src, dst, partner):
        return pltpu.make_async_remote_copy(
            src_ref=src, dst_ref=dst, send_sem=v_send.at[at], recv_sem=v_recv.at[at],
            device_id=partner, device_id_type=MESH,
        )

    run_sum_tick(chains, 0)
    held[0] = vectors[...]
    for at, partner in enumerate(({"c": 1 - c}, {"y": 1 - y}, {"x": 1 - x})):
        hop = copy(at, held.at[2 * at], held.at[2 * at + 1], partner)
        hop.start()
        hop.wait()
        total = held[2 * at] + held[2 * at + 1]
        if at < 2:
            held[2 * at + 2] = total
        else:
            four[z] = total
    run_sum_tick(chains, 1)
    z_up, z_down = copy(3, four.at[z], four.at[z], {"z": up}), copy(4, four.at[z], four.at[z], {"z": down})
    z_more = copy(5, four.at[down], four.at[down], {"z": up})
    z_up.start()
    z_down.start()
    z_up.wait()
    z_more.start()
    for at in range(2, len(slots) + TICKS):
        run_sum_tick(chains, at)
    z_down.wait()
    z_more.wait()
    vectors_out[...] = (four[0] + four[1]) + (four[2] + four[3])
    frames_finish()


def sum_last(terms, frames, vectors, slots):
    count = len(terms)
    block = terms[0].shape[3]
    dma = pltpu.SemaphoreType.DMA
    crossings = 3 * len(slots) + 1
    whole = pl.BlockSpec(memory_space=pltpu.VMEM)
    return pl.pallas_call(
        functools.partial(sum_last_kernel, slots, count),
        in_specs=[ANY] * (count + 1) + [whole],
        out_specs=[ANY] * (count + 1) + [whole],
        out_shape=[jax.ShapeDtypeStruct((block, t.shape[4]), BRAIN) for t in terms]
        + [jax.ShapeDtypeStruct(frames.shape, BRAIN), jax.ShapeDtypeStruct(vectors.shape, FLOAT)],
        scratch_shapes=[
            dma((len(slots), 3, 5)), dma((len(slots), 3, 5)), dma((len(slots), 3, 2)),
            dma((crossings,)), dma((crossings,)), dma((crossings,)), dma((6,)), dma((6,)),
            pltpu.VMEM((6, *vectors.shape), FLOAT), pltpu.VMEM((4, *vectors.shape), FLOAT),
            *sum_scratch(slots, block),
        ],
        compiler_params=pltpu.CompilerParams(
            collective_id=4, has_side_effects=True, vmem_limit_bytes=58 * 2**20
        ),
        name="sum_last",
    )(*terms, frames, vectors)


def slots_of(widths):
    slots = []
    for which, width in enumerate(widths):
        tiles = width // LANES
        if tiles < 6:
            slots.append((which, 0, (width, 0, 0)))
        elif tiles == 6:
            sizes = (3, 2, 1) if len(slots) % 2 else (2, 3, 1)
            slots.append((which, 0, tuple(LANES * s for s in sizes)))
        else:
            for at in range(0, tiles, 8):
                here = min(8, tiles - at)
                many = -(-3 * here // 8)
                sizes = (many, min(many, here - many), max(0, here - 2 * many))
                slots.append((which, at * LANES, tuple(LANES * s for s in sizes)))
    return tuple(slots)


def normalize(values, gain_vec, bias_vec):
    center = values - jnp.mean(values, -1, keepdims=True)
    spread = jnp.mean(center * center, -1, keepdims=True)
    return center * lax.rsqrt(spread + EPSILON) * gain_vec + bias_vec


def norm_back(values, gain_vec, grads):
    center = values - jnp.mean(values, -1, keepdims=True)
    scale_row = lax.rsqrt(jnp.mean(center * center, -1, keepdims=True) + EPSILON)
    normal = center * scale_row
    scaled = grads * gain_vec
    inner = jnp.mean(scaled * normal, -1, keepdims=True)
    grad_values = scale_row * (scaled - jnp.mean(scaled, -1, keepdims=True) - normal * inner)
    return grad_values, jnp.sum(grads * normal, 0), jnp.sum(grads, 0)


def gelu_pair(u):
    half_erf = 0.5 * (1.0 + lax.erf(u * (0.5**0.5)))
    density = jnp.exp(-0.5 * u * u) * ((2.0 * np.pi) ** -0.5)
    return (u * half_erf).astype(BRAIN), (half_erf + u * density).astype(BRAIN)


def split_heads(values):
    return values.reshape(values.shape[0], -1, HEAD_DIM)


def merge_heads(values):
    return values.reshape(values.shape[0], -1)


def attend_cross(q, k, v):
    scores = jnp.einsum("qhd,khd->hqk", q, k, preferred_element_type=FLOAT) * SCALE
    top = jnp.max(scores, -1, keepdims=True)
    e = jnp.exp(scores - top)
    total = jnp.sum(e, -1, keepdims=True)
    probs = e / total
    out = jnp.einsum("hqk,khd->qhd", probs.astype(BRAIN), v, preferred_element_type=FLOAT)
    return merge_heads(out).astype(BRAIN), (top + jnp.log(total))[..., 0]


def attend_cross_back(q, k, v, do, lse):
    scores = jnp.einsum("qhd,khd->hqk", q, k, preferred_element_type=FLOAT) * SCALE
    probs = jnp.exp(scores - lse[..., None])
    dp = jnp.einsum("qhd,khd->hqk", do, v, preferred_element_type=FLOAT)
    inner = jnp.sum(probs * dp, -1, keepdims=True)
    ds = (probs * (dp - inner)).astype(BRAIN)
    dq = jnp.einsum("hqk,khd->qhd", ds, k, preferred_element_type=FLOAT) * SCALE
    dk = jnp.einsum("hqk,qhd->khd", ds, q, preferred_element_type=FLOAT) * SCALE
    dv = jnp.einsum("hqk,qhd->khd", probs.astype(BRAIN), do, preferred_element_type=FLOAT)
    return tuple(merge_heads(t).astype(BRAIN) for t in (dq, dk, dv))


def on_device(
    inputs, text_states, teacher, valid_frames,
    self_norm_gain, self_norm_bias, self_query, self_key, self_value, self_out,
    cross_norm_gain, cross_norm_bias, cross_query, cross_key, cross_value, cross_out,
    feed_norm_gain, feed_norm_bias, feed_in, feed_out,
):
    at_core, at_y = lax.axis_index("c"), lax.axis_index("y")
    real, width = inputs.shape[1], inputs.shape[2]
    half = -(-real // ROWS) * ROWS
    block = self_query.shape[0]

    fits = ring_fit()

    tiny = [self_norm_gain, self_norm_bias, cross_norm_gain, cross_norm_bias, feed_norm_gain, feed_norm_bias]
    count = jnp.sum(valid_frames)
    digits = jnp.stack([count // 64, count % 64]).astype(BRAIN)
    digits = jnp.where((jnp.arange(block) == 0)[:, None], digits[None, :], jnp.zeros((), BRAIN))
    tiny = jnp.pad(jnp.concatenate([jnp.stack(tiny, 1), digits], 1), ((0, 0), (0, LANES - 8)))
    early = [tiny, self_query, self_key, self_value, self_out.T, cross_out.T, cross_query, cross_key, cross_value]
    late = [feed_in, feed_out.T]
    early_slots = slots_of([v.shape[1] for v in early])
    late_slots = slots_of([v.shape[1] for v in late])

    def padded(v):
        return jnp.pad(v, ((0, half - real), (0, 0)))

    frames = padded(inputs[0])
    flags = jnp.pad(valid_frames[0][:, None].astype(BRAIN), ((0, 0), (0, LANES - 1)))
    target = padded(jnp.concatenate([teacher[0], flags], 1))
    if fits:
        *early, x_all, target, text = gather_first(early, frames, target, text_states[0], early_slots)
        early = [joined(v) for v in early]
        x_all = joined(x_all)
    else:
        early = [lax.all_gather(swap_clip(v), CHIPS, axis=0, tiled=True) for v in early]
        x_own = swap_clip(frames)
        x_all = jnp.concatenate([x_own, swap_core(x_own)], 0)
        target, text = swap_clip(target), swap_clip(text_states[0])
    tiny, w_q, w_k, w_v, w_so, w_co, w_cq, w_ck, w_cv = early
    counted = jnp.sum(tiny[:, 6:8].astype(FLOAT), 0)
    counted = counted[0] * 64.0 + counted[1]
    token_count = counted + swap_core(counted)
    gains = tiny.T.astype(FLOAT)
    valid = target[:, width : width + 1].astype(FLOAT)
    target = target[:, :width].astype(FLOAT)

    def both(own):
        return jnp.concatenate([own, swap_core(own)], 0)

    def summed(left, weight):
        far = dot_nt(left[half:], weight).astype(BRAIN)
        got = swap_core(far)
        return dot_nt(left[:half], weight) + got.astype(FLOAT)

    h1 = normalize(x_all.astype(FLOAT), gains[0], gains[1]).astype(BRAIN)
    q1 = dot_nn(h1, w_q).astype(BRAIN)
    k1 = dot_nn(h1, w_k).astype(BRAIN)
    v1 = dot_nn(h1, w_v).astype(BRAIN)
    if fits:
        o1, lse1, *late = gather_attend(q1, k1, v1, real, late, late_slots)
        w_fi, w_fo = (joined(v) for v in late)
    else:
        o1, lse1 = attend_self(q1, k1, v1, real)
        w_fi, w_fo = (lax.all_gather(swap_clip(v), CHIPS, axis=0, tiled=True) for v in late)
    x0 = x_all[:half].astype(FLOAT)
    x1 = x0 + summed(o1, w_so)
    h2 = both(normalize(x1, gains[2], gains[3]).astype(BRAIN))
    q2 = dot_nn(h2, w_cq).astype(BRAIN)
    k2 = dot_nn(text, w_ck).astype(BRAIN)
    v2 = dot_nn(text, w_cv).astype(BRAIN)
    o2, lse2 = attend_cross(split_heads(q2), split_heads(k2), split_heads(v2))
    x2 = x1 + summed(o2, w_co)
    h3 = both(normalize(x2, gains[4], gains[5]).astype(BRAIN))
    g, slope = gelu_pair(dot_nn(h3, w_fi))
    y = x2 + summed(g, w_fo)
    home = y.astype(BRAIN)
    deviation = y - target
    error = jnp.sum(valid * deviation * deviation)
    tokens_all = real * lax.axis_size(("z", "x", "c", "y"))
    dy = (2.0 * tokens_all / token_count) * valid * deviation

    dyb = both(dy.astype(BRAIN))
    fo_grad = dot_tn(dyb, g).astype(BRAIN)
    du = (slope.astype(FLOAT) * dot_nn(dyb, w_fo)).astype(BRAIN)
    fi_grad = dot_tn(h3, du).astype(BRAIN)
    term, gain3, bias3 = norm_back(x2, gains[4], summed(du, w_fi))
    dx2 = dy + term
    dx2b = both(dx2.astype(BRAIN))
    co_grad = dot_tn(dx2b, o2).astype(BRAIN)
    do2 = dot_nn(dx2b, w_co).astype(BRAIN)
    dq2, dk2, dv2 = attend_cross_back(
        split_heads(q2), split_heads(k2), split_heads(v2), split_heads(do2), lse2
    )
    cq_grad = dot_tn(h2, dq2).astype(BRAIN)
    ck_grad = dot_tn(text, dk2).astype(BRAIN)
    cv_grad = dot_tn(text, dv2).astype(BRAIN)
    text_part = (dot_nt(dk2, w_ck) + dot_nt(dv2, w_cv)).astype(BRAIN)
    text_mine = jnp.where(at_core == 0, text_part[:, : width // 2], text_part[:, width // 2 :])
    text_far = jnp.where(at_core == 0, text_part[:, width // 2 :], text_part[:, : width // 2])
    text_sum = text_mine.astype(FLOAT) + swap_core(text_far).astype(FLOAT)
    text_grad = swap_clip(text_sum.astype(BRAIN)).astype(FLOAT)[None]
    term, gain2, bias2 = norm_back(x1, gains[2], summed(dq2, w_cq))
    dx1 = dx2 + term
    dx1b = both(dx1.astype(BRAIN))
    so_grad = dot_tn(dx1b, o1).astype(BRAIN)
    do1 = dot_nn(dx1b, w_so).astype(BRAIN)
    wide = [fi_grad, fo_grad]
    if fits:
        dq1, dk1, dv1, *wide, home = sum_attend(
            q1, k1, v1, do1, o1, lse1, real, [by_chip(v) for v in wide], home, late_slots
        )
    else:
        dq1, dk1, dv1 = attend_self_back(q1, k1, v1, do1, o1, lse1, real)
        wide = [swap_clip(lax.psum_scatter(v, CHIPS, scatter_dimension=0, tiled=True)) for v in wide]
        home = swap_clip(home)
    layer_out = home[:real][None]
    fi_grad, fo_grad = (v.astype(FLOAT) for v in wide)
    dh1_far = dot_nt(dq1[half:], w_q) + dot_nt(dk1[half:], w_k) + dot_nt(dv1[half:], w_v)
    dh1_got = swap_core(dh1_far.astype(BRAIN))
    dh1 = dot_nt(dq1[:half], w_q) + dot_nt(dk1[:half], w_k) + dot_nt(dv1[:half], w_v)
    term, gain1, bias1 = norm_back(x0, gains[0], dh1 + dh1_got.astype(FLOAT))
    frames = (dx1 + term).astype(BRAIN)
    q_grad = dot_tn(h1, dq1).astype(BRAIN)
    k_grad = dot_tn(h1, dk1).astype(BRAIN)
    v_grad = dot_tn(h1, dv1).astype(BRAIN)

    vectors = jnp.stack([gain1, bias1, gain2, bias2, gain3, bias3])
    vectors = jnp.concatenate([vectors, jnp.full((2, width), error)], 0)
    grads = [so_grad, co_grad, cq_grad, ck_grad, cv_grad, q_grad, k_grad, v_grad]
    if fits:
        slots = slots_of([v.shape[1] for v in grads])
        *grads, frames, vectors = sum_last([by_chip(v) for v in grads], frames, vectors, slots)
    else:
        grads = [swap_clip(lax.psum_scatter(v, CHIPS, scatter_dimension=0, tiled=True)) for v in grads]
        frames = swap_clip(frames)
        vectors = lax.psum(vectors, ("z", "x", "c", "y"))
    so_grad, co_grad, cq_grad, ck_grad, cv_grad, q_grad, k_grad, v_grad = (v.astype(FLOAT) for v in grads)
    inputs_grad = frames[:real].astype(FLOAT)[None]
    loss = vectors[6, 0] / (width * token_count)
    mine = block // 2
    place = (lax.axis_index(("z", "x", "c")) * 2 + at_y) * mine
    norms = lax.dynamic_slice(vectors, (0, place), (8, mine))
    return (
        loss, layer_out, inputs_grad, text_grad,
        norms[0], norms[1], q_grad, k_grad, v_grad, so_grad.T,
        norms[2], norms[3], cq_grad, ck_grad, cv_grad, co_grad.T,
        norms[4], norms[5], fi_grad, fo_grad.T,
    )


def solution(mesh):
    outer = mesh.shape["dp"] // 4
    fine = Mesh(np.array(mesh.devices).reshape(outer, 2, 2, 2), ("z", "x", "c", "y"))
    dp = ("z", "x", "c")
    frames = P(dp, "y", None)
    vector, wide, tall = P(dp), P(dp, "y"), P("y", dp)
    small = P(("z", "x", "c", "y"))
    attention = (vector, vector, wide, wide, wide, tall)
    return jax.shard_map(
        on_device,
        mesh=fine,
        in_specs=(frames, P(dp, None, None), frames, P(dp, "y"), *attention, *attention, vector, vector, wide, tall),
        out_specs=(
            P(), frames, frames, P(dp, None, "y"),
            small, small, wide, wide, wide, tall,
            small, small, wide, wide, wide, tall,
            small, small, wide, tall,
        ),
        check_vma=False,
    )
```

```python
import functools

import jax
import jax.numpy as jnp
import numpy as np
from jax import lax
from jax.experimental import pallas as pl
from jax.experimental.pallas import tpu as pltpu
from jax.sharding import Mesh
from jax.sharding import PartitionSpec as P

HEAD_DIM = 64
LANES = 128
ROWS = 256
FLOAT = jnp.float32
BRAIN = jnp.bfloat16
NEGATIVE = -1e30
EPSILON = 1e-05
SCALE = HEAD_DIM ** (-0.5)
CHIPS = ("z", "x", "y")
MESH = pl.DeviceIdType.MESH


def swap_core(v):
    return lax.ppermute(v, "c", [(0, 1), (1, 0)])


def swap_clip(v):
    return lax.ppermute(v, ("c", "y"), [(0, 0), (1, 2), (2, 1), (3, 3)])


def ring_fit():
    return lax.axis_size("z") == 4 and lax.axis_size("x") == 2 and lax.axis_size("y") == 2


def by_chip(v):
    return v.reshape(4, 2, 2, v.shape[0] // 16, v.shape[1])


def joined(v):
    return v.reshape(-1, v.shape[-1])


def dot_nt(a, b, **kw):
    return lax.dot_general(a, b, (((1,), (1,)), ((), ())), preferred_element_type=FLOAT, **kw)


def dot_nn(a, b):
    return lax.dot_general(a, b, (((1,), (0,)), ((), ())), preferred_element_type=FLOAT)


def dot_tn(a, b):
    return lax.dot_general(a, b, (((0,), (0,)), ((), ())), preferred_element_type=FLOAT)


def attend_kernel(half, real, q_ref, k_ref, v_ref, o_ref, lse_ref):
    core = lax.axis_index("c")
    per_half = half // ROWS
    blocks = 2 * per_half
    lane = lax.broadcasted_iota(jnp.int32, (ROWS, LANES), 1)
    first = lane < HEAD_DIM
    rows_at = lax.broadcasted_iota(jnp.int32, (ROWS, ROWS), 0)
    cols_at = lax.broadcasted_iota(jnp.int32, (ROWS, ROWS), 1)

    def place(i):
        start = jnp.where(core == i // per_half, 0, half) + (i % per_half) * ROWS
        return pl.ds(pl.multiple_of(start, ROWS), ROWS)

    for i in range(blocks):
        queries = q_ref[place(i), :].astype(FLOAT) * SCALE
        outs = []
        logs = []
        for head in range(2):
            mine = first if head == 0 else jnp.logical_not(first)
            masked = jnp.where(mine, queries, 0.0).astype(BRAIN)
            scores = []
            for j in range(i + 1):
                s = dot_nt(masked, k_ref[place(j), :])
                if j == i:
                    s = jnp.where(cols_at <= rows_at, s, NEGATIVE)
                elif j == per_half - 1:
                    s = jnp.where(cols_at < real - (per_half - 1) * ROWS, s, NEGATIVE)
                scores.append(s)
            top = scores[0]
            for s in scores[1:]:
                top = jnp.maximum(top, s)
            top = jnp.max(top, 1, keepdims=True)
            total = None
            out = None
            for j in range(i + 1):
                e = jnp.exp(scores[j] - top)
                total = e if total is None else total + e
                term = dot_nn(e.astype(BRAIN), v_ref[place(j), :])
                out = term if out is None else out + term
            total = jnp.sum(total, 1, keepdims=True)
            outs.append(out / total)
            logs.append(top + jnp.log(total))
        o_ref[place(i), :] = jnp.where(first, outs[0], outs[1]).astype(BRAIN)
        both = jnp.where(lane == 0, logs[0], logs[1])
        lse_ref[0, :, i * ROWS : (i + 1) * ROWS] = both.T[:8, :]


def attend_self(q, k, v, real):
    rows, width = q.shape
    pairs = width // LANES
    spec = pl.BlockSpec((rows, LANES), lambda p: (0, p))
    return pl.pallas_call(
        functools.partial(attend_kernel, rows // 2, real),
        grid=(pairs,),
        in_specs=[spec, spec, spec],
        out_specs=[spec, pl.BlockSpec((1, 8, rows), lambda p: (p, 0, 0))],
        out_shape=[
            jax.ShapeDtypeStruct((rows, width), BRAIN),
            jax.ShapeDtypeStruct((pairs, 8, rows), FLOAT),
        ],
        compiler_params=pltpu.CompilerParams(vmem_limit_bytes=48 * 2**20),
        cost_estimate=pl.CostEstimate(
            flops=10 * rows * rows * width, bytes_accessed=8 * rows * width, transcendentals=0
        ),
        name="attend",
    )(q, k, v)


def attend_back_kernel(
    half, real, q_ref, k_ref, v_ref, do_ref, o_ref, lse_ref, dq_ref, dk_ref, dv_ref,
    dq_sum, dk_sum, dv_sum, inner, hook=None,
):
    core = lax.axis_index("c")
    per_half = half // ROWS
    blocks = 2 * per_half
    first = lax.broadcasted_iota(jnp.int32, (ROWS, LANES), 1) < HEAD_DIM
    key_at = lax.broadcasted_iota(jnp.int32, (ROWS, ROWS), 0)
    query_at = lax.broadcasted_iota(jnp.int32, (ROWS, ROWS), 1)
    pick = lax.broadcasted_iota(jnp.int32, (8, LANES), 1) // HEAD_DIM
    pick = (pick == lax.broadcasted_iota(jnp.int32, (8, LANES), 0)).astype(FLOAT)

    def place(i):
        start = jnp.where(core == i // per_half, 0, half) + (i % per_half) * ROWS
        return pl.ds(pl.multiple_of(start, ROWS), ROWS)

    for i in range(blocks):
        product = do_ref[place(i), :].astype(FLOAT) * o_ref[place(i), :].astype(FLOAT)
        inner[:, i * ROWS : (i + 1) * ROWS] = dot_nt(pick, product, precision=lax.Precision.HIGHEST)
    dq_sum[...] = jnp.zeros_like(dq_sum)

    for j in range(blocks):
        if hook is not None:
            hook(j)
        keys = k_ref[place(j), :]
        values = v_ref[place(j), :]
        dk_sum[...] = jnp.zeros_like(dk_sum)
        dv_sum[...] = jnp.zeros_like(dv_sum)

        def query_step(i, carry, j=j, keys=keys, values=values):
            rows = pl.ds(pl.multiple_of(i * ROWS, ROWS), ROWS)
            queries = q_ref[place(i), :].astype(FLOAT) * SCALE
            grads = do_ref[place(i), :].astype(FLOAT)
            dead = jnp.logical_and(key_at + j * ROWS >= real, key_at + j * ROWS < half)
            keep = jnp.logical_and(key_at + j * ROWS <= query_at + i * ROWS, jnp.logical_not(dead))
            dqs = []
            dk = dk_sum[...]
            dv = dv_sum[...]
            for head in range(2):
                mine = first if head == 0 else jnp.logical_not(first)
                q_m = jnp.where(mine, queries, 0.0).astype(BRAIN)
                do_m = jnp.where(mine, grads, 0.0).astype(BRAIN)
                s = dot_nt(keys, q_m)
                p = jnp.where(keep, jnp.exp(s - lse_ref[0, head : head + 1, rows]), 0.0)
                dp = dot_nt(values, do_m)
                ds = (p * (dp - inner[head : head + 1, rows])).astype(BRAIN)
                dv = dv + dot_nn(p.astype(BRAIN), do_m)
                dk = dk + dot_nn(ds, q_m)
                dqs.append(dot_tn(ds, keys))
            dk_sum[...] = dk
            dv_sum[...] = dv
            dq_sum[rows, :] += jnp.where(first, dqs[0], dqs[1])
            return carry

        lax.fori_loop(j, blocks, query_step, 0)
        dk_ref[place(j), :] = dk_sum[...].astype(BRAIN)
        dv_ref[place(j), :] = dv_sum[...].astype(BRAIN)

    for i in range(blocks):
        dq_ref[place(i), :] = (dq_sum[i * ROWS : (i + 1) * ROWS, :] * SCALE).astype(BRAIN)


def attend_self_back(q, k, v, do, o, lse, real):
    rows, width = q.shape
    pairs = width // LANES
    spec = pl.BlockSpec((rows, LANES), lambda p: (0, p))
    return pl.pallas_call(
        functools.partial(attend_back_kernel, rows // 2, real),
        grid=(pairs,),
        in_specs=[spec] * 5 + [pl.BlockSpec((1, 8, rows), lambda p: (p, 0, 0))],
        out_specs=[spec] * 3,
        scratch_shapes=[
            pltpu.VMEM((rows, LANES), FLOAT),
            pltpu.VMEM((ROWS, LANES), FLOAT),
            pltpu.VMEM((ROWS, LANES), FLOAT),
            pltpu.VMEM((8, rows), FLOAT),
        ],
        out_shape=[jax.ShapeDtypeStruct((rows, width), BRAIN)] * 3,
        compiler_params=pltpu.CompilerParams(vmem_limit_bytes=48 * 2**20),
        cost_estimate=pl.CostEstimate(
            flops=25 * rows * rows * width, bytes_accessed=16 * rows * width, transcendentals=0
        ),
        name="attend_back",
    )(q, k, v, do, o, lse)


ORDERS = ("zxy", "zyx", "xyz")
TICKS = 5
SUM_TIME = 1.6


def whereabouts():
    z, x, c, y = (lax.axis_index(name) for name in ("z", "x", "c", "y"))
    return z, x, c, y, lax.rem(z + 1, 4), lax.rem(z + 3, 4), lax.rem(z + 2, 4)


def greet(c, y, up, down, x, cores):
    barrier = pltpu.get_barrier_semaphore()
    partners = [{"z": up}, {"z": down}, {"x": 1 - x}, {"y": 1 - y}]
    if cores:
        partners.append({"c": 1 - c})
    for partner in partners:
        pl.semaphore_signal(barrier, inc=1, device_id=partner, device_id_type=MESH)

    @pl.when(c != y)
    def _():
        pl.semaphore_signal(barrier, inc=1, device_id={"c": y, "y": c}, device_id_type=MESH)
        pl.semaphore_wait(barrier, len(partners) + 1)

    @pl.when(c == y)
    def _():
        pl.semaphore_wait(barrier, len(partners))


def one(i):
    return pl.ds(i, 1)


class Crossing:
    def __init__(self, c, y, send, recv, local):
        self.c, self.y, self.send, self.recv, self.local = c, y, send, recv, local
        self.used = 0

    def begin(self, src, dst):
        start, finish = self.prepare(src, dst)
        start()
        return finish

    def prepare(self, src, dst):
        at = self.used
        self.used += 1
        far = pltpu.make_async_remote_copy(
            src_ref=src, dst_ref=dst, send_sem=self.send.at[at], recv_sem=self.recv.at[at],
            device_id={"c": self.y, "y": self.c}, device_id_type=MESH,
        )
        near = pltpu.make_async_copy(src, dst, self.local.at[at])

        def start():
            @pl.when(self.c != self.y)
            def _():
                far.start()

            @pl.when(self.c == self.y)
            def _():
                near.start()

        def finish():
            @pl.when(self.c != self.y)
            def _():
                far.wait()

            @pl.when(self.c == self.y)
            def _():
                near.wait()

        return start, finish


def gather_events(where, slots, weights, send, recv):
    z, x, c, y, up, down, across = where
    every = slice(None)
    chains = []
    for number, (which, start, sizes) in enumerate(slots):
        ref = weights[which]
        ticks = [[] for _ in range(TICKS)]
        for kind, order in enumerate(ORDERS):
            size = sizes[kind]
            if size == 0:
                continue
            columns = pl.ds(start, size)
            start += size

            def copy(at, region, partner, ref=ref, columns=columns, kind=kind, number=number):
                view = ref.at[(*region, every, columns)]
                return pltpu.make_async_remote_copy(
                    src_ref=view, dst_ref=view, send_sem=send.at[number, kind, at],
                    recv_sem=recv.at[number, kind, at], device_id=partner, device_id_type=MESH,
                )

            if order == "xyz":
                by_x = copy(0, (one(z), one(x), one(y)), {"x": 1 - x})
                by_y = copy(1, (one(z), every, one(y)), {"y": 1 - y})
                rest = (every, every)
            else:
                rest = (one(x), one(y))
            z_up = copy(2, (one(z), *rest), {"z": up})
            z_down = copy(3, (one(z), *rest), {"z": down})
            z_more = copy(4, (one(down), *rest), {"z": up})
            if order == "xyz":
                ticks[0] += [by_x.start]
                ticks[1] += [by_x.wait, by_y.start]
                ticks[2] += [by_y.wait, z_up.start, z_down.start]
                ticks[3] += [z_up.wait, z_more.start]
                ticks[4] += [z_down.wait, z_more.wait]
            else:
                if order == "zxy":
                    near = copy(0, (every, one(x), one(y)), {"x": 1 - x})
                    far = copy(1, (every, every, one(y)), {"y": 1 - y})
                else:
                    near = copy(0, (every, one(x), one(y)), {"y": 1 - y})
                    far = copy(1, (every, one(x), every), {"x": 1 - x})
                ticks[0] += [z_up.start, z_down.start]
                ticks[1] += [z_up.wait, z_more.start]
                ticks[2] += [z_down.wait, z_more.wait, near.start]
                ticks[3] += [near.wait, far.start]
                ticks[4] += [far.wait]
        chains.append(ticks)
    return chains


def run_tick(chains, at):
    for number, ticks in enumerate(chains):
        if 0 <= at - number < TICKS:
            for event in ticks[at - number]:
                event()


def total_ticks(slots):
    return len(slots) + TICKS - 1


def bring_own(crossing, where, slots, chains, blocks, weights):
    z, x, c = where[:3]
    for which, (block, weight) in enumerate(zip(blocks, weights)):
        start, finish = crossing.prepare(block, weight.at[z, x, c])
        number = [slot[0] for slot in slots].index(which)
        chains[number][0].insert(0, finish)
        yield start


ANY = pl.BlockSpec(memory_space=pl.ANY)
NEEDED_FIRST = 4


def gather_kernel(slots, count, real, *refs):
    blocks, (frames, text, target, block) = refs[:count], refs[count : count + 4]
    refs = refs[count + 4 :]
    weights, (own_out, text_out, target_out, block_out) = refs[:count], refs[count : count + 4]
    gains_ref, h_ref, q_ref, k_ref, v_ref, o_ref, lse_ref = refs[count + 4 : count + 11]
    send, recv, cross_send, cross_recv, cross_local, core_send, core_recv, loads, tiny, both, held = refs[count + 11 :]
    rows, width = h_ref.shape
    half = rows // 2
    pairs = q_ref.shape[1] // LANES
    where = whereabouts()
    z, x, c, y, up, down, across = where
    crossing = Crossing(c, y, cross_send, cross_recv, cross_local)
    chains = gather_events(where, slots, weights, send, recv)
    starts = list(bring_own(crossing, where, slots, chains, blocks, weights))
    frames_start, frames_finish = crossing.prepare(frames, both.at[0])
    moves = [crossing.prepare(*pair) for pair in ((text, text_out), (block, block_out), (target, target_out))]
    sibling = pltpu.make_async_remote_copy(
        src_ref=both.at[0], dst_ref=both.at[1], send_sem=core_send, recv_sem=core_recv,
        device_id={"c": 1 - c}, device_id_type=MESH,
    )
    keep = pltpu.make_async_copy(both.at[0], own_out, loads.at[4])
    fetch = [pltpu.make_async_copy(weights[0], tiny, loads.at[0])]
    fetch += [pltpu.make_async_copy(weights[i + 1], held.at[i], loads.at[i + 1]) for i in range(3)]

    def tick(at):
        for number in reversed(range(len(slots))):
            stage = at - number
            last = TICKS if number < NEEDED_FIRST else TICKS - 1
            if 0 <= stage < last:
                run_events(chains[number][stage])

    greet(c, y, up, down, x, True)
    for start in starts[:NEEDED_FIRST]:
        start()
    frames_start()
    for start in starts[NEEDED_FIRST:]:
        start()
    for start, _ in moves:
        start()
    ready = NEEDED_FIRST + TICKS - 1
    for at in range(ready):
        tick(at)
        if at == 3:
            frames_finish()
            sibling.start()
            keep.start()
        if at == ready - 4:
            fetch[0].start()
    for copy in fetch[1:]:
        copy.start()
    sibling.wait()
    fetch[0].wait()
    gains_ref[...] = tiny[...].reshape(width, LANES).astype(FLOAT).T[:8, :]

    def norm_step(i, carry):
        here = pl.ds(pl.multiple_of(i * LANES, LANES), LANES)
        for side in range(2):
            there = pl.ds(pl.multiple_of(side * half + i * LANES, LANES), LANES)
            h_ref[there, :] = normalize(both[side, here, :].astype(FLOAT), gains_ref[0:1, :], gains_ref[1:2, :]).astype(BRAIN)
        return carry

    lax.fori_loop(0, half // LANES, norm_step, 0)
    later = list(range(ready, len(slots) + TICKS - 2))
    tick(later.pop(0))
    for i, out in enumerate((q_ref, k_ref, v_ref)):
        fetch[i + 1].wait()

        def project_step(r, carry, i=i, out=out):
            here = pl.ds(pl.multiple_of(r * ROWS, ROWS), ROWS)
            out[here, :] = dot_nn(h_ref[here, :], held[i].reshape(width, -1)).astype(BRAIN)
            return carry

        lax.fori_loop(0, rows // ROWS, project_step, 0)
        if later:
            tick(later.pop(0))

    def pair_step(p, carry):
        for turn in range(pairs):
            if turn < len(later):
                @pl.when(p == turn)
                def _(turn=turn):
                    tick(later[turn])

        lanes = pl.ds(pl.multiple_of(p * LANES, LANES), LANES)
        every = slice(None)
        q, k, v, o = (ref.at[every, lanes] for ref in (q_ref, k_ref, v_ref, o_ref))
        attend_kernel(half, real, q, k, v, o, lse_ref.at[pl.ds(p, 1)])
        return carry

    lax.fori_loop(0, pairs, pair_step, 0)
    for at in later[pairs:]:
        tick(at)
    for ticks in chains[NEEDED_FIRST:]:
        run_events(ticks[TICKS - 1])
    keep.wait()
    for _, finish in moves:
        finish()


def gather(blocks, frames, text, target, block, real, slots):
    count = len(blocks)
    rows, width = 2 * frames.shape[0], frames.shape[1]
    share = blocks[1].shape[1]
    pairs = share // LANES
    crossings = count + 4
    dma = pltpu.SemaphoreType.DMA
    vmem = pl.BlockSpec(memory_space=pltpu.VMEM)
    heads = jax.ShapeDtypeStruct((rows, share), BRAIN)
    gathered = [jax.ShapeDtypeStruct((4, 2, 2, *b.shape), BRAIN) for b in blocks]
    return pl.pallas_call(
        functools.partial(gather_kernel, slots, count, real),
        out_shape=[
            *gathered,
            *[jax.ShapeDtypeStruct(v.shape, v.dtype) for v in (frames, text, target, block)],
            jax.ShapeDtypeStruct((8, width), FLOAT), jax.ShapeDtypeStruct((rows, width), BRAIN),
            heads, heads, heads, heads, jax.ShapeDtypeStruct((pairs, 8, rows), FLOAT),
        ],
        in_specs=[ANY] * (count + 4),
        out_specs=[ANY] * (count + 4) + [vmem] * 7,
        scratch_shapes=[
            dma((len(slots), 3, 5)), dma((len(slots), 3, 5)),
            dma((crossings,)), dma((crossings,)), dma((crossings,)), dma, dma, dma((5,)),
            pltpu.VMEM(gathered[0].shape, BRAIN), pltpu.VMEM((2, *frames.shape), BRAIN),
            pltpu.VMEM((3, *gathered[1].shape), BRAIN),
        ],
        compiler_params=pltpu.CompilerParams(
            collective_id=1, has_side_effects=True, vmem_limit_bytes=56 * 2**20
        ),
        name="gather",
    )(*blocks, frames, text, target, block)


def plus(*terms):
    total = terms[0].astype(FLOAT)
    for term in terms[1:]:
        total = total + term.astype(FLOAT)
    return total.astype(BRAIN)


def sum_scratch(slots, rows):
    shapes = []
    for _, _, sizes in slots:
        for kind, order in enumerate(ORDERS):
            size = sizes[kind]
            if size == 0:
                continue
            if order == "xyz":
                leads = [(2, 2, 2), (2, 2), (2, 2), (2, 2), (2,), ()]
            else:
                leads = [(4,), (4,), (), (), (), ()]
            shapes += [pltpu.VMEM((*lead, rows, size), BRAIN) for lead in leads]
    return shapes


def sum_landings(slots, rows):
    return [
        jax.ShapeDtypeStruct((4, 2, rows, sizes[kind]), BRAIN)
        for _, _, sizes in slots
        for kind, order in enumerate(ORDERS)
        if sizes[kind] and order != "xyz"
    ]


def sum_events(where, slots, terms, outs, landings, buffers, pads, crossing, send, recv, local):
    z, x, c, y, up, down, across = where
    every = slice(None)
    chains = []
    taken = landed = 0
    for number, (which, start, sizes) in enumerate(slots):
        ref, out = terms[which], outs[which]
        ticks = [[] for _ in range(TICKS + 1)]
        after, later = [], []
        for kind, order in enumerate(ORDERS):
            size = sizes[kind]
            if size == 0:
                continue
            columns = pl.ds(start, size)
            start += size
            need = 6
            held = buffers[taken : taken + need]
            taken += need

            def copy(at, src, dst, partner, kind=kind, number=number):
                return pltpu.make_async_remote_copy(
                    src_ref=src, dst_ref=dst, send_sem=send.at[number, kind, at],
                    recv_sem=recv.at[number, kind, at], device_id=partner, device_id_type=MESH,
                )

            def view(*region, ref=ref, columns=columns):
                return ref.at[(*region, every, columns)]

            if order == "xyz":
                own, from_two, from_down, from_up, from_y, from_x = held
                load_a = pltpu.make_async_copy(view(z, every, every), own.at[0], local.at[number, kind, 0])
                load_b = pltpu.make_async_copy(view(down, every, every), own.at[1], local.at[number, kind, 1])
                s_three = copy(0, view(up, every, every), from_down, {"z": up})
                s_two = copy(1, view(across, every, every), from_two, {"z": down})
                s_one = copy(2, own.at[1], from_up, {"z": down})
                s_y = copy(3, own.at[0, every, 1 - y], from_y, {"y": 1 - y})
                s_x = copy(4, from_y.at[1 - x], from_x, {"x": 1 - x})

                def add_two(own=own, from_two=from_two):
                    for i in range(2):
                        for j in range(2):
                            own[1, i, j] = plus(own[1, i, j], from_two[i, j])

                def add_z(own=own, a=from_down, b=from_up):
                    for i in range(2):
                        for j in range(2):
                            own[0, i, j] = plus(own[0, i, j], a[i, j], b[i, j])

                def add_y(own=own, from_y=from_y):
                    for i in range(2):
                        from_y[i] = plus(own[0, i, y], from_y[i])

                def add_x(from_y=from_y, from_x=from_x):
                    from_x[...] = plus(from_y[x], from_x[...])

                ticks[0] += [load_a.start, load_b.start, s_three.start, s_two.start]
                ticks[1] += [s_two.wait, load_b.wait, add_two, s_one.start]
                ticks[2] += [s_three.wait, load_a.wait, s_one.wait, add_z, s_y.start]
                ticks[3] += [s_y.wait, add_y, s_x.start]
                ticks[4] += [s_x.wait, add_x]
                final = from_x
            else:
                from_second, far, from_two, from_down, from_up, total = held
                landing = landings[landed]
                landed += 1
                mine_at, got_at = (pad.at[every, every, pl.ds(0, size)] for pad in pads[kind])
                mine_pad, got_pad = pads[kind]
                if order == "zxy":
                    mine, theirs = view(every, 1 - x, y), view(every, every, 1 - y)
                    first, second = {"y": 1 - y}, {"x": 1 - x}
                    side = x
                else:
                    mine, theirs = view(every, x, 1 - y), view(every, 1 - x, every)
                    first, second = {"x": 1 - x}, {"y": 1 - y}
                    side = y
                load_mine = pltpu.make_async_copy(mine, mine_at, local.at[number, kind, 0])
                load_got = pltpu.make_async_copy(landing.at[every, 1 - side], got_at, local.at[number, kind, 1])
                load_near = pltpu.make_async_copy(view(every, x, y), mine_at, local.at[number, kind, 2])
                load_rest = pltpu.make_async_copy(landing.at[every, side], got_at, local.at[number, kind, 3])
                s_first = copy(0, theirs, landing, first)
                s_second = copy(1, far, from_second, second)
                s_three = copy(2, from_second.at[up], from_down, {"z": up})
                s_two = copy(3, from_second.at[across], from_two, {"z": down})
                s_one = copy(4, from_second.at[down], from_up, {"z": down})

                def add_first(mine=mine_pad, got=got_pad, size=size, far=far):
                    for i in range(4):
                        far[i] = plus(mine[i, :, :size], got[i, :, :size])

                def add_second(mine=mine_pad, got=got_pad, size=size, more=from_second):
                    for i in range(4):
                        more[i] = plus(mine[i, :, :size], got[i, :, :size], more[i])

                def add_two(more=from_second, two=from_two):
                    more[down] = plus(more[down], two[...])

                def add_z(more=from_second, a=from_down, b=from_up, total=total):
                    total[...] = plus(more[z], a[...], b[...])

                ticks[0] += [s_first.start]
                ticks[1] += [s_first.wait, load_mine.start, load_got.start]
                after += [load_mine.wait, load_got.wait, add_first, s_second.start]
                ticks[2] += [s_second.wait, load_near.start, load_rest.start]
                later += [load_near.wait, load_rest.wait, add_second, s_three.start, s_two.start]
                ticks[3] += [s_two.wait, add_two, s_one.start]
                ticks[4] += [s_three.wait, s_one.wait, add_z]
                final = total

            leave, left = crossing.prepare(final, out.at[every, columns])
            ticks[4] += [leave]
            ticks[5] += [left]
        ticks[1] += after
        ticks[2] += later
        chains.append(ticks)
    return chains


def sum_order(count):
    shares = ((1, 0.5), (2, 0.27), (3, 0.08), (4, 0.1), (5, 0.05))
    order = []
    passed = 0.0
    for tick, part in shares:
        order += [(n, tick, passed + part * (n + 1) / count) for n in range(count)]
        passed += part
    return order


def run_events(events):
    for event in events:
        event()


def sum_kernel(slots, count, real, *refs):
    terms, refs = refs[:count], refs[count:]
    home, block, q, k, v, do, o, h, w_q, w_k, w_v, x0, dx1, lse, gains, vectors = refs[:16]
    refs = refs[16:]
    outs, (home_out, frames_out, block_out, vectors_out) = refs[: count + 3], refs[count + 3 : count + 7]
    refs = refs[count + 7 :]
    lands = len([1 for _, _, sizes in slots for kind, order in enumerate(ORDERS) if sizes[kind] and order != "xyz"])
    landings, refs = refs[:lands], refs[lands:]
    send, recv, local, cross_send, cross_recv, cross_local, v_send, v_recv, h_send, h_recv, loads = refs[:11]
    four, ring, pad_a, pad_b, pad_c, pad_d, grads, grad_terms, far, got, near = refs[11:22]
    half, width = x0.shape
    rows, share = q.shape
    pairs = share // LANES
    tiles = rows // ROWS
    quarter = width // 4
    where = whereabouts()
    z, x, c, y, up, down, across = where
    every = slice(None)
    crossing = Crossing(c, y, cross_send, cross_recv, cross_local)
    all_terms = [*terms, *(grad_terms.at[i] for i in range(3))]
    pads = ((pad_a, pad_b), (pad_c, pad_d))
    chains = sum_events(where, slots, all_terms, outs, landings, refs[22:], pads, crossing, send, recv, local)
    early = [n for n, slot in enumerate(slots) if slot[0] < count]
    late = [n for n, slot in enumerate(slots) if slot[0] >= count]
    home_start, home_finish = crossing.prepare(home, home_out)
    block_start, block_finish = crossing.prepare(block, block_out)
    frames_start, frames_finish = crossing.prepare(far, frames_out)
    greet(c, y, up, down, x, True)
    for n in early:
        run_events(chains[n][0])
    block_start()
    home_start()

    work = tiles * (tiles + 1) // 2
    times = [p + sum(tiles - i for i in range(j)) / work for p in range(pairs) for j in range(tiles)]
    times += [pairs + 0.5 * i for i in range(1, 5)]
    spots = {}
    for number, tick, part in sum_order(len(early)):
        due = part * SUM_TIME * pairs
        later = [i for i, time in enumerate(times) if time >= due]
        spots.setdefault(later[0] if later else len(times), []).append((early[number], tick))

    def at_spot(spot):
        for number, tick in spots.get(spot, []):
            run_events(chains[number][tick])

    def attention(pair_in, dq_sum, dk_sum, dv_sum, inner):
        def load(p, i):
            lanes = pl.ds(pl.multiple_of(p * LANES, LANES), LANES)
            slot = lax.rem(p, 2)
            source = (q, k, v, do, o)[i]
            return pltpu.make_async_copy(source.at[every, lanes], pair_in.at[slot, i], loads.at[slot, i])

        for i in range(5):
            load(0, i).start()

        def pair_step(p, carry):
            @pl.when(p + 1 < pairs)
            def _():
                for i in range(5):
                    load(p + 1, i).start()

            for i in range(5):
                load(p, i).wait()

            def hook(j):
                for turn in range(pairs):
                    if turn * tiles + j in spots:
                        @pl.when(p == turn)
                        def _(turn=turn):
                            at_spot(turn * tiles + j)

            lanes = pl.ds(pl.multiple_of(p * LANES, LANES), LANES)
            slot = lax.rem(p, 2)
            attend_back_kernel(
                half, real, *(pair_in.at[slot, i] for i in range(5)), lse.at[pl.ds(p, 1)],
                *(grads.at[i, every, lanes] for i in range(3)), dq_sum, dk_sum, dv_sum, inner, hook=hook,
            )
            return carry

        lax.fori_loop(0, pairs, pair_step, 0)

    pl.run_scoped(
        attention,
        pltpu.VMEM((2, 5, rows, LANES), BRAIN), pltpu.VMEM((rows, LANES), FLOAT),
        pltpu.VMEM((ROWS, LANES), FLOAT), pltpu.VMEM((ROWS, LANES), FLOAT), pltpu.VMEM((8, rows), FLOAT),
    )

    def exchange(part):
        columns = pl.ds(part * quarter, quarter)
        return pltpu.make_async_remote_copy(
            src_ref=far.at[every, columns], dst_ref=got.at[every, columns], send_sem=h_send.at[part],
            recv_sem=h_recv.at[part], device_id={"c": 1 - c}, device_id_type=MESH,
        )

    def projections(h_in, w_in):
        def load(part, i):
            slot = part % 2
            if i == 3:
                return pltpu.make_async_copy(h.at[every, pl.ds(part * quarter, quarter)], h_in.at[slot], loads.at[slot, 3])
            return pltpu.make_async_copy((w_q, w_k, w_v)[i].at[part], w_in.at[slot, i], loads.at[slot, i])

        for i in range(4):
            load(0, i).start()
        for part in range(4):
            if part < 3:
                for i in range(4):
                    load(part + 1, i).start()
            for i in range(4):
                load(part, i).wait()
            slot = part % 2
            columns = pl.ds(part * quarter, quarter)

            def grad_step(i, carry, part=part, slot=slot):
                product = dot_tn(h_in[slot], grads[i]).astype(BRAIN)
                grad_terms[i, part] = product.reshape(grad_terms.shape[2:])
                return carry

            def back_step(r, carry, slot=slot, columns=columns, out=None, base=0):
                here = pl.ds(pl.multiple_of(r * ROWS, ROWS), ROWS)
                there = pl.ds(pl.multiple_of(base + r * ROWS, ROWS), ROWS)
                total = dot_nt(grads[0, there, :], w_in[slot, 0].reshape(quarter, share))
                for i in (1, 2):
                    total = total + dot_nt(grads[i, there, :], w_in[slot, i].reshape(quarter, share))
                out[here, columns] = total.astype(out.dtype)
                return carry

            lax.fori_loop(0, half // ROWS, functools.partial(back_step, out=far, base=half), 0)
            exchange(part).start()
            lax.fori_loop(0, half // ROWS, functools.partial(back_step, out=near), 0)
            lax.fori_loop(0, 3, grad_step, 0)
            at_spot(pairs * tiles + part)

    pl.run_scoped(
        projections, pltpu.VMEM((2, rows, quarter), BRAIN), pltpu.VMEM((2, 3, *w_q.shape[1:]), BRAIN)
    )
    for n in late:
        run_events(chains[n][0])
    for part in range(4):
        exchange(part).wait()
    four[...] = vectors[...]

    def norm(x_in, dx_in):
        size = x_in.shape[1]

        def load(i):
            slot = lax.rem(i, 2)
            here = pl.ds(pl.multiple_of(i * size, size), size)
            return (
                pltpu.make_async_copy(x0.at[here], x_in.at[slot], loads.at[slot, 0]),
                pltpu.make_async_copy(dx1.at[here], dx_in.at[slot], loads.at[slot, 1]),
            )

        for copy in load(0):
            copy.start()

        def step(i, carry):
            @pl.when(i + 1 < half // size)
            def _():
                for copy in load(i + 1):
                    copy.start()

            for copy in load(i):
                copy.wait()
            slot = lax.rem(i, 2)
            here = pl.ds(pl.multiple_of(i * size, size), size)
            flow = near[here, :].astype(FLOAT) + got[here, :].astype(FLOAT)
            values, gain_sum, bias_sum = norm_back(x_in[slot].astype(FLOAT), gains[0:1, :], flow)
            far[here, :] = (dx_in[slot] + values).astype(BRAIN)
            four[0:1, :] += gain_sum[None, :]
            four[1:2, :] += bias_sum[None, :]
            return carry

        lax.fori_loop(0, half // size, step, 0)

    pl.run_scoped(norm, pltpu.VMEM((2, 96, width), BRAIN), pltpu.VMEM((2, 96, width), FLOAT))
    frames_start()

    def hop(at, src, dst, partner):
        return pltpu.make_async_remote_copy(
            src_ref=src, dst_ref=dst, send_sem=v_send.at[at], recv_sem=v_recv.at[at],
            device_id=partner, device_id_type=MESH,
        )

    held = ring
    held[0] = four[...]
    for at, partner in enumerate(({"c": 1 - c}, {"y": 1 - y}, {"x": 1 - x})):
        turn = hop(at, held.at[2 * at], held.at[2 * at + 1], partner)
        turn.start()
        turn.wait()
        total = held[2 * at] + held[2 * at + 1]
        if at < 2:
            held[2 * at + 2] = total
        else:
            held[6 + z] = total
    z_up = hop(3, held.at[6 + z], held.at[6 + z], {"z": up})
    z_down = hop(4, held.at[6 + z], held.at[6 + z], {"z": down})
    z_more = hop(5, held.at[6 + down], held.at[6 + down], {"z": up})
    z_up.start()
    z_down.start()
    z_up.wait()
    z_more.start()
    for number, tick in spots.get(len(times), []):
        run_events(chains[number][tick])
    for tick in range(1, TICKS + 1):
        for n in late:
            run_events(chains[n][tick])
    z_down.wait()
    z_more.wait()
    vectors_out[...] = (held[6] + held[7]) + (held[8] + held[9])
    home_finish()
    block_finish()
    frames_finish()


def sum_gradients(terms, home, block, attention, h, weights, x0, dx1, lse, gains, vectors, real, slots):
    count = len(terms)
    rows, share = attention[0].shape
    half, width = x0.shape
    size = terms[0].shape[3]
    crossings = 3 * len(slots) + 3
    dma = pltpu.SemaphoreType.DMA
    vmem = pl.BlockSpec(memory_space=pltpu.VMEM)
    landings = sum_landings(slots, size)
    widths = [t.shape[4] for t in terms] + [share] * 3
    most = [max(sizes[kind] for _, _, sizes in slots) for kind in range(2)]
    results = pl.pallas_call(
        functools.partial(sum_kernel, slots, count, real),
        in_specs=[ANY] * (count + 13) + [vmem] * 3,
        out_specs=[ANY] * (count + 6) + [vmem] + [ANY] * len(landings),
        out_shape=[jax.ShapeDtypeStruct((size, n), BRAIN) for n in widths]
        + [jax.ShapeDtypeStruct(home.shape, BRAIN), jax.ShapeDtypeStruct(x0.shape, BRAIN)]
        + [jax.ShapeDtypeStruct(block.shape, BRAIN), jax.ShapeDtypeStruct(vectors.shape, FLOAT)]
        + landings,
        scratch_shapes=[
            dma((len(slots), 3, 5)), dma((len(slots), 3, 5)), dma((len(slots), 3, 4)),
            dma((crossings,)), dma((crossings,)), dma((crossings,)), dma((6,)), dma((6,)),
            dma((4,)), dma((4,)), dma((2, 5)),
            pltpu.VMEM(vectors.shape, FLOAT), pltpu.VMEM((10, *vectors.shape), FLOAT),
            *[pltpu.VMEM((4, size, most[kind]), BRAIN) for kind in (0, 0, 1, 1)],
            pltpu.VMEM((3, rows, share), BRAIN), pltpu.VMEM((3, 4, 2, 2, size, share), BRAIN),
            pltpu.VMEM((half, width), BRAIN), pltpu.VMEM((half, width), BRAIN), pltpu.VMEM((half, width), BRAIN),
            *sum_scratch(slots, size),
        ],
        compiler_params=pltpu.CompilerParams(
            collective_id=3, has_side_effects=True, vmem_limit_bytes=58 * 2**20
        ),
        name="sum_gradients",
    )(*terms, home, block, *attention, h, *weights, x0, dx1, lse, gains, vectors)
    return results[: count + 7]


def slots_of(widths, six=((1, 4, 1), (0, 4, 2), (1, 4, 1)), eight=(1, 5, 2), last=None):
    slots = []
    for which, width in enumerate(widths):
        tiles = width // LANES
        ways = last if last and which >= len(widths) - 3 else six
        if tiles == 6:
            slots.append((which, 0, tuple(LANES * n for n in ways[len(slots) % len(ways)])))
        elif tiles % 8 == 0:
            for at in range(0, tiles, 8):
                slots.append((which, at * LANES, tuple(LANES * n for n in eight)))
        else:
            slots.append((which, 0, (width, 0, 0)))
    return tuple(slots)


def normalize(values, gain_vec, bias_vec):
    center = values - jnp.mean(values, -1, keepdims=True)
    spread = jnp.mean(center * center, -1, keepdims=True)
    return center * lax.rsqrt(spread + EPSILON) * gain_vec + bias_vec


def norm_back(values, gain_vec, grads):
    center = values - jnp.mean(values, -1, keepdims=True)
    scale_row = lax.rsqrt(jnp.mean(center * center, -1, keepdims=True) + EPSILON)
    normal = center * scale_row
    scaled = grads * gain_vec
    inner = jnp.mean(scaled * normal, -1, keepdims=True)
    grad_values = scale_row * (scaled - jnp.mean(scaled, -1, keepdims=True) - normal * inner)
    return grad_values, jnp.sum(grads * normal, 0), jnp.sum(grads, 0)


def gelu_pair(u):
    half_erf = 0.5 * (1.0 + lax.erf(u * (0.5**0.5)))
    density = jnp.exp(-0.5 * u * u) * ((2.0 * np.pi) ** -0.5)
    return (u * half_erf).astype(BRAIN), (half_erf + u * density).astype(BRAIN)


def split_heads(values):
    return values.reshape(values.shape[0], -1, HEAD_DIM)


def merge_heads(values):
    return values.reshape(values.shape[0], -1)


def attend_cross(q, k, v):
    scores = jnp.einsum("qhd,khd->hqk", q, k, preferred_element_type=FLOAT) * SCALE
    top = jnp.max(scores, -1, keepdims=True)
    e = jnp.exp(scores - top)
    total = jnp.sum(e, -1, keepdims=True)
    probs = e / total
    out = jnp.einsum("hqk,khd->qhd", probs.astype(BRAIN), v, preferred_element_type=FLOAT)
    return merge_heads(out).astype(BRAIN), (top + jnp.log(total))[..., 0]


def attend_cross_back(q, k, v, do, lse):
    scores = jnp.einsum("qhd,khd->hqk", q, k, preferred_element_type=FLOAT) * SCALE
    probs = jnp.exp(scores - lse[..., None])
    dp = jnp.einsum("qhd,khd->hqk", do, v, preferred_element_type=FLOAT)
    inner = jnp.sum(probs * dp, -1, keepdims=True)
    ds = (probs * (dp - inner)).astype(BRAIN)
    dq = jnp.einsum("hqk,khd->qhd", ds, k, preferred_element_type=FLOAT) * SCALE
    dk = jnp.einsum("hqk,qhd->khd", ds, q, preferred_element_type=FLOAT) * SCALE
    dv = jnp.einsum("hqk,qhd->khd", probs.astype(BRAIN), do, preferred_element_type=FLOAT)
    return tuple(merge_heads(t).astype(BRAIN) for t in (dq, dk, dv))


def on_device(
    inputs, text_states, teacher, valid_frames,
    self_norm_gain, self_norm_bias, self_query, self_key, self_value, self_out,
    cross_norm_gain, cross_norm_bias, cross_query, cross_key, cross_value, cross_out,
    feed_norm_gain, feed_norm_bias, feed_in, feed_out,
):
    at_core, at_y = lax.axis_index("c"), lax.axis_index("y")
    real, width = inputs.shape[1], inputs.shape[2]
    half = -(-real // ROWS) * ROWS
    block, share = self_query.shape
    hidden = feed_in.shape[1]

    fits = ring_fit()

    tiny = [self_norm_gain, self_norm_bias, cross_norm_gain, cross_norm_bias, feed_norm_gain, feed_norm_bias]
    count = jnp.sum(valid_frames)
    digits = jnp.stack([count // 64, count % 64]).astype(BRAIN)
    digits = jnp.where((jnp.arange(block) == 0)[:, None], digits[None, :], jnp.zeros((), BRAIN))
    tiny = jnp.pad(jnp.concatenate([jnp.stack(tiny, 1), digits], 1), ((0, 0), (0, LANES - 8)))
    weights = [
        tiny, self_query, self_key, self_value, self_out.T, cross_query, cross_key, cross_value, cross_out.T, feed_in
    ]
    feed_rows = feed_out.T

    def both(own):
        return jnp.concatenate([own, swap_core(own)], 0)

    def summed(left, weight):
        far = dot_nt(left[half:], weight).astype(BRAIN)
        got = swap_core(far)
        return dot_nt(left[:half], weight) + got.astype(FLOAT)

    def padded(v):
        return jnp.pad(v, ((0, half - real), (0, 0)))

    frames = padded(inputs[0])
    flags = jnp.pad(valid_frames[0][:, None].astype(BRAIN), ((0, 0), (0, LANES - 1)))
    target = padded(jnp.concatenate([teacher[0], flags], 1))
    if fits:
        slots = slots_of([v.shape[1] for v in weights])
        *weights, x_own, text, target, feed_rows, gains, h1, q1, k1, v1, o1, lse1 = gather(
            weights, frames, text_states[0], target, feed_rows, real, slots
        )
        weights = [joined(v) for v in weights]
    else:
        weights = [lax.all_gather(swap_clip(v), CHIPS, axis=0, tiled=True) for v in weights]
        x_own, text, target, feed_rows = (swap_clip(v) for v in (frames, text_states[0], target, feed_rows))
        gains = weights[0].T.astype(FLOAT)
        x_all = jnp.concatenate([x_own, swap_core(x_own)], 0)
        h1 = normalize(x_all.astype(FLOAT), gains[0], gains[1]).astype(BRAIN)
        q1, k1, v1 = (dot_nn(h1, w).astype(BRAIN) for w in weights[1:4])
        o1, lse1 = attend_self(q1, k1, v1, real)
    tiny, w_q, w_k, w_v, w_so, w_cq, w_ck, w_cv, w_co, w_fi = weights
    counted = jnp.sum(tiny[:, 6:8].astype(FLOAT), 0)
    counted = counted[0] * 64.0 + counted[1]
    token_count = counted + swap_core(counted)
    w_fo = lax.all_gather(feed_rows, CHIPS, axis=0, tiled=True)
    valid = target[:, width : width + 1].astype(FLOAT)
    target = target[:, :width].astype(FLOAT)
    x0 = x_own.astype(FLOAT)
    x1 = x0 + summed(o1, w_so)
    h2 = both(normalize(x1, gains[2], gains[3]).astype(BRAIN))
    q2 = dot_nn(h2, w_cq).astype(BRAIN)
    k2 = dot_nn(text, w_ck).astype(BRAIN)
    v2 = dot_nn(text, w_cv).astype(BRAIN)
    o2, lse2 = attend_cross(split_heads(q2), split_heads(k2), split_heads(v2))
    x2 = x1 + summed(o2, w_co)
    h3 = both(normalize(x2, gains[4], gains[5]).astype(BRAIN))
    g, slope = gelu_pair(dot_nn(h3, w_fi))
    y = x2 + summed(g, w_fo)
    home = y.astype(BRAIN)
    deviation = y - target
    error = jnp.sum(valid * deviation * deviation)
    tokens_all = real * lax.axis_size(("z", "x", "c", "y"))
    dy = (2.0 * tokens_all / token_count) * valid * deviation

    dyb = both(dy.astype(BRAIN))
    cut = hidden - share
    fo_grad = dot_tn(dyb, g[:, :cut]).astype(BRAIN)
    dyb, fo_grad = lax.optimization_barrier((dyb, fo_grad))
    fo_grad = lax.psum_scatter(fo_grad, CHIPS, scatter_dimension=0, tiled=True)
    fo_rest = dot_tn(dyb, g[:, cut:]).astype(BRAIN)
    du = (slope.astype(FLOAT) * dot_nn(dyb, w_fo)).astype(BRAIN)
    fi_grad = dot_tn(h3, du).astype(BRAIN)
    term, gain3, bias3 = norm_back(x2, gains[4], summed(du, w_fi))
    dx2 = dy + term
    dx2b = both(dx2.astype(BRAIN))
    co_grad = dot_tn(dx2b, o2).astype(BRAIN)
    do2 = dot_nn(dx2b, w_co).astype(BRAIN)
    dq2, dk2, dv2 = attend_cross_back(
        split_heads(q2), split_heads(k2), split_heads(v2), split_heads(do2), lse2
    )
    cq_grad = dot_tn(h2, dq2).astype(BRAIN)
    ck_grad = dot_tn(text, dk2).astype(BRAIN)
    cv_grad = dot_tn(text, dv2).astype(BRAIN)
    text_part = (dot_nt(dk2, w_ck) + dot_nt(dv2, w_cv)).astype(BRAIN)
    text_mine = jnp.where(at_core == 0, text_part[:, : width // 2], text_part[:, width // 2 :])
    text_far = jnp.where(at_core == 0, text_part[:, width // 2 :], text_part[:, : width // 2])
    text_sum = text_mine.astype(FLOAT) + swap_core(text_far).astype(FLOAT)
    text_grad = swap_clip(text_sum.astype(BRAIN)).astype(FLOAT)[None]
    term, gain2, bias2 = norm_back(x1, gains[2], summed(dq2, w_cq))
    dx1 = dx2 + term
    dx1b = both(dx1.astype(BRAIN))
    so_grad = dot_tn(dx1b, o1).astype(BRAIN)
    do1 = dot_nn(dx1b, w_so).astype(BRAIN)
    zero = jnp.zeros((width,), FLOAT)
    vectors = jnp.stack([zero, zero, gain2, bias2, gain3, bias3])
    vectors = jnp.concatenate([vectors, jnp.full((2, width), error)], 0)
    grads = [fi_grad, fo_rest, co_grad, cq_grad, ck_grad, cv_grad, so_grad]
    if fits:
        slots = slots_of(
            [v.shape[1] for v in grads] + [w_q.shape[1]] * 3, six=((1, 4, 1), (1, 3, 2)), eight=(1, 5, 2), last=((0, 4, 2),)
        )
        *grads, home, frames, fo_grad, vectors = sum_gradients(
            [by_chip(v) for v in grads], home, fo_grad, (q1, k1, v1, do1, o1), h1,
            [by_chip(v) for v in (w_q, w_k, w_v)], x_own, dx1, lse1, gains, vectors, real, slots,
        )
    else:
        dq1, dk1, dv1 = attend_self_back(q1, k1, v1, do1, o1, lse1, real)
        dh1 = dot_nt(dq1, w_q) + dot_nt(dk1, w_k) + dot_nt(dv1, w_v)
        dh1 = dh1[:half] + swap_core(dh1[half:].astype(BRAIN)).astype(FLOAT)
        term, gain1, bias1 = norm_back(x0, gains[0], dh1)
        frames = swap_clip((dx1 + term).astype(BRAIN))
        grads += [dot_tn(h1, d).astype(BRAIN) for d in (dq1, dk1, dv1)]
        grads = [swap_clip(lax.psum_scatter(v, CHIPS, scatter_dimension=0, tiled=True)) for v in grads]
        home, fo_grad = swap_clip(home), swap_clip(fo_grad)
        vectors = lax.psum(vectors.at[:2].set(jnp.stack([gain1, bias1])), ("z", "x", "c", "y"))
    layer_out = home[:real][None]
    inputs_grad = frames[None].astype(FLOAT)[:, :real]
    fo_grad, *grads = (v.astype(FLOAT) for v in (fo_grad, *grads))
    fi_grad, fo_rest, co_grad, cq_grad, ck_grad, cv_grad, so_grad, q_grad, k_grad, v_grad = grads
    fo_grad = jnp.concatenate([fo_grad.T, fo_rest.T], 0)
    loss = vectors[6, 0] / (width * token_count)
    mine = block // 2
    place = (lax.axis_index(("z", "x", "c")) * 2 + at_y) * mine
    norms = lax.dynamic_slice(vectors, (0, place), (8, mine))
    return (
        loss, layer_out, inputs_grad, text_grad,
        norms[0], norms[1], q_grad, k_grad, v_grad, so_grad.T,
        norms[2], norms[3], cq_grad, ck_grad, cv_grad, co_grad.T,
        norms[4], norms[5], fi_grad, fo_grad,
    )


def solution(mesh):
    outer = mesh.shape["dp"] // 4
    fine = Mesh(np.array(mesh.devices).reshape(outer, 2, 2, 2), ("z", "x", "c", "y"))
    dp = ("z", "x", "c")
    frames = P(dp, "y", None)
    vector, wide, tall = P(dp), P(dp, "y"), P("y", dp)
    small = P(("z", "x", "c", "y"))
    attention = (vector, vector, wide, wide, wide, tall)
    return jax.shard_map(
        on_device,
        mesh=fine,
        in_specs=(frames, P(dp, None, None), frames, P(dp, "y"), *attention, *attention, vector, vector, wide, tall),
        out_specs=(
            P(), frames, frames, P(dp, None, "y"),
            small, small, wide, wide, wide, tall,
            small, small, wide, wide, wide, tall,
            small, small, wide, tall,
        ),
        check_vma=False,
    )
```

```python
import functools

import jax
import jax.numpy as jnp
import numpy as np
from jax import lax
from jax.experimental import pallas as pl
from jax.experimental.pallas import tpu as pltpu
from jax.sharding import Mesh
from jax.sharding import PartitionSpec as P

HEAD_DIM = 64
LANES = 128
ROWS = 256
FLOAT = jnp.float32
BRAIN = jnp.bfloat16
NEGATIVE = -1e30
EPSILON = 1e-05
SCALE = HEAD_DIM ** (-0.5)
CHIPS = ("z", "x", "y")
MESH = pl.DeviceIdType.MESH


def swap_core(v):
    return lax.ppermute(v, "c", [(0, 1), (1, 0)])


def swap_clip(v):
    return lax.ppermute(v, ("c", "y"), [(0, 0), (1, 2), (2, 1), (3, 3)])


def swap_others(v):
    return lax.ppermute(v, ("c", "y"), [(1, 2), (2, 1)])


def ring_fit():
    return lax.axis_size("z") == 4 and lax.axis_size("x") == 2 and lax.axis_size("y") == 2


def by_chip(v):
    return v.reshape(4, 2, 2, v.shape[0] // 16, v.shape[1])


def joined(v):
    return v.reshape(-1, v.shape[-1])


def dot_nt(a, b, **kw):
    return lax.dot_general(a, b, (((1,), (1,)), ((), ())), preferred_element_type=FLOAT, **kw)


def dot_nn(a, b):
    return lax.dot_general(a, b, (((1,), (0,)), ((), ())), preferred_element_type=FLOAT)


def dot_tn(a, b):
    return lax.dot_general(a, b, (((0,), (0,)), ((), ())), preferred_element_type=FLOAT)


def attend_kernel(half, real, q_ref, k_ref, v_ref, o_ref, lse_ref):
    core = lax.axis_index("c")
    per_half = half // ROWS
    blocks = 2 * per_half
    lane = lax.broadcasted_iota(jnp.int32, (ROWS, LANES), 1)
    first = lane < HEAD_DIM
    rows_at = lax.broadcasted_iota(jnp.int32, (ROWS, ROWS), 0)
    cols_at = lax.broadcasted_iota(jnp.int32, (ROWS, ROWS), 1)

    def place(i):
        start = jnp.where(core == i // per_half, 0, half) + (i % per_half) * ROWS
        return pl.ds(pl.multiple_of(start, ROWS), ROWS)

    for i in range(blocks):
        queries = q_ref[place(i), :].astype(FLOAT) * SCALE
        outs = []
        logs = []
        for head in range(2):
            mine = first if head == 0 else jnp.logical_not(first)
            masked = jnp.where(mine, queries, 0.0).astype(BRAIN)
            scores = []
            for j in range(i + 1):
                s = dot_nt(masked, k_ref[place(j), :])
                if j == i:
                    s = jnp.where(cols_at <= rows_at, s, NEGATIVE)
                elif j == per_half - 1:
                    s = jnp.where(cols_at < real - (per_half - 1) * ROWS, s, NEGATIVE)
                scores.append(s)
            top = scores[0]
            for s in scores[1:]:
                top = jnp.maximum(top, s)
            top = jnp.max(top, 1, keepdims=True)
            total = None
            out = None
            for j in range(i + 1):
                e = jnp.exp(scores[j] - top)
                total = e if total is None else total + e
                term = dot_nn(e.astype(BRAIN), v_ref[place(j), :])
                out = term if out is None else out + term
            total = jnp.sum(total, 1, keepdims=True)
            outs.append(out / total)
            logs.append(top + jnp.log(total))
        o_ref[place(i), :] = jnp.where(first, outs[0], outs[1]).astype(BRAIN)
        both = jnp.where(lane == 0, logs[0], logs[1])
        lse_ref[0, :, i * ROWS : (i + 1) * ROWS] = both.T[:8, :]


def attend_self(q, k, v, real):
    rows, width = q.shape
    pairs = width // LANES
    spec = pl.BlockSpec((rows, LANES), lambda p: (0, p))
    return pl.pallas_call(
        functools.partial(attend_kernel, rows // 2, real),
        grid=(pairs,),
        in_specs=[spec, spec, spec],
        out_specs=[spec, pl.BlockSpec((1, 8, rows), lambda p: (p, 0, 0))],
        out_shape=[
            jax.ShapeDtypeStruct((rows, width), BRAIN),
            jax.ShapeDtypeStruct((pairs, 8, rows), FLOAT),
        ],
        compiler_params=pltpu.CompilerParams(vmem_limit_bytes=48 * 2**20),
        cost_estimate=pl.CostEstimate(
            flops=10 * rows * rows * width, bytes_accessed=8 * rows * width, transcendentals=0
        ),
        name="attend",
    )(q, k, v)


def attend_back_kernel(
    half, real, q_ref, k_ref, v_ref, do_ref, o_ref, lse_ref, dq_ref, dk_ref, dv_ref,
    dq_sum, inner, q_two, do_two, hook=None,
):
    core = lax.axis_index("c")
    per_half = half // ROWS
    blocks = 2 * per_half
    first = lax.broadcasted_iota(jnp.int32, (ROWS, LANES), 1) < HEAD_DIM
    key_at = lax.broadcasted_iota(jnp.int32, (ROWS, 2 * ROWS), 0)
    query_at = lax.broadcasted_iota(jnp.int32, (ROWS, 2 * ROWS), 1) % ROWS
    pick = lax.broadcasted_iota(jnp.int32, (8, LANES), 1) // HEAD_DIM
    pick = (pick == lax.broadcasted_iota(jnp.int32, (8, LANES), 0)).astype(FLOAT)

    def place(i):
        start = jnp.where(core == i // per_half, 0, half) + (i % per_half) * ROWS
        return pl.ds(pl.multiple_of(start, ROWS), ROWS)

    def side_by_side(ref, i):
        return jnp.concatenate([ref[0:1, i * ROWS : (i + 1) * ROWS], ref[1:2, i * ROWS : (i + 1) * ROWS]], 1)

    for i in range(blocks):
        grads = do_ref[place(i), :].astype(FLOAT)
        queries = q_ref[place(i), :].astype(FLOAT) * SCALE
        product = grads * o_ref[place(i), :].astype(FLOAT)
        inner[:, i * ROWS : (i + 1) * ROWS] = dot_nt(pick, product, precision=lax.Precision.HIGHEST)
        q_two[i, :ROWS] = jnp.where(first, queries, 0.0).astype(BRAIN)
        q_two[i, ROWS:] = jnp.where(first, 0.0, queries).astype(BRAIN)
        do_two[i, :ROWS] = jnp.where(first, grads, 0.0).astype(BRAIN)
        do_two[i, ROWS:] = jnp.where(first, 0.0, grads).astype(BRAIN)
    dq_sum[...] = jnp.zeros_like(dq_sum)

    for j in range(blocks):
        if hook is not None:
            hook(j)
        keys = k_ref[place(j), :]
        values = v_ref[place(j), :]
        dk = dv = None
        for i in range(j, blocks):
            rows = pl.ds(i * ROWS, ROWS)
            q_m, do_m = q_two[i], do_two[i]
            s = dot_nt(keys, q_m) - side_by_side(lse_ref.at[0], i)
            if i == j:
                s = jnp.where(key_at <= query_at, s, NEGATIVE)
            elif j == per_half - 1:
                s = jnp.where(key_at < real - j * ROWS, s, NEGATIVE)
            p = jnp.exp(s)
            dp = dot_nt(values, do_m)
            ds = (p * (dp - side_by_side(inner, i))).astype(BRAIN)
            dv_term = dot_nn(p.astype(BRAIN), do_m)
            dk_term = dot_nn(ds, q_m)
            dk = dk_term if dk is None else dk + dk_term
            dv = dv_term if dv is None else dv + dv_term
            dq = dot_tn(ds, keys)
            dq_sum[rows, :] += jnp.where(first, dq[:ROWS], dq[ROWS:])
        dk_ref[place(j), :] = dk.astype(BRAIN)
        dv_ref[place(j), :] = dv.astype(BRAIN)

    for i in range(blocks):
        dq_ref[place(i), :] = (dq_sum[i * ROWS : (i + 1) * ROWS, :] * SCALE).astype(BRAIN)


def attend_self_back(q, k, v, do, o, lse, real):
    rows, width = q.shape
    pairs = width // LANES
    spec = pl.BlockSpec((rows, LANES), lambda p: (0, p))
    return pl.pallas_call(
        functools.partial(attend_back_kernel, rows // 2, real),
        grid=(pairs,),
        in_specs=[spec] * 5 + [pl.BlockSpec((1, 8, rows), lambda p: (p, 0, 0))],
        out_specs=[spec] * 3,
        scratch_shapes=[
            pltpu.VMEM((rows, LANES), FLOAT),
            pltpu.VMEM((8, rows), FLOAT),
            pltpu.VMEM((rows // ROWS, 2 * ROWS, LANES), BRAIN),
            pltpu.VMEM((rows // ROWS, 2 * ROWS, LANES), BRAIN),
        ],
        out_shape=[jax.ShapeDtypeStruct((rows, width), BRAIN)] * 3,
        compiler_params=pltpu.CompilerParams(vmem_limit_bytes=48 * 2**20),
        cost_estimate=pl.CostEstimate(
            flops=25 * rows * rows * width, bytes_accessed=16 * rows * width, transcendentals=0
        ),
        name="attend_back",
    )(q, k, v, do, o, lse)


ORDERS = ("zxy", "zyx", "xyz")
TICKS = 5
SUM_TIME = 3.3


def whereabouts():
    z, x, c, y = (lax.axis_index(name) for name in ("z", "x", "c", "y"))
    return z, x, c, y, lax.rem(z + 1, 4), lax.rem(z + 3, 4), lax.rem(z + 2, 4)


def greet(c, y, up, down, x, cores):
    barrier = pltpu.get_barrier_semaphore()
    partners = [{"z": up}, {"z": down}, {"x": 1 - x}, {"y": 1 - y}]
    if cores:
        partners.append({"c": 1 - c})
    for partner in partners:
        pl.semaphore_signal(barrier, inc=1, device_id=partner, device_id_type=MESH)

    @pl.when(c != y)
    def _():
        pl.semaphore_signal(barrier, inc=1, device_id={"c": y, "y": c}, device_id_type=MESH)
        pl.semaphore_wait(barrier, len(partners) + 1)

    @pl.when(c == y)
    def _():
        pl.semaphore_wait(barrier, len(partners))


def one(i):
    return pl.ds(i, 1)


class Crossing:
    def __init__(self, c, y, send, recv, local):
        self.c, self.y, self.send, self.recv, self.local = c, y, send, recv, local
        self.used = 0

    def begin(self, src, dst):
        start, finish = self.prepare(src, dst)
        start()
        return finish

    def prepare(self, src, dst):
        at = self.used
        self.used += 1
        far = pltpu.make_async_remote_copy(
            src_ref=src, dst_ref=dst, send_sem=self.send.at[at], recv_sem=self.recv.at[at],
            device_id={"c": self.y, "y": self.c}, device_id_type=MESH,
        )
        near = pltpu.make_async_copy(src, dst, self.local.at[at])

        def start():
            @pl.when(self.c != self.y)
            def _():
                far.start()

            @pl.when(self.c == self.y)
            def _():
                near.start()

        def finish():
            @pl.when(self.c != self.y)
            def _():
                far.wait()

            @pl.when(self.c == self.y)
            def _():
                near.wait()

        return start, finish


def gather_events(where, slots, weights, send, recv):
    z, x, c, y, up, down, across = where
    every = slice(None)
    chains = []
    for number, (which, start, sizes) in enumerate(slots):
        ref = weights[which]
        ticks = [[] for _ in range(TICKS)]
        for kind, order in enumerate(ORDERS):
            size = sizes[kind]
            if size == 0:
                continue
            columns = pl.ds(start, size)
            start += size

            def copy(at, region, partner, ref=ref, columns=columns, kind=kind, number=number):
                view = ref.at[(*region, every, columns)]
                return pltpu.make_async_remote_copy(
                    src_ref=view, dst_ref=view, send_sem=send.at[number, kind, at],
                    recv_sem=recv.at[number, kind, at], device_id=partner, device_id_type=MESH,
                )

            if order == "xyz":
                by_x = copy(0, (one(z), one(x), one(y)), {"x": 1 - x})
                by_y = copy(1, (one(z), every, one(y)), {"y": 1 - y})
                rest = (every, every)
            else:
                rest = (one(x), one(y))
            z_up = copy(2, (one(z), *rest), {"z": up})
            z_down = copy(3, (one(z), *rest), {"z": down})
            z_more = copy(4, (one(down), *rest), {"z": up})
            if order == "xyz":
                ticks[0] += [by_x.start]
                ticks[1] += [by_x.wait, by_y.start]
                ticks[2] += [by_y.wait, z_up.start, z_down.start]
                ticks[3] += [z_up.wait, z_more.start]
                ticks[4] += [z_down.wait, z_more.wait]
            else:
                if order == "zxy":
                    near = copy(0, (every, one(x), one(y)), {"x": 1 - x})
                    far = copy(1, (every, every, one(y)), {"y": 1 - y})
                else:
                    near = copy(0, (every, one(x), one(y)), {"y": 1 - y})
                    far = copy(1, (every, one(x), every), {"x": 1 - x})
                ticks[0] += [z_up.start, z_down.start]
                ticks[1] += [z_up.wait, z_more.start]
                ticks[2] += [z_down.wait, z_more.wait, near.start]
                ticks[3] += [near.wait, far.start]
                ticks[4] += [far.wait]
        chains.append(ticks)
    return chains


def run_tick(chains, at):
    for number, ticks in enumerate(chains):
        if 0 <= at - number < TICKS:
            for event in ticks[at - number]:
                event()


def total_ticks(slots):
    return len(slots) + TICKS - 1


def bring_own(crossing, where, slots, chains, blocks, weights):
    z, x, c = where[:3]
    for which, (block, weight) in enumerate(zip(blocks, weights)):
        start, finish = crossing.prepare(block, weight.at[z, x, c])
        number = [slot[0] for slot in slots].index(which)
        chains[number][0].insert(0, finish)
        yield start


ANY = pl.BlockSpec(memory_space=pl.ANY)
NEEDED_FIRST = 4


def gather_kernel(slots, count, real, *refs):
    blocks, (frames, text, target, block) = refs[:count], refs[count : count + 4]
    refs = refs[count + 4 :]
    weights, (own_out, text_out, target_out, block_out) = refs[:count], refs[count : count + 4]
    gains_ref, h_ref, q_ref, k_ref, v_ref, o_ref, lse_ref = refs[count + 4 : count + 11]
    send, recv, cross_send, cross_recv, cross_local, core_send, core_recv, loads, tiny, both, held = refs[count + 11 :]
    rows, width = h_ref.shape
    half = rows // 2
    pairs = q_ref.shape[1] // LANES
    where = whereabouts()
    z, x, c, y, up, down, across = where
    crossing = Crossing(c, y, cross_send, cross_recv, cross_local)
    chains = gather_events(where, slots, weights, send, recv)
    starts = list(bring_own(crossing, where, slots, chains, blocks, weights))
    frames_start, frames_finish = crossing.prepare(frames, both.at[0])
    moves = [crossing.prepare(*pair) for pair in ((text, text_out), (block, block_out), (target, target_out))]
    sibling = pltpu.make_async_remote_copy(
        src_ref=both.at[0], dst_ref=both.at[1], send_sem=core_send, recv_sem=core_recv,
        device_id={"c": 1 - c}, device_id_type=MESH,
    )
    keep = pltpu.make_async_copy(both.at[0], own_out, loads.at[4])
    fetch = [pltpu.make_async_copy(weights[0], tiny, loads.at[0])]
    fetch += [pltpu.make_async_copy(weights[i + 1], held.at[i], loads.at[i + 1]) for i in range(3)]

    def tick(at):
        for number in reversed(range(len(slots))):
            stage = at - number
            last = TICKS if number < NEEDED_FIRST else TICKS - 1
            if 0 <= stage < last:
                run_events(chains[number][stage])

    greet(c, y, up, down, x, True)
    for start in starts[:NEEDED_FIRST]:
        start()
    frames_start()
    for start in starts[NEEDED_FIRST:]:
        start()
    for start, _ in moves:
        start()
    ready = NEEDED_FIRST + TICKS - 1
    for at in range(ready):
        tick(at)
        if at == 3:
            frames_finish()
            sibling.start()
            keep.start()
        if at == ready - 4:
            fetch[0].start()
    for copy in fetch[1:]:
        copy.start()
    sibling.wait()
    fetch[0].wait()
    gains_ref[...] = tiny[...].reshape(width, LANES).astype(FLOAT).T[:8, :]

    def norm_step(i, carry):
        here = pl.ds(pl.multiple_of(i * LANES, LANES), LANES)
        for side in range(2):
            there = pl.ds(pl.multiple_of(side * half + i * LANES, LANES), LANES)
            h_ref[there, :] = normalize(both[side, here, :].astype(FLOAT), gains_ref[0:1, :], gains_ref[1:2, :]).astype(BRAIN)
        return carry

    lax.fori_loop(0, half // LANES, norm_step, 0)
    later = list(range(ready, len(slots) + TICKS - 2))
    tick(later.pop(0))
    for i, out in enumerate((q_ref, k_ref, v_ref)):
        fetch[i + 1].wait()

        def project_step(r, carry, i=i, out=out):
            here = pl.ds(pl.multiple_of(r * ROWS, ROWS), ROWS)
            out[here, :] = dot_nn(h_ref[here, :], held[i].reshape(width, -1)).astype(BRAIN)
            return carry

        lax.fori_loop(0, rows // ROWS, project_step, 0)
        if later:
            tick(later.pop(0))

    def pair_step(p, carry):
        for turn in range(pairs):
            if turn < len(later):
                @pl.when(p == turn)
                def _(turn=turn):
                    tick(later[turn])

        lanes = pl.ds(pl.multiple_of(p * LANES, LANES), LANES)
        every = slice(None)
        q, k, v, o = (ref.at[every, lanes] for ref in (q_ref, k_ref, v_ref, o_ref))
        attend_kernel(half, real, q, k, v, o, lse_ref.at[pl.ds(p, 1)])
        return carry

    lax.fori_loop(0, pairs, pair_step, 0)
    for at in later[pairs:]:
        tick(at)
    for ticks in chains[NEEDED_FIRST:]:
        run_events(ticks[TICKS - 1])
    keep.wait()
    for _, finish in moves:
        finish()


def gather(blocks, frames, text, target, block, real, slots):
    count = len(blocks)
    rows, width = 2 * frames.shape[0], frames.shape[1]
    share = blocks[1].shape[1]
    pairs = share // LANES
    crossings = count + 4
    dma = pltpu.SemaphoreType.DMA
    vmem = pl.BlockSpec(memory_space=pltpu.VMEM)
    heads = jax.ShapeDtypeStruct((rows, share), BRAIN)
    gathered = [jax.ShapeDtypeStruct((4, 2, 2, *b.shape), BRAIN) for b in blocks]
    return pl.pallas_call(
        functools.partial(gather_kernel, slots, count, real),
        out_shape=[
            *gathered,
            *[jax.ShapeDtypeStruct(v.shape, v.dtype) for v in (frames, text, target, block)],
            jax.ShapeDtypeStruct((8, width), FLOAT), jax.ShapeDtypeStruct((rows, width), BRAIN),
            heads, heads, heads, heads, jax.ShapeDtypeStruct((pairs, 8, rows), FLOAT),
        ],
        in_specs=[ANY] * (count + 4),
        out_specs=[ANY] * (count + 4) + [vmem] * 7,
        scratch_shapes=[
            dma((len(slots), 3, 5)), dma((len(slots), 3, 5)),
            dma((crossings,)), dma((crossings,)), dma((crossings,)), dma, dma, dma((5,)),
            pltpu.VMEM(gathered[0].shape, BRAIN), pltpu.VMEM((2, *frames.shape), BRAIN),
            pltpu.VMEM((3, *gathered[1].shape), BRAIN),
        ],
        compiler_params=pltpu.CompilerParams(
            collective_id=1, has_side_effects=True, vmem_limit_bytes=56 * 2**20
        ),
        name="gather",
    )(*blocks, frames, text, target, block)


def plus(*terms):
    total = terms[0].astype(FLOAT)
    for term in terms[1:]:
        total = total + term.astype(FLOAT)
    return total.astype(BRAIN)


def sum_scratch(slots, rows):
    shapes = []
    for _, _, sizes in slots:
        for kind, order in enumerate(ORDERS):
            size = sizes[kind]
            if size == 0:
                continue
            if order == "xyz":
                leads = [(2, 2, 2), (2, 2), (2, 2), (2, 2), (2,), ()]
            else:
                leads = [(4,), (4,), (), (), (), ()]
            shapes += [pltpu.VMEM((*lead, rows, size), BRAIN) for lead in leads]
    return shapes


def sum_landings(slots, rows):
    return [
        jax.ShapeDtypeStruct((4, 2, rows, sizes[kind]), BRAIN)
        for _, _, sizes in slots
        for kind, order in enumerate(ORDERS)
        if sizes[kind] and order != "xyz"
    ]


def sum_events(where, slots, terms, outs, landings, buffers, pads, crossing, send, recv, local):
    z, x, c, y, up, down, across = where
    every = slice(None)
    chains = []
    taken = landed = 0
    for number, (which, start, sizes) in enumerate(slots):
        ref, out = terms[which], outs[which]
        ticks = [[] for _ in range(TICKS + 1)]
        after, later = [], []
        for kind, order in enumerate(ORDERS):
            size = sizes[kind]
            if size == 0:
                continue
            columns = pl.ds(start, size)
            start += size
            need = 6
            held = buffers[taken : taken + need]
            taken += need

            def copy(at, src, dst, partner, kind=kind, number=number):
                return pltpu.make_async_remote_copy(
                    src_ref=src, dst_ref=dst, send_sem=send.at[number, kind, at],
                    recv_sem=recv.at[number, kind, at], device_id=partner, device_id_type=MESH,
                )

            def view(*region, ref=ref, columns=columns):
                return ref.at[(*region, every, columns)]

            if order == "xyz":
                own, from_two, from_down, from_up, from_y, from_x = held
                load_a = pltpu.make_async_copy(view(z, every, every), own.at[0], local.at[number, kind, 0])
                load_b = pltpu.make_async_copy(view(down, every, every), own.at[1], local.at[number, kind, 1])
                s_three = copy(0, view(up, every, every), from_down, {"z": up})
                s_two = copy(1, view(across, every, every), from_two, {"z": down})
                s_one = copy(2, own.at[1], from_up, {"z": down})
                s_y = copy(3, own.at[0, every, 1 - y], from_y, {"y": 1 - y})
                s_x = copy(4, from_y.at[1 - x], from_x, {"x": 1 - x})

                def add_two(own=own, from_two=from_two):
                    for i in range(2):
                        for j in range(2):
                            own[1, i, j] = plus(own[1, i, j], from_two[i, j])

                def add_z(own=own, a=from_down, b=from_up):
                    for i in range(2):
                        for j in range(2):
                            own[0, i, j] = plus(own[0, i, j], a[i, j], b[i, j])

                def add_y(own=own, from_y=from_y):
                    for i in range(2):
                        from_y[i] = plus(own[0, i, y], from_y[i])

                def add_x(from_y=from_y, from_x=from_x):
                    from_x[...] = plus(from_y[x], from_x[...])

                ticks[0] += [load_a.start, load_b.start, s_three.start, s_two.start]
                ticks[1] += [s_two.wait, load_b.wait, add_two, s_one.start]
                ticks[2] += [s_three.wait, load_a.wait, s_one.wait, add_z, s_y.start]
                ticks[3] += [s_y.wait, add_y, s_x.start]
                ticks[4] += [s_x.wait, add_x]
                final = from_x
            else:
                from_second, far, from_two, from_down, from_up, total = held
                landing = landings[landed]
                landed += 1
                mine_at, got_at = (pad.at[every, every, pl.ds(0, size)] for pad in pads[kind])
                mine_pad, got_pad = pads[kind]
                if order == "zxy":
                    mine, theirs = view(every, 1 - x, y), view(every, every, 1 - y)
                    first, second = {"y": 1 - y}, {"x": 1 - x}
                    side = x
                else:
                    mine, theirs = view(every, x, 1 - y), view(every, 1 - x, every)
                    first, second = {"x": 1 - x}, {"y": 1 - y}
                    side = y
                load_mine = pltpu.make_async_copy(mine, mine_at, local.at[number, kind, 0])
                load_got = pltpu.make_async_copy(landing.at[every, 1 - side], got_at, local.at[number, kind, 1])
                load_near = pltpu.make_async_copy(view(every, x, y), mine_at, local.at[number, kind, 2])
                load_rest = pltpu.make_async_copy(landing.at[every, side], got_at, local.at[number, kind, 3])
                s_first = copy(0, theirs, landing, first)
                s_second = copy(1, far, from_second, second)
                s_three = copy(2, from_second.at[up], from_down, {"z": up})
                s_two = copy(3, from_second.at[across], from_two, {"z": down})
                s_one = copy(4, from_second.at[down], from_up, {"z": down})

                def add_first(mine=mine_pad, got=got_pad, size=size, far=far):
                    for i in range(4):
                        far[i] = plus(mine[i, :, :size], got[i, :, :size])

                def add_second(mine=mine_pad, got=got_pad, size=size, more=from_second):
                    for i in range(4):
                        more[i] = plus(mine[i, :, :size], got[i, :, :size], more[i])

                def add_two(more=from_second, two=from_two):
                    more[down] = plus(more[down], two[...])

                def add_z(more=from_second, a=from_down, b=from_up, total=total):
                    total[...] = plus(more[z], a[...], b[...])

                ticks[0] += [s_first.start]
                ticks[1] += [s_first.wait, load_mine.start, load_got.start]
                after += [load_mine.wait, load_got.wait, add_first, s_second.start]
                ticks[2] += [s_second.wait, load_near.start, load_rest.start]
                later += [load_near.wait, load_rest.wait, add_second, s_three.start, s_two.start]
                ticks[3] += [s_two.wait, add_two, s_one.start]
                ticks[4] += [s_three.wait, s_one.wait, add_z]
                final = total

            leave, left = crossing.prepare(final, out.at[every, columns])
            ticks[4] += [leave]
            ticks[5] += [left]
        ticks[1] += after
        ticks[2] += later
        chains.append(ticks)
    return chains


def sum_order(count):
    shares = ((1, 0.5), (2, 0.27), (3, 0.08), (4, 0.1), (5, 0.05))
    order = []
    passed = 0.0
    for tick, part in shares:
        order += [(n, tick, passed + part * (n + 1) / count) for n in range(count)]
        passed += part
    return order


def run_events(events):
    for event in events:
        event()


def sum_kernel(slots, count, real, *refs):
    terms, refs = refs[:count], refs[count:]
    home, q, k, v, do, o, h, w_q, w_k, w_v, x0, dx1, lse, gains, vectors = refs[:15]
    refs = refs[15:]
    outs, (home_out, frames_out, vectors_out) = refs[: count + 3], refs[count + 3 : count + 6]
    refs = refs[count + 6 :]
    lands = len([1 for _, _, sizes in slots for kind, order in enumerate(ORDERS) if sizes[kind] and order != "xyz"])
    landings, refs = refs[:lands], refs[lands:]
    send, recv, local, cross_send, cross_recv, cross_local, v_send, v_recv, h_send, h_recv, loads = refs[:11]
    four, ring, pad_a, pad_b, pad_c, pad_d, grads, grad_terms, far, got, near = refs[11:22]
    half, width = x0.shape
    rows, share = q.shape
    pairs = share // LANES
    tiles = rows // ROWS
    quarter = width // 4
    where = whereabouts()
    z, x, c, y, up, down, across = where
    every = slice(None)
    crossing = Crossing(c, y, cross_send, cross_recv, cross_local)
    all_terms = [*terms, *(grad_terms.at[i] for i in range(3))]
    pads = ((pad_a, pad_b), (pad_c, pad_d))
    chains = sum_events(where, slots, all_terms, outs, landings, refs[22:], pads, crossing, send, recv, local)
    early = [n for n, slot in enumerate(slots) if slot[0] < count]
    late = [n for n, slot in enumerate(slots) if slot[0] >= count]
    home_start, home_finish = crossing.prepare(home, home_out)
    frames_start, frames_finish = crossing.prepare(far, frames_out)
    greet(c, y, up, down, x, True)
    for n in early:
        run_events(chains[n][0])
    home_start()

    work = tiles * (tiles + 1) // 2
    times = [p + sum(tiles - i for i in range(j)) / work for p in range(pairs) for j in range(tiles)]
    times += [pairs + 0.9 * i for i in range(1, 5)]
    spots = {}
    for number, tick, part in sum_order(len(early)):
        due = part * SUM_TIME * pairs
        later = [i for i, time in enumerate(times) if time >= due]
        spots.setdefault(later[0] if later else len(times), []).append((early[number], tick))

    def at_spot(spot):
        for number, tick in spots.get(spot, []):
            run_events(chains[number][tick])

    def attention(pair_in, *held):
        def load(p, i):
            lanes = pl.ds(pl.multiple_of(p * LANES, LANES), LANES)
            slot = lax.rem(p, 2)
            source = (q, k, v, do, o)[i]
            return pltpu.make_async_copy(source.at[every, lanes], pair_in.at[slot, i], loads.at[slot, i])

        for i in range(5):
            load(0, i).start()

        def pair_step(p, carry):
            @pl.when(p + 1 < pairs)
            def _():
                for i in range(5):
                    load(p + 1, i).start()

            for i in range(5):
                load(p, i).wait()

            def hook(j):
                for turn in range(pairs):
                    if turn * tiles + j in spots:
                        @pl.when(p == turn)
                        def _(turn=turn):
                            at_spot(turn * tiles + j)

            lanes = pl.ds(pl.multiple_of(p * LANES, LANES), LANES)
            slot = lax.rem(p, 2)
            attend_back_kernel(
                half, real, *(pair_in.at[slot, i] for i in range(5)), lse.at[pl.ds(p, 1)],
                *(grads.at[i, every, lanes] for i in range(3)), *held, hook=hook,
            )
            return carry

        lax.fori_loop(0, pairs, pair_step, 0)

    pl.run_scoped(
        attention,
        pltpu.VMEM((2, 5, rows, LANES), BRAIN), pltpu.VMEM((rows, LANES), FLOAT), pltpu.VMEM((8, rows), FLOAT),
        pltpu.VMEM((tiles, 2 * ROWS, LANES), BRAIN), pltpu.VMEM((tiles, 2 * ROWS, LANES), BRAIN),
    )

    def exchange(part):
        columns = pl.ds(part * quarter, quarter)
        return pltpu.make_async_remote_copy(
            src_ref=far.at[every, columns], dst_ref=got.at[every, columns], send_sem=h_send.at[part],
            recv_sem=h_recv.at[part], device_id={"c": 1 - c}, device_id_type=MESH,
        )

    def projections(h_in, w_in):
        def load(part, i):
            slot = part % 2
            if i == 3:
                return pltpu.make_async_copy(h.at[every, pl.ds(part * quarter, quarter)], h_in.at[slot], loads.at[slot, 3])
            return pltpu.make_async_copy((w_q, w_k, w_v)[i].at[part], w_in.at[slot, i], loads.at[slot, i])

        for i in range(4):
            load(0, i).start()
        for part in range(4):
            if part < 3:
                for i in range(4):
                    load(part + 1, i).start()
            for i in range(4):
                load(part, i).wait()
            slot = part % 2
            columns = pl.ds(part * quarter, quarter)

            def grad_step(i, carry, part=part, slot=slot):
                product = dot_tn(h_in[slot], grads[i]).astype(BRAIN)
                grad_terms[i, part] = product.reshape(grad_terms.shape[2:])
                return carry

            def back_step(r, carry, slot=slot, columns=columns, out=None, base=0):
                here = pl.ds(pl.multiple_of(r * ROWS, ROWS), ROWS)
                there = pl.ds(pl.multiple_of(base + r * ROWS, ROWS), ROWS)
                total = dot_nt(grads[0, there, :], w_in[slot, 0].reshape(quarter, share))
                for i in (1, 2):
                    total = total + dot_nt(grads[i, there, :], w_in[slot, i].reshape(quarter, share))
                out[here, columns] = total.astype(out.dtype)
                return carry

            lax.fori_loop(0, half // ROWS, functools.partial(back_step, out=far, base=half), 0)
            exchange(part).start()
            lax.fori_loop(0, half // ROWS, functools.partial(back_step, out=near), 0)
            lax.fori_loop(0, 3, grad_step, 0)
            at_spot(pairs * tiles + part)

    pl.run_scoped(
        projections, pltpu.VMEM((2, rows, quarter), BRAIN), pltpu.VMEM((2, 3, *w_q.shape[1:]), BRAIN)
    )
    for n in late:
        run_events(chains[n][0])
    for part in range(4):
        exchange(part).wait()
    four[...] = vectors[...]

    def norm(x_in, dx_in):
        size = x_in.shape[1]

        def load(i):
            slot = lax.rem(i, 2)
            here = pl.ds(pl.multiple_of(i * size, size), size)
            return (
                pltpu.make_async_copy(x0.at[here], x_in.at[slot], loads.at[slot, 0]),
                pltpu.make_async_copy(dx1.at[here], dx_in.at[slot], loads.at[slot, 1]),
            )

        for copy in load(0):
            copy.start()

        def step(i, carry):
            @pl.when(i + 1 < half // size)
            def _():
                for copy in load(i + 1):
                    copy.start()

            for copy in load(i):
                copy.wait()
            slot = lax.rem(i, 2)
            here = pl.ds(pl.multiple_of(i * size, size), size)
            flow = near[here, :].astype(FLOAT) + got[here, :].astype(FLOAT)
            values, gain_sum, bias_sum = norm_back(x_in[slot].astype(FLOAT), gains[0:1, :], flow)
            far[here, :] = (dx_in[slot] + values).astype(BRAIN)
            four[0:1, :] += gain_sum[None, :]
            four[1:2, :] += bias_sum[None, :]
            return carry

        lax.fori_loop(0, half // size, step, 0)

    pl.run_scoped(norm, pltpu.VMEM((2, 96, width), BRAIN), pltpu.VMEM((2, 96, width), FLOAT))
    frames_start()

    def hop(at, src, dst, partner):
        return pltpu.make_async_remote_copy(
            src_ref=src, dst_ref=dst, send_sem=v_send.at[at], recv_sem=v_recv.at[at],
            device_id=partner, device_id_type=MESH,
        )

    held = ring
    held[0] = four[...]
    for at, partner in enumerate(({"c": 1 - c}, {"y": 1 - y}, {"x": 1 - x})):
        turn = hop(at, held.at[2 * at], held.at[2 * at + 1], partner)
        turn.start()
        turn.wait()
        total = held[2 * at] + held[2 * at + 1]
        if at < 2:
            held[2 * at + 2] = total
        else:
            held[6 + z] = total
    z_up = hop(3, held.at[6 + z], held.at[6 + z], {"z": up})
    z_down = hop(4, held.at[6 + z], held.at[6 + z], {"z": down})
    z_more = hop(5, held.at[6 + down], held.at[6 + down], {"z": up})
    z_up.start()
    z_down.start()
    z_up.wait()
    z_more.start()
    rest = spots.get(len(times), []) + [(n, tick) for n in late for tick in range(1, TICKS + 1)]
    for number, tick in sorted(rest, key=lambda event: (event[1], event[0])):
        run_events(chains[number][tick])
    z_down.wait()
    z_more.wait()
    vectors_out[...] = (held[6] + held[7]) + (held[8] + held[9])
    home_finish()
    frames_finish()


def sum_gradients(terms, home, attention, h, weights, x0, dx1, lse, gains, vectors, real, slots):
    count = len(terms)
    rows, share = attention[0].shape
    half, width = x0.shape
    size = terms[0].shape[3]
    crossings = 3 * len(slots) + 2
    dma = pltpu.SemaphoreType.DMA
    vmem = pl.BlockSpec(memory_space=pltpu.VMEM)
    landings = sum_landings(slots, size)
    widths = [t.shape[4] for t in terms] + [share] * 3
    most = [max(sizes[kind] for _, _, sizes in slots) for kind in range(2)]
    results = pl.pallas_call(
        functools.partial(sum_kernel, slots, count, real),
        in_specs=[ANY] * (count + 12) + [vmem] * 3,
        out_specs=[ANY] * (count + 5) + [vmem] + [ANY] * len(landings),
        out_shape=[jax.ShapeDtypeStruct((size, n), BRAIN) for n in widths]
        + [jax.ShapeDtypeStruct(home.shape, BRAIN), jax.ShapeDtypeStruct(x0.shape, BRAIN)]
        + [jax.ShapeDtypeStruct(vectors.shape, FLOAT)]
        + landings,
        scratch_shapes=[
            dma((len(slots), 3, 5)), dma((len(slots), 3, 5)), dma((len(slots), 3, 4)),
            dma((crossings,)), dma((crossings,)), dma((crossings,)), dma((6,)), dma((6,)),
            dma((4,)), dma((4,)), dma((2, 5)),
            pltpu.VMEM(vectors.shape, FLOAT), pltpu.VMEM((10, *vectors.shape), FLOAT),
            *[pltpu.VMEM((4, size, most[kind]), BRAIN) for kind in (0, 0, 1, 1)],
            pltpu.VMEM((3, rows, share), BRAIN), pltpu.VMEM((3, 4, 2, 2, size, share), BRAIN),
            pltpu.VMEM((half, width), BRAIN), pltpu.VMEM((half, width), BRAIN), pltpu.VMEM((half, width), BRAIN),
            *sum_scratch(slots, size),
        ],
        compiler_params=pltpu.CompilerParams(
            collective_id=3, has_side_effects=True, vmem_limit_bytes=58 * 2**20
        ),
        name="sum_gradients",
    )(*terms, home, *attention, h, *weights, x0, dx1, lse, gains, vectors)
    return results[: count + 6]


def slots_of(widths, six=((2, 3, 1), (2, 3, 1), (3, 2, 1)), eight=(3, 3, 2)):
    slots = []
    for which, width in enumerate(widths):
        tiles = width // LANES
        if tiles == 6:
            slots.append((which, 0, tuple(LANES * n for n in six[len(slots) % len(six)])))
        elif tiles % 8 == 0:
            for at in range(0, tiles, 8):
                slots.append((which, at * LANES, tuple(LANES * n for n in eight)))
        else:
            slots.append((which, 0, (width, 0, 0)))
    return tuple(slots)


def normalize(values, gain_vec, bias_vec):
    center = values - jnp.mean(values, -1, keepdims=True)
    spread = jnp.mean(center * center, -1, keepdims=True)
    return center * lax.rsqrt(spread + EPSILON) * gain_vec + bias_vec


def norm_back(values, gain_vec, grads):
    center = values - jnp.mean(values, -1, keepdims=True)
    scale_row = lax.rsqrt(jnp.mean(center * center, -1, keepdims=True) + EPSILON)
    normal = center * scale_row
    scaled = grads * gain_vec
    inner = jnp.mean(scaled * normal, -1, keepdims=True)
    grad_values = scale_row * (scaled - jnp.mean(scaled, -1, keepdims=True) - normal * inner)
    return grad_values, jnp.sum(grads * normal, 0), jnp.sum(grads, 0)


def gelu_pair(u):
    half_erf = 0.5 * (1.0 + lax.erf(u * (0.5**0.5)))
    density = jnp.exp(-0.5 * u * u) * ((2.0 * np.pi) ** -0.5)
    return (u * half_erf).astype(BRAIN), (half_erf + u * density).astype(BRAIN)


def split_heads(values):
    return values.reshape(values.shape[0], -1, HEAD_DIM)


def merge_heads(values):
    return values.reshape(values.shape[0], -1)


def attend_cross(q, k, v):
    scores = jnp.einsum("qhd,khd->hqk", q, k, preferred_element_type=FLOAT) * SCALE
    top = jnp.max(scores, -1, keepdims=True)
    e = jnp.exp(scores - top)
    total = jnp.sum(e, -1, keepdims=True)
    probs = e / total
    out = jnp.einsum("hqk,khd->qhd", probs.astype(BRAIN), v, preferred_element_type=FLOAT)
    return merge_heads(out).astype(BRAIN), (top + jnp.log(total))[..., 0]


def attend_cross_back(q, k, v, do, lse):
    scores = jnp.einsum("qhd,khd->hqk", q, k, preferred_element_type=FLOAT) * SCALE
    probs = jnp.exp(scores - lse[..., None])
    dp = jnp.einsum("qhd,khd->hqk", do, v, preferred_element_type=FLOAT)
    inner = jnp.sum(probs * dp, -1, keepdims=True)
    ds = (probs * (dp - inner)).astype(BRAIN)
    dq = jnp.einsum("hqk,khd->qhd", ds, k, preferred_element_type=FLOAT) * SCALE
    dk = jnp.einsum("hqk,qhd->khd", ds, q, preferred_element_type=FLOAT) * SCALE
    dv = jnp.einsum("hqk,qhd->khd", probs.astype(BRAIN), do, preferred_element_type=FLOAT)
    return tuple(merge_heads(t).astype(BRAIN) for t in (dq, dk, dv))


def on_device(
    inputs, text_states, teacher, valid_frames,
    self_norm_gain, self_norm_bias, self_query, self_key, self_value, self_out,
    cross_norm_gain, cross_norm_bias, cross_query, cross_key, cross_value, cross_out,
    feed_norm_gain, feed_norm_bias, feed_in, feed_out,
):
    at_core, at_y = lax.axis_index("c"), lax.axis_index("y")
    real, width = inputs.shape[1], inputs.shape[2]
    half = -(-real // ROWS) * ROWS
    block, share = self_query.shape
    hidden = feed_in.shape[1]

    fits = ring_fit()

    tiny = [self_norm_gain, self_norm_bias, cross_norm_gain, cross_norm_bias, feed_norm_gain, feed_norm_bias]
    count = jnp.sum(valid_frames)
    digits = jnp.stack([count // 64, count % 64]).astype(BRAIN)
    digits = jnp.where((jnp.arange(block) == 0)[:, None], digits[None, :], jnp.zeros((), BRAIN))
    tiny = jnp.pad(jnp.concatenate([jnp.stack(tiny, 1), digits], 1), ((0, 0), (0, LANES - 8)))
    weights = [
        tiny, self_query, self_key, self_value, self_out.T, cross_query, cross_key, cross_value, cross_out.T, feed_in
    ]
    feed_rows = feed_out.T

    def both(own):
        return jnp.concatenate([own, swap_core(own)], 0)

    def summed(left, weight):
        far = dot_nt(left[half:], weight).astype(BRAIN)
        got = swap_core(far)
        return dot_nt(left[:half], weight) + got.astype(FLOAT)

    def padded(v):
        return jnp.pad(v, ((0, half - real), (0, 0)))

    frames = padded(inputs[0])
    flags = jnp.pad(valid_frames[0][:, None].astype(BRAIN), ((0, 0), (0, LANES - 1)))
    target = padded(jnp.concatenate([teacher[0], flags], 1))
    if fits:
        slots = slots_of([v.shape[1] for v in weights])
        *weights, x_own, text, target, feed_rows, gains, h1, q1, k1, v1, o1, lse1 = gather(
            weights, frames, text_states[0], target, feed_rows, real, slots
        )
        weights = [joined(v) for v in weights]
    else:
        weights = [lax.all_gather(swap_clip(v), CHIPS, axis=0, tiled=True) for v in weights]
        x_own, text, target, feed_rows = (swap_clip(v) for v in (frames, text_states[0], target, feed_rows))
        gains = weights[0].T.astype(FLOAT)
        x_all = jnp.concatenate([x_own, swap_core(x_own)], 0)
        h1 = normalize(x_all.astype(FLOAT), gains[0], gains[1]).astype(BRAIN)
        q1, k1, v1 = (dot_nn(h1, w).astype(BRAIN) for w in weights[1:4])
        o1, lse1 = attend_self(q1, k1, v1, real)
    tiny, w_q, w_k, w_v, w_so, w_cq, w_ck, w_cv, w_co, w_fi = weights
    counted = jnp.sum(tiny[:, 6:8].astype(FLOAT), 0)
    counted = counted[0] * 64.0 + counted[1]
    token_count = counted + swap_core(counted)
    w_fo = lax.all_gather(feed_rows, CHIPS, axis=0, tiled=True)
    valid = target[:, width : width + 1].astype(FLOAT)
    target = target[:, :width].astype(FLOAT)
    x0 = x_own.astype(FLOAT)
    x1 = x0 + summed(o1, w_so)
    h2 = both(normalize(x1, gains[2], gains[3]).astype(BRAIN))
    q2 = dot_nn(h2, w_cq).astype(BRAIN)
    k2 = dot_nn(text, w_ck).astype(BRAIN)
    v2 = dot_nn(text, w_cv).astype(BRAIN)
    o2, lse2 = attend_cross(split_heads(q2), split_heads(k2), split_heads(v2))
    x2 = x1 + summed(o2, w_co)
    h3 = both(normalize(x2, gains[4], gains[5]).astype(BRAIN))
    g, slope = gelu_pair(dot_nn(h3, w_fi))
    y = x2 + summed(g, w_fo)
    home = y.astype(BRAIN)
    deviation = y - target
    error = jnp.sum(valid * deviation * deviation)
    tokens_all = real * lax.axis_size(("z", "x", "c", "y"))
    dy = (2.0 * tokens_all / token_count) * valid * deviation

    dyb = both(dy.astype(BRAIN))
    fo_grad = dot_tn(dyb, g).astype(BRAIN)
    dyb, fo_grad = lax.optimization_barrier((dyb, fo_grad))
    fo_grad = lax.psum_scatter(fo_grad, CHIPS, scatter_dimension=0, tiled=True)
    du = (slope.astype(FLOAT) * dot_nn(dyb, w_fo)).astype(BRAIN)
    fi_grad = dot_tn(h3, du).astype(BRAIN)
    term, gain3, bias3 = norm_back(x2, gains[4], summed(du, w_fi))
    dx2 = dy + term
    dx2b = both(dx2.astype(BRAIN))
    co_grad = dot_tn(dx2b, o2).astype(BRAIN)
    do2 = dot_nn(dx2b, w_co).astype(BRAIN)
    dq2, dk2, dv2 = attend_cross_back(
        split_heads(q2), split_heads(k2), split_heads(v2), split_heads(do2), lse2
    )
    cq_grad = dot_tn(h2, dq2).astype(BRAIN)
    ck_grad = dot_tn(text, dk2).astype(BRAIN)
    cv_grad = dot_tn(text, dv2).astype(BRAIN)
    text_part = (dot_nt(dk2, w_ck) + dot_nt(dv2, w_cv)).astype(BRAIN)
    text_mine = jnp.where(at_core == 0, text_part[:, : width // 2], text_part[:, width // 2 :])
    text_far = jnp.where(at_core == 0, text_part[:, width // 2 :], text_part[:, : width // 2])
    text_sum = text_mine.astype(FLOAT) + swap_core(text_far).astype(FLOAT)
    text_grad = swap_clip(text_sum.astype(BRAIN)).astype(FLOAT)[None]
    term, gain2, bias2 = norm_back(x1, gains[2], summed(dq2, w_cq))
    dx1 = dx2 + term
    dx1b = both(dx1.astype(BRAIN))
    so_grad = dot_tn(dx1b, o1).astype(BRAIN)
    do1 = dot_nn(dx1b, w_so).astype(BRAIN)
    zero = jnp.zeros((width,), FLOAT)
    vectors = jnp.stack([zero, zero, gain2, bias2, gain3, bias3])
    vectors = jnp.concatenate([vectors, jnp.full((2, width), error)], 0)
    grads = [fi_grad, co_grad, cq_grad, ck_grad, cv_grad, so_grad]
    if fits:
        slots = slots_of([v.shape[1] for v in grads] + [share] * 3, six=((2, 2, 2),))
        *grads, home, frames, vectors = sum_gradients(
            [by_chip(v) for v in grads], home, (q1, k1, v1, do1, o1), h1,
            [by_chip(v) for v in (w_q, w_k, w_v)], x_own, dx1, lse1, gains, vectors, real, slots,
        )
    else:
        dq1, dk1, dv1 = attend_self_back(q1, k1, v1, do1, o1, lse1, real)
        dh1 = dot_nt(dq1, w_q) + dot_nt(dk1, w_k) + dot_nt(dv1, w_v)
        dh1 = dh1[:half] + swap_core(dh1[half:].astype(BRAIN)).astype(FLOAT)
        term, gain1, bias1 = norm_back(x0, gains[0], dh1)
        frames = swap_clip((dx1 + term).astype(BRAIN))
        grads += [dot_tn(h1, d).astype(BRAIN) for d in (dq1, dk1, dv1)]
        grads = [swap_clip(lax.psum_scatter(v, CHIPS, scatter_dimension=0, tiled=True)) for v in grads]
        home = swap_clip(home)
        vectors = lax.psum(vectors.at[:2].set(jnp.stack([gain1, bias1])), ("z", "x", "c", "y"))
    layer_out = home[:real][None]
    inputs_grad = frames[None].astype(FLOAT)[:, :real]
    fi_grad, co_grad, cq_grad, ck_grad, cv_grad, so_grad, q_grad, k_grad, v_grad = (v.astype(FLOAT) for v in grads)
    fo_grad = jnp.where(at_core == at_y, fo_grad, swap_others(fo_grad)).astype(FLOAT).T
    loss = vectors[6, 0] / (width * token_count)
    mine = block // 2
    place = (lax.axis_index(("z", "x", "c")) * 2 + at_y) * mine
    norms = lax.dynamic_slice(vectors, (0, place), (8, mine))
    return (
        loss, layer_out, inputs_grad, text_grad,
        norms[0], norms[1], q_grad, k_grad, v_grad, so_grad.T,
        norms[2], norms[3], cq_grad, ck_grad, cv_grad, co_grad.T,
        norms[4], norms[5], fi_grad, fo_grad,
    )


def solution(mesh):
    outer = mesh.shape["dp"] // 4
    fine = Mesh(np.array(mesh.devices).reshape(outer, 2, 2, 2), ("z", "x", "c", "y"))
    dp = ("z", "x", "c")
    frames = P(dp, "y", None)
    vector, wide, tall = P(dp), P(dp, "y"), P("y", dp)
    small = P(("z", "x", "c", "y"))
    attention = (vector, vector, wide, wide, wide, tall)
    return jax.shard_map(
        on_device,
        mesh=fine,
        in_specs=(frames, P(dp, None, None), frames, P(dp, "y"), *attention, *attention, vector, vector, wide, tall),
        out_specs=(
            P(), frames, frames, P(dp, None, "y"),
            small, small, wide, wide, wide, tall,
            small, small, wide, wide, wide, tall,
            small, small, wide, tall,
        ),
        check_vma=False,
    )
```

```python
import functools

import jax
import jax.numpy as jnp
import numpy as np
from jax import lax
from jax.experimental import pallas as pl
from jax.experimental.pallas import tpu as pltpu
from jax.sharding import Mesh
from jax.sharding import PartitionSpec as P

HEAD_DIM = 64
LANES = 128
ROWS = 256
FLOAT = jnp.float32
BRAIN = jnp.bfloat16
NEGATIVE = -1e30
EPSILON = 1e-05
SCALE = HEAD_DIM ** (-0.5)
CHIPS = ("z", "x", "y")
MESH = pl.DeviceIdType.MESH


def swap_core(v):
    return lax.ppermute(v, "c", [(0, 1), (1, 0)])


def swap_clip(v):
    return lax.ppermute(v, ("c", "y"), [(0, 0), (1, 2), (2, 1), (3, 3)])


def swap_others(v):
    return lax.ppermute(v, ("c", "y"), [(1, 2), (2, 1)])


def swap_weight(v):
    return jnp.where(lax.axis_index("c") == lax.axis_index("y"), v, swap_others(v))


def ring_fit():
    return lax.axis_size("z") == 4 and lax.axis_size("x") == 2 and lax.axis_size("y") == 2


def by_chip(v):
    return v.reshape(4, 2, 2, v.shape[0] // 16, v.shape[1])


def joined(v):
    return v.reshape(-1, v.shape[-1])


def dot_nt(a, b, **kw):
    return lax.dot_general(a, b, (((1,), (1,)), ((), ())), preferred_element_type=FLOAT, **kw)


def dot_nn(a, b):
    return lax.dot_general(a, b, (((1,), (0,)), ((), ())), preferred_element_type=FLOAT)


def dot_tn(a, b):
    return lax.dot_general(a, b, (((0,), (0,)), ((), ())), preferred_element_type=FLOAT)


def attend_kernel(half, real, q_ref, k_ref, v_ref, o_ref, lse_ref):
    core = lax.axis_index("c")
    per_half = half // ROWS
    blocks = 2 * per_half
    lane = lax.broadcasted_iota(jnp.int32, (ROWS, LANES), 1)
    first = lane < HEAD_DIM
    rows_at = lax.broadcasted_iota(jnp.int32, (ROWS, ROWS), 0)
    cols_at = lax.broadcasted_iota(jnp.int32, (ROWS, ROWS), 1)

    def place(i):
        start = jnp.where(core == i // per_half, 0, half) + (i % per_half) * ROWS
        return pl.ds(pl.multiple_of(start, ROWS), ROWS)

    for i in range(blocks):
        queries = q_ref[place(i), :].astype(FLOAT) * SCALE
        outs = []
        logs = []
        for head in range(2):
            mine = first if head == 0 else jnp.logical_not(first)
            masked = jnp.where(mine, queries, 0.0).astype(BRAIN)
            scores = []
            for j in range(i + 1):
                s = dot_nt(masked, k_ref[place(j), :])
                if j == i:
                    s = jnp.where(cols_at <= rows_at, s, NEGATIVE)
                elif j == per_half - 1:
                    s = jnp.where(cols_at < real - (per_half - 1) * ROWS, s, NEGATIVE)
                scores.append(s)
            top = scores[0]
            for s in scores[1:]:
                top = jnp.maximum(top, s)
            top = jnp.max(top, 1, keepdims=True)
            total = None
            out = None
            for j in range(i + 1):
                e = jnp.exp(scores[j] - top)
                total = e if total is None else total + e
                term = dot_nn(e.astype(BRAIN), v_ref[place(j), :])
                out = term if out is None else out + term
            total = jnp.sum(total, 1, keepdims=True)
            outs.append(out / total)
            logs.append(top + jnp.log(total))
        o_ref[place(i), :] = jnp.where(first, outs[0], outs[1]).astype(BRAIN)
        both = jnp.where(lane == 0, logs[0], logs[1])
        lse_ref[0, :, i * ROWS : (i + 1) * ROWS] = both.T[:8, :]


def attend_self(q, k, v, real):
    rows, width = q.shape
    pairs = width // LANES
    spec = pl.BlockSpec((rows, LANES), lambda p: (0, p))
    return pl.pallas_call(
        functools.partial(attend_kernel, rows // 2, real),
        grid=(pairs,),
        in_specs=[spec, spec, spec],
        out_specs=[spec, pl.BlockSpec((1, 8, rows), lambda p: (p, 0, 0))],
        out_shape=[
            jax.ShapeDtypeStruct((rows, width), BRAIN),
            jax.ShapeDtypeStruct((pairs, 8, rows), FLOAT),
        ],
        compiler_params=pltpu.CompilerParams(vmem_limit_bytes=48 * 2**20),
        cost_estimate=pl.CostEstimate(
            flops=10 * rows * rows * width, bytes_accessed=8 * rows * width, transcendentals=0
        ),
        name="attend",
    )(q, k, v)


def attend_back_kernel(
    half, real, q_ref, k_ref, v_ref, do_ref, o_ref, lse_ref, dq_ref, dk_ref, dv_ref,
    dq_sum, inner, q_two, do_two, hook=None,
):
    core = lax.axis_index("c")
    per_half = half // ROWS
    blocks = 2 * per_half
    first = lax.broadcasted_iota(jnp.int32, (ROWS, LANES), 1) < HEAD_DIM
    key_at = lax.broadcasted_iota(jnp.int32, (ROWS, 2 * ROWS), 0)
    query_at = lax.broadcasted_iota(jnp.int32, (ROWS, 2 * ROWS), 1) % ROWS
    pick = lax.broadcasted_iota(jnp.int32, (8, LANES), 1) // HEAD_DIM
    pick = (pick == lax.broadcasted_iota(jnp.int32, (8, LANES), 0)).astype(FLOAT)

    def place(i):
        start = jnp.where(core == i // per_half, 0, half) + (i % per_half) * ROWS
        return pl.ds(pl.multiple_of(start, ROWS), ROWS)

    def side_by_side(ref, i):
        return jnp.concatenate([ref[0:1, i * ROWS : (i + 1) * ROWS], ref[1:2, i * ROWS : (i + 1) * ROWS]], 1)

    for i in range(blocks):
        grads = do_ref[place(i), :].astype(FLOAT)
        queries = q_ref[place(i), :].astype(FLOAT) * SCALE
        product = grads * o_ref[place(i), :].astype(FLOAT)
        inner[:, i * ROWS : (i + 1) * ROWS] = dot_nt(pick, product, precision=lax.Precision.HIGHEST)
        q_two[i, :ROWS] = jnp.where(first, queries, 0.0).astype(BRAIN)
        q_two[i, ROWS:] = jnp.where(first, 0.0, queries).astype(BRAIN)
        do_two[i, :ROWS] = jnp.where(first, grads, 0.0).astype(BRAIN)
        do_two[i, ROWS:] = jnp.where(first, 0.0, grads).astype(BRAIN)
    dq_sum[...] = jnp.zeros_like(dq_sum)

    for j in range(blocks):
        if hook is not None:
            hook(j)
        keys = k_ref[place(j), :]
        values = v_ref[place(j), :]
        dk = dv = None
        for i in range(j, blocks):
            rows = pl.ds(i * ROWS, ROWS)
            q_m, do_m = q_two[i], do_two[i]
            s = dot_nt(keys, q_m) - side_by_side(lse_ref.at[0], i)
            if i == j:
                s = jnp.where(key_at <= query_at, s, NEGATIVE)
            elif j == per_half - 1:
                s = jnp.where(key_at < real - j * ROWS, s, NEGATIVE)
            p = jnp.exp(s)
            dp = dot_nt(values, do_m)
            ds = (p * (dp - side_by_side(inner, i))).astype(BRAIN)
            dv_term = dot_nn(p.astype(BRAIN), do_m)
            dk_term = dot_nn(ds, q_m)
            dk = dk_term if dk is None else dk + dk_term
            dv = dv_term if dv is None else dv + dv_term
            dq = dot_tn(ds, keys)
            dq_sum[rows, :] += jnp.where(first, dq[:ROWS], dq[ROWS:])
        dk_ref[place(j), :] = dk.astype(BRAIN)
        dv_ref[place(j), :] = dv.astype(BRAIN)

    for i in range(blocks):
        dq_ref[place(i), :] = (dq_sum[i * ROWS : (i + 1) * ROWS, :] * SCALE).astype(BRAIN)


def attend_self_back(q, k, v, do, o, lse, real):
    rows, width = q.shape
    pairs = width // LANES
    spec = pl.BlockSpec((rows, LANES), lambda p: (0, p))
    return pl.pallas_call(
        functools.partial(attend_back_kernel, rows // 2, real),
        grid=(pairs,),
        in_specs=[spec] * 5 + [pl.BlockSpec((1, 8, rows), lambda p: (p, 0, 0))],
        out_specs=[spec] * 3,
        scratch_shapes=[
            pltpu.VMEM((rows, LANES), FLOAT),
            pltpu.VMEM((8, rows), FLOAT),
            pltpu.VMEM((rows // ROWS, 2 * ROWS, LANES), BRAIN),
            pltpu.VMEM((rows // ROWS, 2 * ROWS, LANES), BRAIN),
        ],
        out_shape=[jax.ShapeDtypeStruct((rows, width), BRAIN)] * 3,
        compiler_params=pltpu.CompilerParams(vmem_limit_bytes=48 * 2**20),
        cost_estimate=pl.CostEstimate(
            flops=25 * rows * rows * width, bytes_accessed=16 * rows * width, transcendentals=0
        ),
        name="attend_back",
    )(q, k, v, do, o, lse)


ORDERS = ("zxy", "zyx", "xyz")
TICKS = 5
SUM_TIME = 2.2


def whereabouts():
    z, x, c, y = (lax.axis_index(name) for name in ("z", "x", "c", "y"))
    return z, x, c, y, lax.rem(z + 1, 4), lax.rem(z + 3, 4), lax.rem(z + 2, 4)


def greet(c, y, up, down, x, cores):
    barrier = pltpu.get_barrier_semaphore()
    partners = [{"z": up}, {"z": down}, {"x": 1 - x}, {"y": 1 - y}]
    if cores:
        partners.append({"c": 1 - c})
    for partner in partners:
        pl.semaphore_signal(barrier, inc=1, device_id=partner, device_id_type=MESH)

    @pl.when(c != y)
    def _():
        pl.semaphore_signal(barrier, inc=1, device_id={"c": y, "y": c}, device_id_type=MESH)
        pl.semaphore_wait(barrier, len(partners) + 1)

    @pl.when(c == y)
    def _():
        pl.semaphore_wait(barrier, len(partners))


def one(i):
    return pl.ds(i, 1)


class Crossing:
    def __init__(self, c, y, send, recv, local):
        self.c, self.y, self.send, self.recv, self.local = c, y, send, recv, local
        self.used = 0

    def begin(self, src, dst):
        start, finish = self.prepare(src, dst)
        start()
        return finish

    def prepare(self, src, dst):
        at = self.used
        self.used += 1
        far = pltpu.make_async_remote_copy(
            src_ref=src, dst_ref=dst, send_sem=self.send.at[at], recv_sem=self.recv.at[at],
            device_id={"c": self.y, "y": self.c}, device_id_type=MESH,
        )
        near = pltpu.make_async_copy(src, dst, self.local.at[at])

        def start():
            @pl.when(self.c != self.y)
            def _():
                far.start()

            @pl.when(self.c == self.y)
            def _():
                near.start()

        def finish():
            @pl.when(self.c != self.y)
            def _():
                far.wait()

            @pl.when(self.c == self.y)
            def _():
                near.wait()

        return start, finish


def gather_events(where, slots, weights, send, recv):
    z, x, c, y, up, down, across = where
    every = slice(None)
    chains = []
    for number, (which, start, sizes) in enumerate(slots):
        ref = weights[which]
        ticks = [[] for _ in range(TICKS)]
        for kind, order in enumerate(ORDERS):
            size = sizes[kind]
            if size == 0:
                continue
            columns = pl.ds(start, size)
            start += size

            def copy(at, region, partner, ref=ref, columns=columns, kind=kind, number=number):
                view = ref.at[(*region, every, columns)]
                return pltpu.make_async_remote_copy(
                    src_ref=view, dst_ref=view, send_sem=send.at[number, kind, at],
                    recv_sem=recv.at[number, kind, at], device_id=partner, device_id_type=MESH,
                )

            if order == "xyz":
                by_x = copy(0, (one(z), one(x), one(y)), {"x": 1 - x})
                by_y = copy(1, (one(z), every, one(y)), {"y": 1 - y})
                rest = (every, every)
            else:
                rest = (one(x), one(y))
            z_up = copy(2, (one(z), *rest), {"z": up})
            z_down = copy(3, (one(z), *rest), {"z": down})
            z_more = copy(4, (one(down), *rest), {"z": up})
            if order == "xyz":
                ticks[0] += [by_x.start]
                ticks[1] += [by_x.wait, by_y.start]
                ticks[2] += [by_y.wait, z_up.start, z_down.start]
                ticks[3] += [z_up.wait, z_more.start]
                ticks[4] += [z_down.wait, z_more.wait]
            else:
                if order == "zxy":
                    near = copy(0, (every, one(x), one(y)), {"x": 1 - x})
                    far = copy(1, (every, every, one(y)), {"y": 1 - y})
                else:
                    near = copy(0, (every, one(x), one(y)), {"y": 1 - y})
                    far = copy(1, (every, one(x), every), {"x": 1 - x})
                ticks[0] += [z_up.start, z_down.start]
                ticks[1] += [z_up.wait, z_more.start]
                ticks[2] += [z_down.wait, z_more.wait, near.start]
                ticks[3] += [near.wait, far.start]
                ticks[4] += [far.wait]
        chains.append(ticks)
    return chains


def run_tick(chains, at):
    for number, ticks in enumerate(chains):
        if 0 <= at - number < TICKS:
            for event in ticks[at - number]:
                event()


def total_ticks(slots):
    return len(slots) + TICKS - 1


def bring_own(crossing, where, slots, chains, blocks, weights):
    z, x, c = where[:3]
    for which, (block, weight) in enumerate(zip(blocks, weights)):
        start, finish = crossing.prepare(block, weight.at[z, x, c])
        number = [slot[0] for slot in slots].index(which)
        chains[number][0].insert(0, finish)
        yield start


ANY = pl.BlockSpec(memory_space=pl.ANY)
NEEDED_FIRST = 4


def gather_kernel(slots, count, real, *refs):
    blocks, (frames, text, target) = refs[:count], refs[count : count + 3]
    refs = refs[count + 3 :]
    weights, (own_out, text_out, target_out) = refs[:count], refs[count : count + 3]
    gains_ref, h_ref, q_ref, k_ref, v_ref, o_ref, lse_ref = refs[count + 3 : count + 10]
    send, recv, cross_send, cross_recv, cross_local, core_send, core_recv, loads, tiny, both, held = refs[count + 10 :]
    rows, width = h_ref.shape
    half = rows // 2
    pairs = q_ref.shape[1] // LANES
    where = whereabouts()
    z, x, c, y, up, down, across = where
    crossing = Crossing(c, y, cross_send, cross_recv, cross_local)
    chains = gather_events(where, slots, weights, send, recv)
    starts = list(bring_own(crossing, where, slots, chains, blocks, weights))
    frames_start, frames_finish = crossing.prepare(frames, both.at[0])
    moves = [crossing.prepare(*pair) for pair in ((text, text_out), (target, target_out))]
    sibling = pltpu.make_async_remote_copy(
        src_ref=both.at[0], dst_ref=both.at[1], send_sem=core_send, recv_sem=core_recv,
        device_id={"c": 1 - c}, device_id_type=MESH,
    )
    keep = pltpu.make_async_copy(both.at[0], own_out, loads.at[4])
    fetch = [pltpu.make_async_copy(weights[0], tiny, loads.at[0])]
    fetch += [pltpu.make_async_copy(weights[i + 1], held.at[i], loads.at[i + 1]) for i in range(3)]

    def tick(at):
        for number in reversed(range(len(slots))):
            stage = at - number
            last = TICKS if number < NEEDED_FIRST else TICKS - 1
            if 0 <= stage < last:
                run_events(chains[number][stage])

    greet(c, y, up, down, x, True)
    for start in starts[:NEEDED_FIRST]:
        start()
    frames_start()
    for start in starts[NEEDED_FIRST:]:
        start()
    for start, _ in moves:
        start()
    ready = NEEDED_FIRST + TICKS - 1
    for at in range(ready):
        tick(at)
        if at == 3:
            frames_finish()
            sibling.start()
            keep.start()
        if at == ready - 4:
            fetch[0].start()
    for copy in fetch[1:]:
        copy.start()
    sibling.wait()
    fetch[0].wait()
    gains_ref[...] = tiny[...].reshape(width, LANES).astype(FLOAT).T[:8, :]

    def norm_step(i, carry):
        here = pl.ds(pl.multiple_of(i * LANES, LANES), LANES)
        for side in range(2):
            there = pl.ds(pl.multiple_of(side * half + i * LANES, LANES), LANES)
            h_ref[there, :] = normalize(both[side, here, :].astype(FLOAT), gains_ref[0:1, :], gains_ref[1:2, :]).astype(BRAIN)
        return carry

    lax.fori_loop(0, half // LANES, norm_step, 0)
    later = list(range(ready, len(slots) + TICKS - 2))
    tick(later.pop(0))
    for i, out in enumerate((q_ref, k_ref, v_ref)):
        fetch[i + 1].wait()

        def project_step(r, carry, i=i, out=out):
            here = pl.ds(pl.multiple_of(r * ROWS, ROWS), ROWS)
            out[here, :] = dot_nn(h_ref[here, :], held[i].reshape(width, -1)).astype(BRAIN)
            return carry

        lax.fori_loop(0, rows // ROWS, project_step, 0)
        if later:
            tick(later.pop(0))

    def pair_step(p, carry):
        for turn in range(pairs):
            if turn < len(later):
                @pl.when(p == turn)
                def _(turn=turn):
                    tick(later[turn])

        lanes = pl.ds(pl.multiple_of(p * LANES, LANES), LANES)
        every = slice(None)
        q, k, v, o = (ref.at[every, lanes] for ref in (q_ref, k_ref, v_ref, o_ref))
        attend_kernel(half, real, q, k, v, o, lse_ref.at[pl.ds(p, 1)])
        return carry

    lax.fori_loop(0, pairs, pair_step, 0)
    for at in later[pairs:]:
        tick(at)
    for ticks in chains[NEEDED_FIRST:]:
        run_events(ticks[TICKS - 1])
    keep.wait()
    for _, finish in moves:
        finish()


def gather(blocks, frames, text, target, real, slots):
    count = len(blocks)
    rows, width = 2 * frames.shape[0], frames.shape[1]
    share = blocks[1].shape[1]
    pairs = share // LANES
    crossings = count + 3
    dma = pltpu.SemaphoreType.DMA
    vmem = pl.BlockSpec(memory_space=pltpu.VMEM)
    heads = jax.ShapeDtypeStruct((rows, share), BRAIN)
    gathered = [jax.ShapeDtypeStruct((4, 2, 2, *b.shape), BRAIN) for b in blocks]
    return pl.pallas_call(
        functools.partial(gather_kernel, slots, count, real),
        out_shape=[
            *gathered,
            *[jax.ShapeDtypeStruct(v.shape, v.dtype) for v in (frames, text, target)],
            jax.ShapeDtypeStruct((8, width), FLOAT), jax.ShapeDtypeStruct((rows, width), BRAIN),
            heads, heads, heads, heads, jax.ShapeDtypeStruct((pairs, 8, rows), FLOAT),
        ],
        in_specs=[ANY] * (count + 3),
        out_specs=[ANY] * (count + 3) + [vmem] * 7,
        scratch_shapes=[
            dma((len(slots), 3, 5)), dma((len(slots), 3, 5)),
            dma((crossings,)), dma((crossings,)), dma((crossings,)), dma, dma, dma((5,)),
            pltpu.VMEM(gathered[0].shape, BRAIN), pltpu.VMEM((2, *frames.shape), BRAIN),
            pltpu.VMEM((3, *gathered[1].shape), BRAIN),
        ],
        compiler_params=pltpu.CompilerParams(
            collective_id=1, has_side_effects=True, vmem_limit_bytes=56 * 2**20
        ),
        name="gather",
    )(*blocks, frames, text, target)


def plus(*terms):
    total = terms[0].astype(FLOAT)
    for term in terms[1:]:
        total = total + term.astype(FLOAT)
    return total.astype(BRAIN)


def sum_scratch(slots, rows):
    shapes = []
    for _, _, sizes in slots:
        for kind, order in enumerate(ORDERS):
            size = sizes[kind]
            if size == 0:
                continue
            if order == "xyz":
                leads = [(2, 2, 2), (2, 2), (2, 2), (2, 2), (2,), ()]
            else:
                leads = [(4,), (4,), (), (), (), ()]
            shapes += [pltpu.VMEM((*lead, rows, size), BRAIN) for lead in leads]
    return shapes


def sum_landings(slots, rows):
    return [
        jax.ShapeDtypeStruct((4, 2, rows, sizes[kind]), BRAIN)
        for _, _, sizes in slots
        for kind, order in enumerate(ORDERS)
        if sizes[kind] and order != "xyz"
    ]


def sum_events(where, slots, terms, outs, landings, buffers, pads, crossing, send, recv, local):
    z, x, c, y, up, down, across = where
    every = slice(None)
    chains = []
    taken = landed = 0
    for number, (which, start, sizes) in enumerate(slots):
        ref, out = terms[which], outs[which]
        ticks = [[] for _ in range(TICKS + 1)]
        after, later = [], []
        for kind, order in enumerate(ORDERS):
            size = sizes[kind]
            if size == 0:
                continue
            columns = pl.ds(start, size)
            start += size
            need = 6
            held = buffers[taken : taken + need]
            taken += need

            def copy(at, src, dst, partner, kind=kind, number=number):
                return pltpu.make_async_remote_copy(
                    src_ref=src, dst_ref=dst, send_sem=send.at[number, kind, at],
                    recv_sem=recv.at[number, kind, at], device_id=partner, device_id_type=MESH,
                )

            def view(*region, ref=ref, columns=columns):
                return ref.at[(*region, every, columns)]

            if order == "xyz":
                own, from_two, from_down, from_up, from_y, from_x = held
                load_a = pltpu.make_async_copy(view(z, every, every), own.at[0], local.at[number, kind, 0])
                load_b = pltpu.make_async_copy(view(down, every, every), own.at[1], local.at[number, kind, 1])
                s_three = copy(0, view(up, every, every), from_down, {"z": up})
                s_two = copy(1, view(across, every, every), from_two, {"z": down})
                s_one = copy(2, own.at[1], from_up, {"z": down})
                s_y = copy(3, own.at[0, every, 1 - y], from_y, {"y": 1 - y})
                s_x = copy(4, from_y.at[1 - x], from_x, {"x": 1 - x})

                def add_two(own=own, from_two=from_two):
                    for i in range(2):
                        for j in range(2):
                            own[1, i, j] = plus(own[1, i, j], from_two[i, j])

                def add_z(own=own, a=from_down, b=from_up):
                    for i in range(2):
                        for j in range(2):
                            own[0, i, j] = plus(own[0, i, j], a[i, j], b[i, j])

                def add_y(own=own, from_y=from_y):
                    for i in range(2):
                        from_y[i] = plus(own[0, i, y], from_y[i])

                def add_x(from_y=from_y, from_x=from_x):
                    from_x[...] = plus(from_y[x], from_x[...])

                ticks[0] += [load_a.start, load_b.start, s_three.start, s_two.start]
                ticks[1] += [s_two.wait, load_b.wait, add_two, s_one.start]
                ticks[2] += [s_three.wait, load_a.wait, s_one.wait, add_z, s_y.start]
                ticks[3] += [s_y.wait, add_y, s_x.start]
                ticks[4] += [s_x.wait, add_x]
                final = from_x
            else:
                from_second, far, from_two, from_down, from_up, total = held
                landing = landings[landed]
                landed += 1
                mine_at, got_at = (pad.at[every, every, pl.ds(0, size)] for pad in pads[kind])
                mine_pad, got_pad = pads[kind]
                if order == "zxy":
                    mine, theirs = view(every, 1 - x, y), view(every, every, 1 - y)
                    first, second = {"y": 1 - y}, {"x": 1 - x}
                    side = x
                else:
                    mine, theirs = view(every, x, 1 - y), view(every, 1 - x, every)
                    first, second = {"x": 1 - x}, {"y": 1 - y}
                    side = y
                load_mine = pltpu.make_async_copy(mine, mine_at, local.at[number, kind, 0])
                load_got = pltpu.make_async_copy(landing.at[every, 1 - side], got_at, local.at[number, kind, 1])
                load_near = pltpu.make_async_copy(view(every, x, y), mine_at, local.at[number, kind, 2])
                load_rest = pltpu.make_async_copy(landing.at[every, side], got_at, local.at[number, kind, 3])
                s_first = copy(0, theirs, landing, first)
                s_second = copy(1, far, from_second, second)
                s_three = copy(2, from_second.at[up], from_down, {"z": up})
                s_two = copy(3, from_second.at[across], from_two, {"z": down})
                s_one = copy(4, from_second.at[down], from_up, {"z": down})

                def add_first(mine=mine_pad, got=got_pad, size=size, far=far):
                    for i in range(4):
                        far[i] = plus(mine[i, :, :size], got[i, :, :size])

                def add_second(mine=mine_pad, got=got_pad, size=size, more=from_second):
                    for i in range(4):
                        more[i] = plus(mine[i, :, :size], got[i, :, :size], more[i])

                def add_two(more=from_second, two=from_two):
                    more[down] = plus(more[down], two[...])

                def add_z(more=from_second, a=from_down, b=from_up, total=total):
                    total[...] = plus(more[z], a[...], b[...])

                ticks[0] += [s_first.start]
                ticks[1] += [s_first.wait, load_mine.start, load_got.start]
                after += [load_mine.wait, load_got.wait, add_first, s_second.start]
                ticks[2] += [s_second.wait, load_near.start, load_rest.start]
                later += [load_near.wait, load_rest.wait, add_second, s_three.start, s_two.start]
                ticks[3] += [s_two.wait, add_two, s_one.start]
                ticks[4] += [s_three.wait, s_one.wait, add_z]
                final = total

            leave, left = crossing.prepare(final, out.at[every, columns])
            ticks[4] += [leave]
            ticks[5] += [left]
        ticks[1] += after
        ticks[2] += later
        chains.append(ticks)
    return chains


def sum_order(count):
    shares = ((1, 0.5), (2, 0.27), (3, 0.08), (4, 0.1), (5, 0.05))
    order = []
    passed = 0.0
    for tick, part in shares:
        order += [(n, tick, passed + part * (n + 1) / count) for n in range(count)]
        passed += part
    return order


def run_events(events):
    for event in events:
        event()


def sum_kernel(slots, count, real, *refs):
    terms, refs = refs[:count], refs[count:]
    home, q, k, v, do, o, h, w_q, w_k, w_v, x0, dx1, lse, gains, vectors = refs[:15]
    refs = refs[15:]
    outs, (home_out, frames_out, vectors_out) = refs[: count + 3], refs[count + 3 : count + 6]
    refs = refs[count + 6 :]
    lands = len([1 for _, _, sizes in slots for kind, order in enumerate(ORDERS) if sizes[kind] and order != "xyz"])
    landings, refs = refs[:lands], refs[lands:]
    send, recv, local, cross_send, cross_recv, cross_local, v_send, v_recv, h_send, h_recv, loads = refs[:11]
    four, ring, pad_a, pad_b, pad_c, pad_d, grads, grad_terms, far, got, near = refs[11:22]
    half, width = x0.shape
    rows, share = q.shape
    pairs = share // LANES
    tiles = rows // ROWS
    quarter = width // 4
    where = whereabouts()
    z, x, c, y, up, down, across = where
    every = slice(None)
    crossing = Crossing(c, y, cross_send, cross_recv, cross_local)
    all_terms = [*terms, *(grad_terms.at[i] for i in range(3))]
    pads = ((pad_a, pad_b), (pad_c, pad_d))
    chains = sum_events(where, slots, all_terms, outs, landings, refs[22:], pads, crossing, send, recv, local)
    early = [n for n, slot in enumerate(slots) if slot[0] < count]
    late = [n for n, slot in enumerate(slots) if slot[0] >= count]
    home_start, home_finish = crossing.prepare(home, home_out)
    frames_start, frames_finish = crossing.prepare(far, frames_out)
    greet(c, y, up, down, x, True)
    for n in early:
        run_events(chains[n][0])
    home_start()

    work = tiles * (tiles + 1) // 2
    times = [p + sum(tiles - i for i in range(j)) / work for p in range(pairs) for j in range(tiles)]
    times += [pairs + 0.9 * i for i in range(1, 5)]
    spots = {}
    for number, tick, part in sum_order(len(early)):
        due = part * SUM_TIME * pairs
        later = [i for i, time in enumerate(times) if time >= due]
        spots.setdefault(later[0] if later else len(times), []).append((early[number], tick))

    def at_spot(spot):
        for number, tick in spots.get(spot, []):
            run_events(chains[number][tick])

    def attention(pair_in, *held):
        def load(p, i):
            lanes = pl.ds(pl.multiple_of(p * LANES, LANES), LANES)
            slot = lax.rem(p, 2)
            source = (q, k, v, do, o)[i]
            return pltpu.make_async_copy(source.at[every, lanes], pair_in.at[slot, i], loads.at[slot, i])

        for i in range(5):
            load(0, i).start()

        def pair_step(p, carry):
            @pl.when(p + 1 < pairs)
            def _():
                for i in range(5):
                    load(p + 1, i).start()

            for i in range(5):
                load(p, i).wait()

            def hook(j):
                for turn in range(pairs):
                    if turn * tiles + j in spots:
                        @pl.when(p == turn)
                        def _(turn=turn):
                            at_spot(turn * tiles + j)

            lanes = pl.ds(pl.multiple_of(p * LANES, LANES), LANES)
            slot = lax.rem(p, 2)
            attend_back_kernel(
                half, real, *(pair_in.at[slot, i] for i in range(5)), lse.at[pl.ds(p, 1)],
                *(grads.at[i, every, lanes] for i in range(3)), *held, hook=hook,
            )
            return carry

        lax.fori_loop(0, pairs, pair_step, 0)

    pl.run_scoped(
        attention,
        pltpu.VMEM((2, 5, rows, LANES), BRAIN), pltpu.VMEM((rows, LANES), FLOAT), pltpu.VMEM((8, rows), FLOAT),
        pltpu.VMEM((tiles, 2 * ROWS, LANES), BRAIN), pltpu.VMEM((tiles, 2 * ROWS, LANES), BRAIN),
    )

    def exchange(part):
        columns = pl.ds(part * quarter, quarter)
        return pltpu.make_async_remote_copy(
            src_ref=far.at[every, columns], dst_ref=got.at[every, columns], send_sem=h_send.at[part],
            recv_sem=h_recv.at[part], device_id={"c": 1 - c}, device_id_type=MESH,
        )

    def projections(h_in, w_in):
        def load(part, i):
            slot = part % 2
            if i == 3:
                return pltpu.make_async_copy(h.at[every, pl.ds(part * quarter, quarter)], h_in.at[slot], loads.at[slot, 3])
            return pltpu.make_async_copy((w_q, w_k, w_v)[i].at[part], w_in.at[slot, i], loads.at[slot, i])

        for i in range(4):
            load(0, i).start()
        for part in range(4):
            if part < 3:
                for i in range(4):
                    load(part + 1, i).start()
            for i in range(4):
                load(part, i).wait()
            slot = part % 2
            columns = pl.ds(part * quarter, quarter)

            def grad_step(i, carry, part=part, slot=slot):
                product = dot_tn(h_in[slot], grads[i]).astype(BRAIN)
                grad_terms[i, part] = product.reshape(grad_terms.shape[2:])
                return carry

            def back_step(r, carry, slot=slot, columns=columns, out=None, base=0):
                here = pl.ds(pl.multiple_of(r * ROWS, ROWS), ROWS)
                there = pl.ds(pl.multiple_of(base + r * ROWS, ROWS), ROWS)
                total = dot_nt(grads[0, there, :], w_in[slot, 0].reshape(quarter, share))
                for i in (1, 2):
                    total = total + dot_nt(grads[i, there, :], w_in[slot, i].reshape(quarter, share))
                out[here, columns] = total.astype(out.dtype)
                return carry

            lax.fori_loop(0, half // ROWS, functools.partial(back_step, out=far, base=half), 0)
            exchange(part).start()
            lax.fori_loop(0, half // ROWS, functools.partial(back_step, out=near), 0)
            lax.fori_loop(0, 3, grad_step, 0)
            at_spot(pairs * tiles + part)

    pl.run_scoped(
        projections, pltpu.VMEM((2, rows, quarter), BRAIN), pltpu.VMEM((2, 3, *w_q.shape[1:]), BRAIN)
    )
    for n in late:
        run_events(chains[n][0])
    for part in range(4):
        exchange(part).wait()
    four[...] = vectors[...]

    def norm(x_in, dx_in):
        size = x_in.shape[1]

        def load(i):
            slot = lax.rem(i, 2)
            here = pl.ds(pl.multiple_of(i * size, size), size)
            return (
                pltpu.make_async_copy(x0.at[here], x_in.at[slot], loads.at[slot, 0]),
                pltpu.make_async_copy(dx1.at[here], dx_in.at[slot], loads.at[slot, 1]),
            )

        for copy in load(0):
            copy.start()

        def step(i, carry):
            @pl.when(i + 1 < half // size)
            def _():
                for copy in load(i + 1):
                    copy.start()

            for copy in load(i):
                copy.wait()
            slot = lax.rem(i, 2)
            here = pl.ds(pl.multiple_of(i * size, size), size)
            flow = near[here, :].astype(FLOAT) + got[here, :].astype(FLOAT)
            values, gain_sum, bias_sum = norm_back(x_in[slot].astype(FLOAT), gains[0:1, :], flow)
            far[here, :] = (dx_in[slot] + values).astype(BRAIN)
            four[0:1, :] += gain_sum[None, :]
            four[1:2, :] += bias_sum[None, :]
            return carry

        lax.fori_loop(0, half // size, step, 0)

    pl.run_scoped(norm, pltpu.VMEM((2, 96, width), BRAIN), pltpu.VMEM((2, 96, width), FLOAT))
    frames_start()

    def hop(at, src, dst, partner):
        return pltpu.make_async_remote_copy(
            src_ref=src, dst_ref=dst, send_sem=v_send.at[at], recv_sem=v_recv.at[at],
            device_id=partner, device_id_type=MESH,
        )

    held = ring
    held[0] = four[...]
    for at, partner in enumerate(({"c": 1 - c}, {"y": 1 - y}, {"x": 1 - x})):
        turn = hop(at, held.at[2 * at], held.at[2 * at + 1], partner)
        turn.start()
        turn.wait()
        total = held[2 * at] + held[2 * at + 1]
        if at < 2:
            held[2 * at + 2] = total
        else:
            held[6 + z] = total
    z_up = hop(3, held.at[6 + z], held.at[6 + z], {"z": up})
    z_down = hop(4, held.at[6 + z], held.at[6 + z], {"z": down})
    z_more = hop(5, held.at[6 + down], held.at[6 + down], {"z": up})
    z_up.start()
    z_down.start()
    z_up.wait()
    z_more.start()
    rest = spots.get(len(times), []) + [(n, tick) for n in late for tick in range(1, TICKS + 1)]
    for number, tick in sorted(rest, key=lambda event: (event[1], event[0])):
        run_events(chains[number][tick])
    z_down.wait()
    z_more.wait()
    vectors_out[...] = (held[6] + held[7]) + (held[8] + held[9])
    home_finish()
    frames_finish()


def sum_gradients(terms, home, attention, h, weights, x0, dx1, lse, gains, vectors, real, slots):
    count = len(terms)
    rows, share = attention[0].shape
    half, width = x0.shape
    size = terms[0].shape[3]
    crossings = 3 * len(slots) + 2
    dma = pltpu.SemaphoreType.DMA
    vmem = pl.BlockSpec(memory_space=pltpu.VMEM)
    landings = sum_landings(slots, size)
    widths = [t.shape[4] for t in terms] + [share] * 3
    most = [max(sizes[kind] for _, _, sizes in slots) for kind in range(2)]
    results = pl.pallas_call(
        functools.partial(sum_kernel, slots, count, real),
        in_specs=[ANY] * (count + 12) + [vmem] * 3,
        out_specs=[ANY] * (count + 5) + [vmem] + [ANY] * len(landings),
        out_shape=[jax.ShapeDtypeStruct((size, n), BRAIN) for n in widths]
        + [jax.ShapeDtypeStruct(home.shape, BRAIN), jax.ShapeDtypeStruct(x0.shape, BRAIN)]
        + [jax.ShapeDtypeStruct(vectors.shape, FLOAT)]
        + landings,
        scratch_shapes=[
            dma((len(slots), 3, 5)), dma((len(slots), 3, 5)), dma((len(slots), 3, 4)),
            dma((crossings,)), dma((crossings,)), dma((crossings,)), dma((6,)), dma((6,)),
            dma((4,)), dma((4,)), dma((2, 5)),
            pltpu.VMEM(vectors.shape, FLOAT), pltpu.VMEM((10, *vectors.shape), FLOAT),
            *[pltpu.VMEM((4, size, most[kind]), BRAIN) for kind in (0, 0, 1, 1)],
            pltpu.VMEM((3, rows, share), BRAIN), pltpu.VMEM((3, 4, 2, 2, size, share), BRAIN),
            pltpu.VMEM((half, width), BRAIN), pltpu.VMEM((half, width), BRAIN), pltpu.VMEM((half, width), BRAIN),
            *sum_scratch(slots, size),
        ],
        compiler_params=pltpu.CompilerParams(
            collective_id=3, has_side_effects=True, vmem_limit_bytes=58 * 2**20
        ),
        name="sum_gradients",
    )(*terms, home, *attention, h, *weights, x0, dx1, lse, gains, vectors)
    return results[: count + 6]


def slots_of(widths, six=((2, 3, 1), (2, 3, 1), (3, 2, 1)), eight=(3, 3, 2)):
    slots = []
    for which, width in enumerate(widths):
        tiles = width // LANES
        if tiles == 6:
            slots.append((which, 0, tuple(LANES * n for n in six[len(slots) % len(six)])))
        elif tiles % 8 == 0:
            for at in range(0, tiles, 8):
                slots.append((which, at * LANES, tuple(LANES * n for n in eight)))
        else:
            slots.append((which, 0, (width, 0, 0)))
    return tuple(slots)


def normalize(values, gain_vec, bias_vec):
    center = values - jnp.mean(values, -1, keepdims=True)
    spread = jnp.mean(center * center, -1, keepdims=True)
    return center * lax.rsqrt(spread + EPSILON) * gain_vec + bias_vec


def norm_back(values, gain_vec, grads):
    center = values - jnp.mean(values, -1, keepdims=True)
    scale_row = lax.rsqrt(jnp.mean(center * center, -1, keepdims=True) + EPSILON)
    normal = center * scale_row
    scaled = grads * gain_vec
    inner = jnp.mean(scaled * normal, -1, keepdims=True)
    grad_values = scale_row * (scaled - jnp.mean(scaled, -1, keepdims=True) - normal * inner)
    return grad_values, jnp.sum(grads * normal, 0), jnp.sum(grads, 0)


def gelu_pair(u):
    half_erf = 0.5 * (1.0 + lax.erf(u * (0.5**0.5)))
    density = jnp.exp(-0.5 * u * u) * ((2.0 * np.pi) ** -0.5)
    return (u * half_erf).astype(BRAIN), (half_erf + u * density).astype(BRAIN)


def split_heads(values):
    return values.reshape(values.shape[0], -1, HEAD_DIM)


def merge_heads(values):
    return values.reshape(values.shape[0], -1)


def attend_cross(q, k, v):
    scores = jnp.einsum("qhd,khd->hqk", q, k, preferred_element_type=FLOAT) * SCALE
    top = jnp.max(scores, -1, keepdims=True)
    e = jnp.exp(scores - top)
    total = jnp.sum(e, -1, keepdims=True)
    probs = e / total
    out = jnp.einsum("hqk,khd->qhd", probs.astype(BRAIN), v, preferred_element_type=FLOAT)
    return merge_heads(out).astype(BRAIN), (top + jnp.log(total))[..., 0]


def attend_cross_back(q, k, v, do, lse):
    scores = jnp.einsum("qhd,khd->hqk", q, k, preferred_element_type=FLOAT) * SCALE
    probs = jnp.exp(scores - lse[..., None])
    dp = jnp.einsum("qhd,khd->hqk", do, v, preferred_element_type=FLOAT)
    inner = jnp.sum(probs * dp, -1, keepdims=True)
    ds = (probs * (dp - inner)).astype(BRAIN)
    dq = jnp.einsum("hqk,khd->qhd", ds, k, preferred_element_type=FLOAT) * SCALE
    dk = jnp.einsum("hqk,qhd->khd", ds, q, preferred_element_type=FLOAT) * SCALE
    dv = jnp.einsum("hqk,qhd->khd", probs.astype(BRAIN), do, preferred_element_type=FLOAT)
    return tuple(merge_heads(t).astype(BRAIN) for t in (dq, dk, dv))


def on_device(
    inputs, text_states, teacher, valid_frames,
    self_norm_gain, self_norm_bias, self_query, self_key, self_value, self_out,
    cross_norm_gain, cross_norm_bias, cross_query, cross_key, cross_value, cross_out,
    feed_norm_gain, feed_norm_bias, feed_in, feed_out,
):
    at_core, at_y = lax.axis_index("c"), lax.axis_index("y")
    real, width = inputs.shape[1], inputs.shape[2]
    half = -(-real // ROWS) * ROWS
    block, share = self_query.shape
    hidden = feed_in.shape[1]

    fits = ring_fit()

    tiny = [self_norm_gain, self_norm_bias, cross_norm_gain, cross_norm_bias, feed_norm_gain, feed_norm_bias]
    count = jnp.sum(valid_frames)
    digits = jnp.stack([count // 64, count % 64]).astype(BRAIN)
    digits = jnp.where((jnp.arange(block) == 0)[:, None], digits[None, :], jnp.zeros((), BRAIN))
    tiny = jnp.pad(jnp.concatenate([jnp.stack(tiny, 1), digits], 1), ((0, 0), (0, LANES - 8)))
    weights = [
        tiny, self_query, self_key, self_value, self_out.T, cross_query, cross_key, cross_value, cross_out.T
    ]
    wide = [swap_weight(v) for v in (feed_in, feed_out.T)]

    def both(own):
        return jnp.concatenate([own, swap_core(own)], 0)

    def summed(left, weight):
        far = dot_nt(left[half:], weight).astype(BRAIN)
        got = swap_core(far)
        return dot_nt(left[:half], weight) + got.astype(FLOAT)

    def padded(v):
        return jnp.pad(v, ((0, half - real), (0, 0)))

    frames = padded(inputs[0])
    flags = jnp.pad(valid_frames[0][:, None].astype(BRAIN), ((0, 0), (0, LANES - 1)))
    target = padded(jnp.concatenate([teacher[0], flags], 1))
    if fits:
        slots = slots_of([v.shape[1] for v in weights])
        frames, *wide = lax.optimization_barrier((frames, *wide))
        *weights, x_own, text, target, gains, h1, q1, k1, v1, o1, lse1 = gather(
            weights, frames, text_states[0], target, real, slots
        )
        weights = [joined(v) for v in weights]
    else:
        weights = [lax.all_gather(swap_clip(v), CHIPS, axis=0, tiled=True) for v in weights]
        x_own, text, target = (swap_clip(v) for v in (frames, text_states[0], target))
        gains = weights[0].T.astype(FLOAT)
        x_all = jnp.concatenate([x_own, swap_core(x_own)], 0)
        h1 = normalize(x_all.astype(FLOAT), gains[0], gains[1]).astype(BRAIN)
        q1, k1, v1 = (dot_nn(h1, w).astype(BRAIN) for w in weights[1:4])
        o1, lse1 = attend_self(q1, k1, v1, real)
    tiny, w_q, w_k, w_v, w_so, w_cq, w_ck, w_cv, w_co = weights
    w_fi, w_fo = (lax.all_gather(v, CHIPS, axis=0, tiled=True) for v in wide)
    counted = jnp.sum(tiny[:, 6:8].astype(FLOAT), 0)
    counted = counted[0] * 64.0 + counted[1]
    token_count = counted + swap_core(counted)
    valid = target[:, width : width + 1].astype(FLOAT)
    target = target[:, :width].astype(FLOAT)
    x0 = x_own.astype(FLOAT)
    x1 = x0 + summed(o1, w_so)
    h2 = both(normalize(x1, gains[2], gains[3]).astype(BRAIN))
    q2 = dot_nn(h2, w_cq).astype(BRAIN)
    k2 = dot_nn(text, w_ck).astype(BRAIN)
    v2 = dot_nn(text, w_cv).astype(BRAIN)
    o2, lse2 = attend_cross(split_heads(q2), split_heads(k2), split_heads(v2))
    x2 = x1 + summed(o2, w_co)
    h3 = both(normalize(x2, gains[4], gains[5]).astype(BRAIN))
    g, slope = gelu_pair(dot_nn(h3, w_fi))
    y = x2 + summed(g, w_fo)
    home = y.astype(BRAIN)
    deviation = y - target
    error = jnp.sum(valid * deviation * deviation)
    tokens_all = real * lax.axis_size(("z", "x", "c", "y"))
    dy = (2.0 * tokens_all / token_count) * valid * deviation

    dyb = both(dy.astype(BRAIN))
    fo_grad = dot_tn(dyb, g).astype(BRAIN)
    dyb, fo_grad = lax.optimization_barrier((dyb, fo_grad))
    fo_grad = lax.psum_scatter(fo_grad, CHIPS, scatter_dimension=0, tiled=True)
    du = (slope.astype(FLOAT) * dot_nn(dyb, w_fo)).astype(BRAIN)
    fi_grad = dot_tn(h3, du).astype(BRAIN)
    fi_grad = lax.psum_scatter(fi_grad, CHIPS, scatter_dimension=0, tiled=True)
    term, gain3, bias3 = norm_back(x2, gains[4], summed(du, w_fi))
    dx2 = dy + term
    dx2b = both(dx2.astype(BRAIN))
    co_grad = dot_tn(dx2b, o2).astype(BRAIN)
    do2 = dot_nn(dx2b, w_co).astype(BRAIN)
    dq2, dk2, dv2 = attend_cross_back(
        split_heads(q2), split_heads(k2), split_heads(v2), split_heads(do2), lse2
    )
    cq_grad = dot_tn(h2, dq2).astype(BRAIN)
    ck_grad = dot_tn(text, dk2).astype(BRAIN)
    cv_grad = dot_tn(text, dv2).astype(BRAIN)
    text_part = (dot_nt(dk2, w_ck) + dot_nt(dv2, w_cv)).astype(BRAIN)
    text_mine = jnp.where(at_core == 0, text_part[:, : width // 2], text_part[:, width // 2 :])
    text_far = jnp.where(at_core == 0, text_part[:, width // 2 :], text_part[:, : width // 2])
    text_sum = text_mine.astype(FLOAT) + swap_core(text_far).astype(FLOAT)
    text_grad = swap_clip(text_sum.astype(BRAIN)).astype(FLOAT)[None]
    term, gain2, bias2 = norm_back(x1, gains[2], summed(dq2, w_cq))
    dx1 = dx2 + term
    dx1b = both(dx1.astype(BRAIN))
    so_grad = dot_tn(dx1b, o1).astype(BRAIN)
    do1 = dot_nn(dx1b, w_so).astype(BRAIN)
    zero = jnp.zeros((width,), FLOAT)
    vectors = jnp.stack([zero, zero, gain2, bias2, gain3, bias3])
    vectors = jnp.concatenate([vectors, jnp.full((2, width), error)], 0)
    grads = [co_grad, cq_grad, ck_grad, cv_grad, so_grad]
    if fits:
        slots = slots_of([v.shape[1] for v in grads] + [share] * 3, six=((2, 2, 2),))
        *grads, home, frames, vectors = sum_gradients(
            [by_chip(v) for v in grads], home, (q1, k1, v1, do1, o1), h1,
            [by_chip(v) for v in (w_q, w_k, w_v)], x_own, dx1, lse1, gains, vectors, real, slots,
        )
    else:
        dq1, dk1, dv1 = attend_self_back(q1, k1, v1, do1, o1, lse1, real)
        dh1 = dot_nt(dq1, w_q) + dot_nt(dk1, w_k) + dot_nt(dv1, w_v)
        dh1 = dh1[:half] + swap_core(dh1[half:].astype(BRAIN)).astype(FLOAT)
        term, gain1, bias1 = norm_back(x0, gains[0], dh1)
        frames = swap_clip((dx1 + term).astype(BRAIN))
        grads += [dot_tn(h1, d).astype(BRAIN) for d in (dq1, dk1, dv1)]
        grads = [swap_clip(lax.psum_scatter(v, CHIPS, scatter_dimension=0, tiled=True)) for v in grads]
        home = swap_clip(home)
        vectors = lax.psum(vectors.at[:2].set(jnp.stack([gain1, bias1])), ("z", "x", "c", "y"))
    layer_out = home[:real][None]
    inputs_grad = frames[None].astype(FLOAT)[:, :real]
    co_grad, cq_grad, ck_grad, cv_grad, so_grad, q_grad, k_grad, v_grad = (v.astype(FLOAT) for v in grads)
    fi_grad, fo_grad = swap_weight(fi_grad).astype(FLOAT), swap_weight(fo_grad).astype(FLOAT).T
    loss = vectors[6, 0] / (width * token_count)
    mine = block // 2
    place = (lax.axis_index(("z", "x", "c")) * 2 + at_y) * mine
    norms = lax.dynamic_slice(vectors, (0, place), (8, mine))
    return (
        loss, layer_out, inputs_grad, text_grad,
        norms[0], norms[1], q_grad, k_grad, v_grad, so_grad.T,
        norms[2], norms[3], cq_grad, ck_grad, cv_grad, co_grad.T,
        norms[4], norms[5], fi_grad, fo_grad,
    )


def solution(mesh):
    outer = mesh.shape["dp"] // 4
    fine = Mesh(np.array(mesh.devices).reshape(outer, 2, 2, 2), ("z", "x", "c", "y"))
    dp = ("z", "x", "c")
    frames = P(dp, "y", None)
    vector, wide, tall = P(dp), P(dp, "y"), P("y", dp)
    small = P(("z", "x", "c", "y"))
    attention = (vector, vector, wide, wide, wide, tall)
    return jax.shard_map(
        on_device,
        mesh=fine,
        in_specs=(frames, P(dp, None, None), frames, P(dp, "y"), *attention, *attention, vector, vector, wide, tall),
        out_specs=(
            P(), frames, frames, P(dp, None, "y"),
            small, small, wide, wide, wide, tall,
            small, small, wide, wide, wide, tall,
            small, small, wide, tall,
        ),
        check_vma=False,
    )
```

```python
import functools

import jax
import jax.numpy as jnp
import numpy as np
from jax import lax
from jax.experimental import pallas as pl
from jax.experimental.pallas import tpu as pltpu
from jax.sharding import Mesh
from jax.sharding import PartitionSpec as P

HEAD_DIM = 64
LANES = 128
ROWS = 256
FLOAT = jnp.float32
BRAIN = jnp.bfloat16
NEGATIVE = -1e30
EPSILON = 1e-05
SCALE = HEAD_DIM ** (-0.5)
CHIPS = ("z", "x", "y")
MESH = pl.DeviceIdType.MESH


def swap_core(v):
    return lax.ppermute(v, "c", [(0, 1), (1, 0)])


def swap_clip(v):
    return lax.ppermute(v, ("c", "y"), [(0, 0), (1, 2), (2, 1), (3, 3)])


def swap_others(v):
    return lax.ppermute(v, ("c", "y"), [(1, 2), (2, 1)])


def swap_weight(v):
    return jnp.where(lax.axis_index("c") == lax.axis_index("y"), v, swap_others(v))


def ring_fit():
    return lax.axis_size("z") == 4 and lax.axis_size("x") == 2 and lax.axis_size("y") == 2


def by_chip(v):
    return v.reshape(4, 2, 2, v.shape[0] // 16, v.shape[1])


def joined(v):
    return v.reshape(-1, v.shape[-1])


def dot_nt(a, b, **kw):
    return lax.dot_general(a, b, (((1,), (1,)), ((), ())), preferred_element_type=FLOAT, **kw)


def dot_nn(a, b):
    return lax.dot_general(a, b, (((1,), (0,)), ((), ())), preferred_element_type=FLOAT)


def dot_tn(a, b):
    return lax.dot_general(a, b, (((0,), (0,)), ((), ())), preferred_element_type=FLOAT)


def attend_kernel(half, real, q_ref, k_ref, v_ref, o_ref, lse_ref):
    core = lax.axis_index("c")
    per_half = half // ROWS
    blocks = 2 * per_half
    lane = lax.broadcasted_iota(jnp.int32, (ROWS, LANES), 1)
    first = lane < HEAD_DIM
    rows_at = lax.broadcasted_iota(jnp.int32, (ROWS, ROWS), 0)
    cols_at = lax.broadcasted_iota(jnp.int32, (ROWS, ROWS), 1)

    def place(i):
        start = jnp.where(core == i // per_half, 0, half) + (i % per_half) * ROWS
        return pl.ds(pl.multiple_of(start, ROWS), ROWS)

    for i in range(blocks):
        queries = q_ref[place(i), :].astype(FLOAT) * SCALE
        outs = []
        logs = []
        for head in range(2):
            mine = first if head == 0 else jnp.logical_not(first)
            masked = jnp.where(mine, queries, 0.0).astype(BRAIN)
            scores = []
            for j in range(i + 1):
                s = dot_nt(masked, k_ref[place(j), :])
                if j == i:
                    s = jnp.where(cols_at <= rows_at, s, NEGATIVE)
                elif j == per_half - 1:
                    s = jnp.where(cols_at < real - (per_half - 1) * ROWS, s, NEGATIVE)
                scores.append(s)
            top = scores[0]
            for s in scores[1:]:
                top = jnp.maximum(top, s)
            top = jnp.max(top, 1, keepdims=True)
            total = None
            out = None
            for j in range(i + 1):
                e = jnp.exp(scores[j] - top)
                total = e if total is None else total + e
                term = dot_nn(e.astype(BRAIN), v_ref[place(j), :])
                out = term if out is None else out + term
            total = jnp.sum(total, 1, keepdims=True)
            outs.append(out / total)
            logs.append(top + jnp.log(total))
        o_ref[place(i), :] = jnp.where(first, outs[0], outs[1]).astype(BRAIN)
        both = jnp.where(lane == 0, logs[0], logs[1])
        lse_ref[0, :, i * ROWS : (i + 1) * ROWS] = both.T[:8, :]


def attend_self(q, k, v, real):
    rows, width = q.shape
    pairs = width // LANES
    spec = pl.BlockSpec((rows, LANES), lambda p: (0, p))
    return pl.pallas_call(
        functools.partial(attend_kernel, rows // 2, real),
        grid=(pairs,),
        in_specs=[spec, spec, spec],
        out_specs=[spec, pl.BlockSpec((1, 8, rows), lambda p: (p, 0, 0))],
        out_shape=[
            jax.ShapeDtypeStruct((rows, width), BRAIN),
            jax.ShapeDtypeStruct((pairs, 8, rows), FLOAT),
        ],
        compiler_params=pltpu.CompilerParams(vmem_limit_bytes=48 * 2**20),
        cost_estimate=pl.CostEstimate(
            flops=10 * rows * rows * width, bytes_accessed=8 * rows * width, transcendentals=0
        ),
        name="attend",
    )(q, k, v)


def attend_back_kernel(
    half, real, q_ref, k_ref, v_ref, do_ref, o_ref, lse_ref, dq_ref, dk_ref, dv_ref,
    dq_sum, inner, q_two, do_two, hook=None,
):
    core = lax.axis_index("c")
    per_half = half // ROWS
    blocks = 2 * per_half
    first = lax.broadcasted_iota(jnp.int32, (ROWS, LANES), 1) < HEAD_DIM
    key_at = lax.broadcasted_iota(jnp.int32, (ROWS, 2 * ROWS), 0)
    query_at = lax.broadcasted_iota(jnp.int32, (ROWS, 2 * ROWS), 1) % ROWS
    pick = lax.broadcasted_iota(jnp.int32, (8, LANES), 1) // HEAD_DIM
    pick = (pick == lax.broadcasted_iota(jnp.int32, (8, LANES), 0)).astype(FLOAT)

    def place(i):
        start = jnp.where(core == i // per_half, 0, half) + (i % per_half) * ROWS
        return pl.ds(pl.multiple_of(start, ROWS), ROWS)

    def side_by_side(ref, i):
        return jnp.concatenate([ref[0:1, i * ROWS : (i + 1) * ROWS], ref[1:2, i * ROWS : (i + 1) * ROWS]], 1)

    for i in range(blocks):
        grads = do_ref[place(i), :].astype(FLOAT)
        queries = q_ref[place(i), :].astype(FLOAT) * SCALE
        product = grads * o_ref[place(i), :].astype(FLOAT)
        inner[:, i * ROWS : (i + 1) * ROWS] = dot_nt(pick, product, precision=lax.Precision.HIGHEST)
        q_two[i, :ROWS] = jnp.where(first, queries, 0.0).astype(BRAIN)
        q_two[i, ROWS:] = jnp.where(first, 0.0, queries).astype(BRAIN)
        do_two[i, :ROWS] = jnp.where(first, grads, 0.0).astype(BRAIN)
        do_two[i, ROWS:] = jnp.where(first, 0.0, grads).astype(BRAIN)
    dq_sum[...] = jnp.zeros_like(dq_sum)

    for j in range(blocks):
        if hook is not None:
            hook(j)
        keys = k_ref[place(j), :]
        values = v_ref[place(j), :]
        dk = dv = None
        for i in range(j, blocks):
            rows = pl.ds(i * ROWS, ROWS)
            q_m, do_m = q_two[i], do_two[i]
            s = dot_nt(keys, q_m) - side_by_side(lse_ref.at[0], i)
            if i == j:
                s = jnp.where(key_at <= query_at, s, NEGATIVE)
            elif j == per_half - 1:
                s = jnp.where(key_at < real - j * ROWS, s, NEGATIVE)
            p = jnp.exp(s)
            dp = dot_nt(values, do_m)
            ds = (p * (dp - side_by_side(inner, i))).astype(BRAIN)
            dv_term = dot_nn(p.astype(BRAIN), do_m)
            dk_term = dot_nn(ds, q_m)
            dk = dk_term if dk is None else dk + dk_term
            dv = dv_term if dv is None else dv + dv_term
            dq = dot_tn(ds, keys)
            dq_sum[rows, :] += jnp.where(first, dq[:ROWS], dq[ROWS:])
        dk_ref[place(j), :] = dk.astype(BRAIN)
        dv_ref[place(j), :] = dv.astype(BRAIN)

    for i in range(blocks):
        dq_ref[place(i), :] = (dq_sum[i * ROWS : (i + 1) * ROWS, :] * SCALE).astype(BRAIN)


def attend_self_back(q, k, v, do, o, lse, real):
    rows, width = q.shape
    pairs = width // LANES
    spec = pl.BlockSpec((rows, LANES), lambda p: (0, p))
    return pl.pallas_call(
        functools.partial(attend_back_kernel, rows // 2, real),
        grid=(pairs,),
        in_specs=[spec] * 5 + [pl.BlockSpec((1, 8, rows), lambda p: (p, 0, 0))],
        out_specs=[spec] * 3,
        scratch_shapes=[
            pltpu.VMEM((rows, LANES), FLOAT),
            pltpu.VMEM((8, rows), FLOAT),
            pltpu.VMEM((rows // ROWS, 2 * ROWS, LANES), BRAIN),
            pltpu.VMEM((rows // ROWS, 2 * ROWS, LANES), BRAIN),
        ],
        out_shape=[jax.ShapeDtypeStruct((rows, width), BRAIN)] * 3,
        compiler_params=pltpu.CompilerParams(vmem_limit_bytes=48 * 2**20),
        cost_estimate=pl.CostEstimate(
            flops=25 * rows * rows * width, bytes_accessed=16 * rows * width, transcendentals=0
        ),
        name="attend_back",
    )(q, k, v, do, o, lse)


ORDERS = ("zxy", "zyx", "xyz")
TICKS = 5
SUM_TIME = 2.2


def whereabouts():
    z, x, c, y = (lax.axis_index(name) for name in ("z", "x", "c", "y"))
    return z, x, c, y, lax.rem(z + 1, 4), lax.rem(z + 3, 4), lax.rem(z + 2, 4)


def greet(c, y, up, down, x, cores):
    barrier = pltpu.get_barrier_semaphore()
    partners = [{"z": up}, {"z": down}, {"x": 1 - x}, {"y": 1 - y}]
    if cores:
        partners.append({"c": 1 - c})
    for partner in partners:
        pl.semaphore_signal(barrier, inc=1, device_id=partner, device_id_type=MESH)

    @pl.when(c != y)
    def _():
        pl.semaphore_signal(barrier, inc=1, device_id={"c": y, "y": c}, device_id_type=MESH)
        pl.semaphore_wait(barrier, len(partners) + 1)

    @pl.when(c == y)
    def _():
        pl.semaphore_wait(barrier, len(partners))


def one(i):
    return pl.ds(i, 1)


class Crossing:
    def __init__(self, c, y, send, recv, local):
        self.c, self.y, self.send, self.recv, self.local = c, y, send, recv, local
        self.used = 0

    def begin(self, src, dst):
        start, finish = self.prepare(src, dst)
        start()
        return finish

    def prepare(self, src, dst):
        at = self.used
        self.used += 1
        far = pltpu.make_async_remote_copy(
            src_ref=src, dst_ref=dst, send_sem=self.send.at[at], recv_sem=self.recv.at[at],
            device_id={"c": self.y, "y": self.c}, device_id_type=MESH,
        )
        near = pltpu.make_async_copy(src, dst, self.local.at[at])

        def start():
            @pl.when(self.c != self.y)
            def _():
                far.start()

            @pl.when(self.c == self.y)
            def _():
                near.start()

        def finish():
            @pl.when(self.c != self.y)
            def _():
                far.wait()

            @pl.when(self.c == self.y)
            def _():
                near.wait()

        return start, finish


def gather_events(where, slots, weights, send, recv):
    z, x, c, y, up, down, across = where
    every = slice(None)
    chains = []
    for number, (which, start, sizes) in enumerate(slots):
        ref = weights[which]
        ticks = [[] for _ in range(TICKS)]
        for kind, order in enumerate(ORDERS):
            size = sizes[kind]
            if size == 0:
                continue
            columns = pl.ds(start, size)
            start += size

            def copy(at, region, partner, ref=ref, columns=columns, kind=kind, number=number):
                view = ref.at[(*region, every, columns)]
                return pltpu.make_async_remote_copy(
                    src_ref=view, dst_ref=view, send_sem=send.at[number, kind, at],
                    recv_sem=recv.at[number, kind, at], device_id=partner, device_id_type=MESH,
                )

            if order == "xyz":
                by_x = copy(0, (one(z), one(x), one(y)), {"x": 1 - x})
                by_y = copy(1, (one(z), every, one(y)), {"y": 1 - y})
                rest = (every, every)
            else:
                rest = (one(x), one(y))
            z_up = copy(2, (one(z), *rest), {"z": up})
            z_down = copy(3, (one(z), *rest), {"z": down})
            z_more = copy(4, (one(down), *rest), {"z": up})
            if order == "xyz":
                ticks[0] += [by_x.start]
                ticks[1] += [by_x.wait, by_y.start]
                ticks[2] += [by_y.wait, z_up.start, z_down.start]
                ticks[3] += [z_up.wait, z_more.start]
                ticks[4] += [z_down.wait, z_more.wait]
            else:
                if order == "zxy":
                    near = copy(0, (every, one(x), one(y)), {"x": 1 - x})
                    far = copy(1, (every, every, one(y)), {"y": 1 - y})
                else:
                    near = copy(0, (every, one(x), one(y)), {"y": 1 - y})
                    far = copy(1, (every, one(x), every), {"x": 1 - x})
                ticks[0] += [z_up.start, z_down.start]
                ticks[1] += [z_up.wait, z_more.start]
                ticks[2] += [z_down.wait, z_more.wait, near.start]
                ticks[3] += [near.wait, far.start]
                ticks[4] += [far.wait]
        chains.append(ticks)
    return chains


def run_tick(chains, at):
    for number, ticks in enumerate(chains):
        if 0 <= at - number < TICKS:
            for event in ticks[at - number]:
                event()


def total_ticks(slots):
    return len(slots) + TICKS - 1


def bring_own(crossing, where, slots, chains, blocks, weights):
    z, x, c = where[:3]
    for which, (block, weight) in enumerate(zip(blocks, weights)):
        start, finish = crossing.prepare(block, weight.at[z, x, c])
        number = [slot[0] for slot in slots].index(which)
        chains[number][0].insert(0, finish)
        yield start


ANY = pl.BlockSpec(memory_space=pl.ANY)
NEEDED_FIRST = 4


def gather_kernel(slots, count, real, *refs):
    blocks, (frames, text) = refs[:count], refs[count : count + 2]
    refs = refs[count + 2 :]
    weights, (own_out, text_out) = refs[:count], refs[count : count + 2]
    gains_ref, h_ref, q_ref, k_ref, v_ref, o_ref, lse_ref = refs[count + 2 : count + 9]
    send, recv, cross_send, cross_recv, cross_local, core_send, core_recv, loads, tiny, both, held = refs[count + 9 :]
    rows, width = h_ref.shape
    half = rows // 2
    pairs = q_ref.shape[1] // LANES
    where = whereabouts()
    z, x, c, y, up, down, across = where
    crossing = Crossing(c, y, cross_send, cross_recv, cross_local)
    chains = gather_events(where, slots, weights, send, recv)
    starts = list(bring_own(crossing, where, slots, chains, blocks, weights))
    frames_start, frames_finish = crossing.prepare(frames, both.at[0])
    text_start, text_finish = crossing.prepare(text, text_out)
    sibling = pltpu.make_async_remote_copy(
        src_ref=both.at[0], dst_ref=both.at[1], send_sem=core_send, recv_sem=core_recv,
        device_id={"c": 1 - c}, device_id_type=MESH,
    )
    keep = pltpu.make_async_copy(both.at[0], own_out, loads.at[4])
    fetch = [pltpu.make_async_copy(weights[0], tiny, loads.at[0])]
    fetch += [pltpu.make_async_copy(weights[i + 1], held.at[i], loads.at[i + 1]) for i in range(3)]

    def tick(at):
        for number in reversed(range(len(slots))):
            stage = at - number
            last = TICKS if number < NEEDED_FIRST else TICKS - 1
            if 0 <= stage < last:
                run_events(chains[number][stage])

    greet(c, y, up, down, x, True)
    for start in starts:
        start()
    ready = NEEDED_FIRST + TICKS - 1
    for at in range(ready):
        tick(at)
        if at == 2:
            frames_start()
            text_start()
        if at == 5:
            frames_finish()
            sibling.start()
            keep.start()
        if at == ready - 4:
            fetch[0].start()
    for copy in fetch[1:]:
        copy.start()
    sibling.wait()
    fetch[0].wait()
    gains_ref[...] = tiny[...].reshape(width, LANES).astype(FLOAT).T[:8, :]

    def norm_step(i, carry):
        here = pl.ds(pl.multiple_of(i * LANES, LANES), LANES)
        for side in range(2):
            there = pl.ds(pl.multiple_of(side * half + i * LANES, LANES), LANES)
            h_ref[there, :] = normalize(both[side, here, :].astype(FLOAT), gains_ref[0:1, :], gains_ref[1:2, :]).astype(BRAIN)
        return carry

    lax.fori_loop(0, half // LANES, norm_step, 0)
    later = list(range(ready, len(slots) + TICKS - 2))
    tick(later.pop(0))
    for i, out in enumerate((q_ref, k_ref, v_ref)):
        fetch[i + 1].wait()

        def project_step(r, carry, i=i, out=out):
            here = pl.ds(pl.multiple_of(r * ROWS, ROWS), ROWS)
            out[here, :] = dot_nn(h_ref[here, :], held[i].reshape(width, -1)).astype(BRAIN)
            return carry

        lax.fori_loop(0, rows // ROWS, project_step, 0)
        if later:
            tick(later.pop(0))

    def pair_step(p, carry):
        for turn in range(pairs):
            if turn < len(later):
                @pl.when(p == turn)
                def _(turn=turn):
                    tick(later[turn])

        lanes = pl.ds(pl.multiple_of(p * LANES, LANES), LANES)
        every = slice(None)
        q, k, v, o = (ref.at[every, lanes] for ref in (q_ref, k_ref, v_ref, o_ref))
        attend_kernel(half, real, q, k, v, o, lse_ref.at[pl.ds(p, 1)])
        return carry

    lax.fori_loop(0, pairs, pair_step, 0)
    for at in later[pairs:]:
        tick(at)
    for ticks in chains[NEEDED_FIRST:]:
        run_events(ticks[TICKS - 1])
    keep.wait()
    text_finish()


def gather(blocks, frames, text, real, slots):
    count = len(blocks)
    rows, width = 2 * frames.shape[0], frames.shape[1]
    share = blocks[1].shape[1]
    pairs = share // LANES
    crossings = count + 2
    dma = pltpu.SemaphoreType.DMA
    vmem = pl.BlockSpec(memory_space=pltpu.VMEM)
    heads = jax.ShapeDtypeStruct((rows, share), BRAIN)
    gathered = [jax.ShapeDtypeStruct((4, 2, 2, *b.shape), BRAIN) for b in blocks]
    return pl.pallas_call(
        functools.partial(gather_kernel, slots, count, real),
        out_shape=[
            *gathered,
            *[jax.ShapeDtypeStruct(v.shape, v.dtype) for v in (frames, text)],
            jax.ShapeDtypeStruct((8, width), FLOAT), jax.ShapeDtypeStruct((rows, width), BRAIN),
            heads, heads, heads, heads, jax.ShapeDtypeStruct((pairs, 8, rows), FLOAT),
        ],
        in_specs=[ANY] * (count + 2),
        out_specs=[ANY] * (count + 2) + [vmem] * 7,
        scratch_shapes=[
            dma((len(slots), 3, 5)), dma((len(slots), 3, 5)),
            dma((crossings,)), dma((crossings,)), dma((crossings,)), dma, dma, dma((5,)),
            pltpu.VMEM(gathered[0].shape, BRAIN), pltpu.VMEM((2, *frames.shape), BRAIN),
            pltpu.VMEM((3, *gathered[1].shape), BRAIN),
        ],
        compiler_params=pltpu.CompilerParams(
            collective_id=1, has_side_effects=True, vmem_limit_bytes=56 * 2**20
        ),
        name="gather",
    )(*blocks, frames, text)


def plus(*terms):
    total = terms[0].astype(FLOAT)
    for term in terms[1:]:
        total = total + term.astype(FLOAT)
    return total.astype(BRAIN)


def sum_scratch(slots, rows):
    shapes = []
    for _, _, sizes in slots:
        for kind, order in enumerate(ORDERS):
            size = sizes[kind]
            if size == 0:
                continue
            if order == "xyz":
                leads = [(2, 2, 2), (2, 2), (2, 2), (2, 2), (2,), ()]
            else:
                leads = [(4,), (4,), (), (), (), ()]
            shapes += [pltpu.VMEM((*lead, rows, size), BRAIN) for lead in leads]
    return shapes


def sum_landings(slots, rows):
    return [
        jax.ShapeDtypeStruct((4, 2, rows, sizes[kind]), BRAIN)
        for _, _, sizes in slots
        for kind, order in enumerate(ORDERS)
        if sizes[kind] and order != "xyz"
    ]


def sum_events(where, slots, terms, outs, landings, buffers, pads, crossing, send, recv, local):
    z, x, c, y, up, down, across = where
    every = slice(None)
    chains = []
    taken = landed = 0
    for number, (which, start, sizes) in enumerate(slots):
        ref, out = terms[which], outs[which]
        ticks = [[] for _ in range(TICKS + 1)]
        after, later = [], []
        for kind, order in enumerate(ORDERS):
            size = sizes[kind]
            if size == 0:
                continue
            columns = pl.ds(start, size)
            start += size
            need = 6
            held = buffers[taken : taken + need]
            taken += need

            def copy(at, src, dst, partner, kind=kind, number=number):
                return pltpu.make_async_remote_copy(
                    src_ref=src, dst_ref=dst, send_sem=send.at[number, kind, at],
                    recv_sem=recv.at[number, kind, at], device_id=partner, device_id_type=MESH,
                )

            def view(*region, ref=ref, columns=columns):
                return ref.at[(*region, every, columns)]

            if order == "xyz":
                own, from_two, from_down, from_up, from_y, from_x = held
                load_a = pltpu.make_async_copy(view(z, every, every), own.at[0], local.at[number, kind, 0])
                load_b = pltpu.make_async_copy(view(down, every, every), own.at[1], local.at[number, kind, 1])
                s_three = copy(0, view(up, every, every), from_down, {"z": up})
                s_two = copy(1, view(across, every, every), from_two, {"z": down})
                s_one = copy(2, own.at[1], from_up, {"z": down})
                s_y = copy(3, own.at[0, every, 1 - y], from_y, {"y": 1 - y})
                s_x = copy(4, from_y.at[1 - x], from_x, {"x": 1 - x})

                def add_two(own=own, from_two=from_two):
                    for i in range(2):
                        for j in range(2):
                            own[1, i, j] = plus(own[1, i, j], from_two[i, j])

                def add_z(own=own, a=from_down, b=from_up):
                    for i in range(2):
                        for j in range(2):
                            own[0, i, j] = plus(own[0, i, j], a[i, j], b[i, j])

                def add_y(own=own, from_y=from_y):
                    for i in range(2):
                        from_y[i] = plus(own[0, i, y], from_y[i])

                def add_x(from_y=from_y, from_x=from_x):
                    from_x[...] = plus(from_y[x], from_x[...])

                ticks[0] += [load_a.start, load_b.start, s_three.start, s_two.start]
                ticks[1] += [s_two.wait, load_b.wait, add_two, s_one.start]
                ticks[2] += [s_three.wait, load_a.wait, s_one.wait, add_z, s_y.start]
                ticks[3] += [s_y.wait, add_y, s_x.start]
                ticks[4] += [s_x.wait, add_x]
                final = from_x
            else:
                from_second, far, from_two, from_down, from_up, total = held
                landing = landings[landed]
                landed += 1
                mine_at, got_at = (pad.at[every, every, pl.ds(0, size)] for pad in pads[kind])
                mine_pad, got_pad = pads[kind]
                if order == "zxy":
                    mine, theirs = view(every, 1 - x, y), view(every, every, 1 - y)
                    first, second = {"y": 1 - y}, {"x": 1 - x}
                    side = x
                else:
                    mine, theirs = view(every, x, 1 - y), view(every, 1 - x, every)
                    first, second = {"x": 1 - x}, {"y": 1 - y}
                    side = y
                load_mine = pltpu.make_async_copy(mine, mine_at, local.at[number, kind, 0])
                load_got = pltpu.make_async_copy(landing.at[every, 1 - side], got_at, local.at[number, kind, 1])
                load_near = pltpu.make_async_copy(view(every, x, y), mine_at, local.at[number, kind, 2])
                load_rest = pltpu.make_async_copy(landing.at[every, side], got_at, local.at[number, kind, 3])
                s_first = copy(0, theirs, landing, first)
                s_second = copy(1, far, from_second, second)
                s_three = copy(2, from_second.at[up], from_down, {"z": up})
                s_two = copy(3, from_second.at[across], from_two, {"z": down})
                s_one = copy(4, from_second.at[down], from_up, {"z": down})

                def add_first(mine=mine_pad, got=got_pad, size=size, far=far):
                    for i in range(4):
                        far[i] = plus(mine[i, :, :size], got[i, :, :size])

                def add_second(mine=mine_pad, got=got_pad, size=size, more=from_second):
                    for i in range(4):
                        more[i] = plus(mine[i, :, :size], got[i, :, :size], more[i])

                def add_two(more=from_second, two=from_two):
                    more[down] = plus(more[down], two[...])

                def add_z(more=from_second, a=from_down, b=from_up, total=total):
                    total[...] = plus(more[z], a[...], b[...])

                ticks[0] += [s_first.start]
                ticks[1] += [s_first.wait, load_mine.start, load_got.start]
                after += [load_mine.wait, load_got.wait, add_first, s_second.start]
                ticks[2] += [s_second.wait, load_near.start, load_rest.start]
                later += [load_near.wait, load_rest.wait, add_second, s_three.start, s_two.start]
                ticks[3] += [s_two.wait, add_two, s_one.start]
                ticks[4] += [s_three.wait, s_one.wait, add_z]
                final = total

            leave, left = crossing.prepare(final, out.at[every, columns])
            ticks[4] += [leave]
            ticks[5] += [left]
        ticks[1] += after
        ticks[2] += later
        chains.append(ticks)
    return chains


def sum_order(count):
    shares = ((1, 0.5), (2, 0.27), (3, 0.08), (4, 0.1), (5, 0.05))
    order = []
    passed = 0.0
    for tick, part in shares:
        order += [(n, tick, passed + part * (n + 1) / count) for n in range(count)]
        passed += part
    return order


def run_events(events):
    for event in events:
        event()


def sum_kernel(slots, count, real, *refs):
    terms, refs = refs[:count], refs[count:]
    q, k, v, do, o, h, w_q, w_k, w_v, x0, dx1, lse, gains, vectors = refs[:14]
    refs = refs[14:]
    outs, (frames_out, vectors_out) = refs[: count + 3], refs[count + 3 : count + 5]
    refs = refs[count + 5 :]
    lands = len([1 for _, _, sizes in slots for kind, order in enumerate(ORDERS) if sizes[kind] and order != "xyz"])
    landings, refs = refs[:lands], refs[lands:]
    send, recv, local, cross_send, cross_recv, cross_local, v_send, v_recv, h_send, h_recv, loads = refs[:11]
    four, ring, pad_a, pad_b, pad_c, pad_d, grads, grad_terms, far, got, near = refs[11:22]
    half, width = x0.shape
    rows, share = q.shape
    pairs = share // LANES
    tiles = rows // ROWS
    quarter = width // 4
    where = whereabouts()
    z, x, c, y, up, down, across = where
    every = slice(None)
    crossing = Crossing(c, y, cross_send, cross_recv, cross_local)
    all_terms = [*terms, *(grad_terms.at[i] for i in range(3))]
    pads = ((pad_a, pad_b), (pad_c, pad_d))
    chains = sum_events(where, slots, all_terms, outs, landings, refs[22:], pads, crossing, send, recv, local)
    early = [n for n, slot in enumerate(slots) if slot[0] < count]
    late = [n for n, slot in enumerate(slots) if slot[0] >= count]
    frames_start, frames_finish = crossing.prepare(far, frames_out)
    greet(c, y, up, down, x, True)
    for n in early:
        run_events(chains[n][0])

    work = tiles * (tiles + 1) // 2
    times = [p + sum(tiles - i for i in range(j)) / work for p in range(pairs) for j in range(tiles)]
    times += [pairs + 0.9 * i for i in range(1, 5)]
    spots = {}
    for number, tick, part in sum_order(len(early)):
        due = part * SUM_TIME * pairs
        later = [i for i, time in enumerate(times) if time >= due]
        spots.setdefault(later[0] if later else len(times), []).append((early[number], tick))

    def at_spot(spot):
        for number, tick in spots.get(spot, []):
            run_events(chains[number][tick])

    def attention(pair_in, *held):
        def load(p, i):
            lanes = pl.ds(pl.multiple_of(p * LANES, LANES), LANES)
            slot = lax.rem(p, 2)
            source = (q, k, v, do, o)[i]
            return pltpu.make_async_copy(source.at[every, lanes], pair_in.at[slot, i], loads.at[slot, i])

        for i in range(5):
            load(0, i).start()

        def pair_step(p, carry):
            @pl.when(p + 1 < pairs)
            def _():
                for i in range(5):
                    load(p + 1, i).start()

            for i in range(5):
                load(p, i).wait()

            def hook(j):
                for turn in range(pairs):
                    if turn * tiles + j in spots:
                        @pl.when(p == turn)
                        def _(turn=turn):
                            at_spot(turn * tiles + j)

            lanes = pl.ds(pl.multiple_of(p * LANES, LANES), LANES)
            slot = lax.rem(p, 2)
            attend_back_kernel(
                half, real, *(pair_in.at[slot, i] for i in range(5)), lse.at[pl.ds(p, 1)],
                *(grads.at[i, every, lanes] for i in range(3)), *held, hook=hook,
            )
            return carry

        lax.fori_loop(0, pairs, pair_step, 0)

    pl.run_scoped(
        attention,
        pltpu.VMEM((2, 5, rows, LANES), BRAIN), pltpu.VMEM((rows, LANES), FLOAT), pltpu.VMEM((8, rows), FLOAT),
        pltpu.VMEM((tiles, 2 * ROWS, LANES), BRAIN), pltpu.VMEM((tiles, 2 * ROWS, LANES), BRAIN),
    )

    def exchange(part):
        columns = pl.ds(part * quarter, quarter)
        return pltpu.make_async_remote_copy(
            src_ref=far.at[every, columns], dst_ref=got.at[every, columns], send_sem=h_send.at[part],
            recv_sem=h_recv.at[part], device_id={"c": 1 - c}, device_id_type=MESH,
        )

    def projections(h_in, w_in):
        def load(part, i):
            slot = part % 2
            if i == 3:
                return pltpu.make_async_copy(h.at[every, pl.ds(part * quarter, quarter)], h_in.at[slot], loads.at[slot, 3])
            return pltpu.make_async_copy((w_q, w_k, w_v)[i].at[part], w_in.at[slot, i], loads.at[slot, i])

        for i in range(4):
            load(0, i).start()
        for part in range(4):
            if part < 3:
                for i in range(4):
                    load(part + 1, i).start()
            for i in range(4):
                load(part, i).wait()
            slot = part % 2
            columns = pl.ds(part * quarter, quarter)

            def grad_step(i, carry, part=part, slot=slot):
                product = dot_tn(h_in[slot], grads[i]).astype(BRAIN)
                grad_terms[i, part] = product.reshape(grad_terms.shape[2:])
                return carry

            def back_step(r, carry, slot=slot, columns=columns, out=None, base=0):
                here = pl.ds(pl.multiple_of(r * ROWS, ROWS), ROWS)
                there = pl.ds(pl.multiple_of(base + r * ROWS, ROWS), ROWS)
                total = dot_nt(grads[0, there, :], w_in[slot, 0].reshape(quarter, share))
                for i in (1, 2):
                    total = total + dot_nt(grads[i, there, :], w_in[slot, i].reshape(quarter, share))
                out[here, columns] = total.astype(out.dtype)
                return carry

            lax.fori_loop(0, half // ROWS, functools.partial(back_step, out=far, base=half), 0)
            exchange(part).start()
            lax.fori_loop(0, half // ROWS, functools.partial(back_step, out=near), 0)
            lax.fori_loop(0, 3, grad_step, 0)
            at_spot(pairs * tiles + part)

    pl.run_scoped(
        projections, pltpu.VMEM((2, rows, quarter), BRAIN), pltpu.VMEM((2, 3, *w_q.shape[1:]), BRAIN)
    )
    for n in late:
        run_events(chains[n][0])
    for part in range(4):
        exchange(part).wait()
    four[...] = vectors[...]

    def norm(x_in, dx_in):
        size = x_in.shape[1]

        def load(i):
            slot = lax.rem(i, 2)
            here = pl.ds(pl.multiple_of(i * size, size), size)
            return (
                pltpu.make_async_copy(x0.at[here], x_in.at[slot], loads.at[slot, 0]),
                pltpu.make_async_copy(dx1.at[here], dx_in.at[slot], loads.at[slot, 1]),
            )

        for copy in load(0):
            copy.start()

        def step(i, carry):
            @pl.when(i + 1 < half // size)
            def _():
                for copy in load(i + 1):
                    copy.start()

            for copy in load(i):
                copy.wait()
            slot = lax.rem(i, 2)
            here = pl.ds(pl.multiple_of(i * size, size), size)
            flow = near[here, :].astype(FLOAT) + got[here, :].astype(FLOAT)
            values, gain_sum, bias_sum = norm_back(x_in[slot].astype(FLOAT), gains[0:1, :], flow)
            far[here, :] = (dx_in[slot] + values).astype(BRAIN)
            four[0:1, :] += gain_sum[None, :]
            four[1:2, :] += bias_sum[None, :]
            return carry

        lax.fori_loop(0, half // size, step, 0)

    pl.run_scoped(norm, pltpu.VMEM((2, 96, width), BRAIN), pltpu.VMEM((2, 96, width), FLOAT))
    frames_start()

    def hop(at, src, dst, partner):
        return pltpu.make_async_remote_copy(
            src_ref=src, dst_ref=dst, send_sem=v_send.at[at], recv_sem=v_recv.at[at],
            device_id=partner, device_id_type=MESH,
        )

    held = ring
    held[0] = four[...]
    for at, partner in enumerate(({"c": 1 - c}, {"y": 1 - y}, {"x": 1 - x})):
        turn = hop(at, held.at[2 * at], held.at[2 * at + 1], partner)
        turn.start()
        turn.wait()
        total = held[2 * at] + held[2 * at + 1]
        if at < 2:
            held[2 * at + 2] = total
        else:
            held[6 + z] = total
    z_up = hop(3, held.at[6 + z], held.at[6 + z], {"z": up})
    z_down = hop(4, held.at[6 + z], held.at[6 + z], {"z": down})
    z_more = hop(5, held.at[6 + down], held.at[6 + down], {"z": up})
    z_up.start()
    z_down.start()
    z_up.wait()
    z_more.start()
    rest = spots.get(len(times), []) + [(n, tick) for n in late for tick in range(1, TICKS + 1)]
    for number, tick in sorted(rest, key=lambda event: (event[1], event[0])):
        run_events(chains[number][tick])
    z_down.wait()
    z_more.wait()
    vectors_out[...] = (held[6] + held[7]) + (held[8] + held[9])
    frames_finish()


def sum_gradients(terms, attention, h, weights, x0, dx1, lse, gains, vectors, real, slots):
    count = len(terms)
    rows, share = attention[0].shape
    half, width = x0.shape
    size = terms[0].shape[3]
    crossings = 3 * len(slots) + 1
    dma = pltpu.SemaphoreType.DMA
    vmem = pl.BlockSpec(memory_space=pltpu.VMEM)
    landings = sum_landings(slots, size)
    widths = [t.shape[4] for t in terms] + [share] * 3
    most = [max(sizes[kind] for _, _, sizes in slots) for kind in range(2)]
    results = pl.pallas_call(
        functools.partial(sum_kernel, slots, count, real),
        in_specs=[ANY] * (count + 11) + [vmem] * 3,
        out_specs=[ANY] * (count + 4) + [vmem] + [ANY] * len(landings),
        out_shape=[jax.ShapeDtypeStruct((size, n), BRAIN) for n in widths]
        + [jax.ShapeDtypeStruct(x0.shape, BRAIN)]
        + [jax.ShapeDtypeStruct(vectors.shape, FLOAT)]
        + landings,
        scratch_shapes=[
            dma((len(slots), 3, 5)), dma((len(slots), 3, 5)), dma((len(slots), 3, 4)),
            dma((crossings,)), dma((crossings,)), dma((crossings,)), dma((6,)), dma((6,)),
            dma((4,)), dma((4,)), dma((2, 5)),
            pltpu.VMEM(vectors.shape, FLOAT), pltpu.VMEM((10, *vectors.shape), FLOAT),
            *[pltpu.VMEM((4, size, most[kind]), BRAIN) for kind in (0, 0, 1, 1)],
            pltpu.VMEM((3, rows, share), BRAIN), pltpu.VMEM((3, 4, 2, 2, size, share), BRAIN),
            pltpu.VMEM((half, width), BRAIN), pltpu.VMEM((half, width), BRAIN), pltpu.VMEM((half, width), BRAIN),
            *sum_scratch(slots, size),
        ],
        compiler_params=pltpu.CompilerParams(
            collective_id=3, has_side_effects=True, vmem_limit_bytes=58 * 2**20
        ),
        name="sum_gradients",
    )(*terms, *attention, h, *weights, x0, dx1, lse, gains, vectors)
    return results[: count + 5]


def slots_of(widths, six=((2, 3, 1), (2, 3, 1), (3, 2, 1)), eight=(3, 3, 2)):
    slots = []
    for which, width in enumerate(widths):
        tiles = width // LANES
        if tiles == 6:
            slots.append((which, 0, tuple(LANES * n for n in six[len(slots) % len(six)])))
        elif tiles % 8 == 0:
            for at in range(0, tiles, 8):
                slots.append((which, at * LANES, tuple(LANES * n for n in eight)))
        else:
            slots.append((which, 0, (width, 0, 0)))
    return tuple(slots)


def normalize(values, gain_vec, bias_vec):
    center = values - jnp.mean(values, -1, keepdims=True)
    spread = jnp.mean(center * center, -1, keepdims=True)
    return center * lax.rsqrt(spread + EPSILON) * gain_vec + bias_vec


def norm_back(values, gain_vec, grads):
    center = values - jnp.mean(values, -1, keepdims=True)
    scale_row = lax.rsqrt(jnp.mean(center * center, -1, keepdims=True) + EPSILON)
    normal = center * scale_row
    scaled = grads * gain_vec
    inner = jnp.mean(scaled * normal, -1, keepdims=True)
    grad_values = scale_row * (scaled - jnp.mean(scaled, -1, keepdims=True) - normal * inner)
    return grad_values, jnp.sum(grads * normal, 0), jnp.sum(grads, 0)


def gelu_pair(u):
    half_erf = 0.5 * (1.0 + lax.erf(u * (0.5**0.5)))
    density = jnp.exp(-0.5 * u * u) * ((2.0 * np.pi) ** -0.5)
    return (u * half_erf).astype(BRAIN), (half_erf + u * density).astype(BRAIN)


def split_heads(values):
    return values.reshape(values.shape[0], -1, HEAD_DIM)


def merge_heads(values):
    return values.reshape(values.shape[0], -1)


def attend_cross(q, k, v):
    scores = jnp.einsum("qhd,khd->hqk", q, k, preferred_element_type=FLOAT) * SCALE
    top = jnp.max(scores, -1, keepdims=True)
    e = jnp.exp(scores - top)
    total = jnp.sum(e, -1, keepdims=True)
    probs = e / total
    out = jnp.einsum("hqk,khd->qhd", probs.astype(BRAIN), v, preferred_element_type=FLOAT)
    return merge_heads(out).astype(BRAIN), (top + jnp.log(total))[..., 0]


def attend_cross_back(q, k, v, do, lse):
    scores = jnp.einsum("qhd,khd->hqk", q, k, preferred_element_type=FLOAT) * SCALE
    probs = jnp.exp(scores - lse[..., None])
    dp = jnp.einsum("qhd,khd->hqk", do, v, preferred_element_type=FLOAT)
    inner = jnp.sum(probs * dp, -1, keepdims=True)
    ds = (probs * (dp - inner)).astype(BRAIN)
    dq = jnp.einsum("hqk,khd->qhd", ds, k, preferred_element_type=FLOAT) * SCALE
    dk = jnp.einsum("hqk,qhd->khd", ds, q, preferred_element_type=FLOAT) * SCALE
    dv = jnp.einsum("hqk,qhd->khd", probs.astype(BRAIN), do, preferred_element_type=FLOAT)
    return tuple(merge_heads(t).astype(BRAIN) for t in (dq, dk, dv))


def on_device(
    inputs, text_states, teacher, valid_frames,
    self_norm_gain, self_norm_bias, self_query, self_key, self_value, self_out,
    cross_norm_gain, cross_norm_bias, cross_query, cross_key, cross_value, cross_out,
    feed_norm_gain, feed_norm_bias, feed_in, feed_out,
):
    at_core, at_y = lax.axis_index("c"), lax.axis_index("y")
    real, width = inputs.shape[1], inputs.shape[2]
    half = -(-real // ROWS) * ROWS
    block, share = self_query.shape
    hidden = feed_in.shape[1]

    fits = ring_fit()

    tiny = [self_norm_gain, self_norm_bias, cross_norm_gain, cross_norm_bias, feed_norm_gain, feed_norm_bias]
    count = jnp.sum(valid_frames)
    digits = jnp.stack([count // 64, count % 64]).astype(BRAIN)
    digits = jnp.where((jnp.arange(block) == 0)[:, None], digits[None, :], jnp.zeros((), BRAIN))
    tiny = jnp.pad(jnp.concatenate([jnp.stack(tiny, 1), digits], 1), ((0, 0), (0, LANES - 8)))
    weights = [
        tiny, self_query, self_key, self_value, self_out.T, cross_query, cross_key, cross_value, cross_out.T
    ]
    wide = [swap_weight(v) for v in (feed_in, feed_out.T)]

    def both(own):
        return jnp.concatenate([own, swap_core(own)], 0)

    def summed(left, weight):
        far = dot_nt(left[half:], weight).astype(BRAIN)
        got = swap_core(far)
        return dot_nt(left[:half], weight) + got.astype(FLOAT)

    def padded(v):
        return jnp.pad(v, ((0, half - real), (0, 0)))

    frames = padded(inputs[0])
    flags = jnp.pad(valid_frames[0][:, None].astype(BRAIN), ((0, 0), (0, LANES - 1)))
    target = padded(jnp.concatenate([teacher[0], flags], 1))
    if fits:
        slots = slots_of([v.shape[1] for v in weights], six=((2, 3, 1), (1, 3, 2)))
        frames, *wide = lax.optimization_barrier((frames, *wide))
        *weights, x_own, text, gains, h1, q1, k1, v1, o1, lse1 = gather(
            weights, frames, text_states[0], real, slots
        )
        weights = [joined(v) for v in weights]
    else:
        weights = [lax.all_gather(swap_clip(v), CHIPS, axis=0, tiled=True) for v in weights]
        x_own, text = (swap_clip(v) for v in (frames, text_states[0]))
        gains = weights[0].T.astype(FLOAT)
        x_all = jnp.concatenate([x_own, swap_core(x_own)], 0)
        h1 = normalize(x_all.astype(FLOAT), gains[0], gains[1]).astype(BRAIN)
        q1, k1, v1 = (dot_nn(h1, w).astype(BRAIN) for w in weights[1:4])
        o1, lse1 = attend_self(q1, k1, v1, real)
    tiny, w_q, w_k, w_v, w_so, w_cq, w_ck, w_cv, w_co = weights
    w_fi, w_fo = (lax.all_gather(v, CHIPS, axis=0, tiled=True) for v in wide)
    counted = jnp.sum(tiny[:, 6:8].astype(FLOAT), 0)
    counted = counted[0] * 64.0 + counted[1]
    token_count = counted + swap_core(counted)
    target, x_own = lax.optimization_barrier((target, x_own))
    target = swap_weight(target)
    valid = target[:, width : width + 1].astype(FLOAT)
    target = target[:, :width].astype(FLOAT)
    x0 = x_own.astype(FLOAT)
    x1 = x0 + summed(o1, w_so)
    h2 = both(normalize(x1, gains[2], gains[3]).astype(BRAIN))
    q2 = dot_nn(h2, w_cq).astype(BRAIN)
    k2 = dot_nn(text, w_ck).astype(BRAIN)
    v2 = dot_nn(text, w_cv).astype(BRAIN)
    o2, lse2 = attend_cross(split_heads(q2), split_heads(k2), split_heads(v2))
    x2 = x1 + summed(o2, w_co)
    h3 = both(normalize(x2, gains[4], gains[5]).astype(BRAIN))
    g, slope = gelu_pair(dot_nn(h3, w_fi))
    y = x2 + summed(g, w_fo)
    home = swap_weight(y.astype(BRAIN))
    deviation = y - target
    error = jnp.sum(valid * deviation * deviation)
    tokens_all = real * lax.axis_size(("z", "x", "c", "y"))
    dy = (2.0 * tokens_all / token_count) * valid * deviation

    dyb = both(dy.astype(BRAIN))
    fo_grad = dot_tn(dyb, g).astype(BRAIN)
    dyb, fo_grad = lax.optimization_barrier((dyb, fo_grad))
    fo_grad = lax.psum_scatter(fo_grad, CHIPS, scatter_dimension=0, tiled=True)
    du = (slope.astype(FLOAT) * dot_nn(dyb, w_fo)).astype(BRAIN)
    fi_grad = dot_tn(h3, du).astype(BRAIN)
    fi_grad = lax.psum_scatter(fi_grad, CHIPS, scatter_dimension=0, tiled=True)
    term, gain3, bias3 = norm_back(x2, gains[4], summed(du, w_fi))
    dx2 = dy + term
    dx2b = both(dx2.astype(BRAIN))
    co_grad = dot_tn(dx2b, o2).astype(BRAIN)
    do2 = dot_nn(dx2b, w_co).astype(BRAIN)
    dq2, dk2, dv2 = attend_cross_back(
        split_heads(q2), split_heads(k2), split_heads(v2), split_heads(do2), lse2
    )
    cq_grad = dot_tn(h2, dq2).astype(BRAIN)
    ck_grad = dot_tn(text, dk2).astype(BRAIN)
    cv_grad = dot_tn(text, dv2).astype(BRAIN)
    text_part = (dot_nt(dk2, w_ck) + dot_nt(dv2, w_cv)).astype(BRAIN)
    text_mine = jnp.where(at_core == 0, text_part[:, : width // 2], text_part[:, width // 2 :])
    text_far = jnp.where(at_core == 0, text_part[:, width // 2 :], text_part[:, : width // 2])
    text_sum = text_mine.astype(FLOAT) + swap_core(text_far).astype(FLOAT)
    text_grad = swap_clip(text_sum.astype(BRAIN)).astype(FLOAT)[None]
    term, gain2, bias2 = norm_back(x1, gains[2], summed(dq2, w_cq))
    dx1 = dx2 + term
    dx1b = both(dx1.astype(BRAIN))
    so_grad = dot_tn(dx1b, o1).astype(BRAIN)
    do1 = dot_nn(dx1b, w_so).astype(BRAIN)
    zero = jnp.zeros((width,), FLOAT)
    vectors = jnp.stack([zero, zero, gain2, bias2, gain3, bias3])
    vectors = jnp.concatenate([vectors, jnp.full((2, width), error)], 0)
    grads = [co_grad, cq_grad, ck_grad, cv_grad, so_grad]
    if fits:
        slots = slots_of([v.shape[1] for v in grads] + [share] * 3, six=((2, 2, 2),))
        *grads, frames, vectors = sum_gradients(
            [by_chip(v) for v in grads], (q1, k1, v1, do1, o1), h1,
            [by_chip(v) for v in (w_q, w_k, w_v)], x_own, dx1, lse1, gains, vectors, real, slots,
        )
    else:
        dq1, dk1, dv1 = attend_self_back(q1, k1, v1, do1, o1, lse1, real)
        dh1 = dot_nt(dq1, w_q) + dot_nt(dk1, w_k) + dot_nt(dv1, w_v)
        dh1 = dh1[:half] + swap_core(dh1[half:].astype(BRAIN)).astype(FLOAT)
        term, gain1, bias1 = norm_back(x0, gains[0], dh1)
        frames = swap_clip((dx1 + term).astype(BRAIN))
        grads += [dot_tn(h1, d).astype(BRAIN) for d in (dq1, dk1, dv1)]
        grads = [swap_clip(lax.psum_scatter(v, CHIPS, scatter_dimension=0, tiled=True)) for v in grads]
        vectors = lax.psum(vectors.at[:2].set(jnp.stack([gain1, bias1])), ("z", "x", "c", "y"))
    layer_out = home[:real][None]
    inputs_grad = frames[None].astype(FLOAT)[:, :real]
    co_grad, cq_grad, ck_grad, cv_grad, so_grad, q_grad, k_grad, v_grad = (v.astype(FLOAT) for v in grads)
    fi_grad, fo_grad = swap_weight(fi_grad).astype(FLOAT), swap_weight(fo_grad).astype(FLOAT).T
    loss = vectors[6, 0] / (width * token_count)
    mine = block // 2
    place = (lax.axis_index(("z", "x", "c")) * 2 + at_y) * mine
    norms = lax.dynamic_slice(vectors, (0, place), (8, mine))
    return (
        loss, layer_out, inputs_grad, text_grad,
        norms[0], norms[1], q_grad, k_grad, v_grad, so_grad.T,
        norms[2], norms[3], cq_grad, ck_grad, cv_grad, co_grad.T,
        norms[4], norms[5], fi_grad, fo_grad,
    )


def solution(mesh):
    outer = mesh.shape["dp"] // 4
    fine = Mesh(np.array(mesh.devices).reshape(outer, 2, 2, 2), ("z", "x", "c", "y"))
    dp = ("z", "x", "c")
    frames = P(dp, "y", None)
    vector, wide, tall = P(dp), P(dp, "y"), P("y", dp)
    small = P(("z", "x", "c", "y"))
    attention = (vector, vector, wide, wide, wide, tall)
    return jax.shard_map(
        on_device,
        mesh=fine,
        in_specs=(frames, P(dp, None, None), frames, P(dp, "y"), *attention, *attention, vector, vector, wide, tall),
        out_specs=(
            P(), frames, frames, P(dp, None, "y"),
            small, small, wide, wide, wide, tall,
            small, small, wide, wide, wide, tall,
            small, small, wide, tall,
        ),
        check_vma=False,
    )
```

```python
import functools

import jax
import jax.numpy as jnp
import numpy as np
from jax import lax
from jax.experimental import pallas as pl
from jax.experimental.pallas import tpu as pltpu
from jax.sharding import Mesh
from jax.sharding import PartitionSpec as P

HEAD_DIM = 64
LANES = 128
ROWS = 256
FLOAT = jnp.float32
BRAIN = jnp.bfloat16
NEGATIVE = -1e30
EPSILON = 1e-05
SCALE = HEAD_DIM ** (-0.5)
CHIPS = ("z", "x", "y")
MESH = pl.DeviceIdType.MESH


def swap_core(v):
    return lax.ppermute(v, "c", [(0, 1), (1, 0)])


def swap_clip(v):
    return lax.ppermute(v, ("c", "y"), [(0, 0), (1, 2), (2, 1), (3, 3)])


def swap_others(v):
    return lax.ppermute(v, ("c", "y"), [(1, 2), (2, 1)])


def swap_weight(v):
    return jnp.where(lax.axis_index("c") == lax.axis_index("y"), v, swap_others(v))


def ring_fit():
    return lax.axis_size("z") == 4 and lax.axis_size("x") == 2 and lax.axis_size("y") == 2


def by_chip(v):
    return v.reshape(4, 2, 2, v.shape[0] // 16, v.shape[1])


def joined(v):
    return v.reshape(-1, v.shape[-1])


def dot_nt(a, b, **kw):
    return lax.dot_general(a, b, (((1,), (1,)), ((), ())), preferred_element_type=FLOAT, **kw)


def dot_nn(a, b):
    return lax.dot_general(a, b, (((1,), (0,)), ((), ())), preferred_element_type=FLOAT)


def dot_tn(a, b):
    return lax.dot_general(a, b, (((0,), (0,)), ((), ())), preferred_element_type=FLOAT)


def attend_kernel(half, real, q_ref, k_ref, v_ref, o_ref, lse_ref):
    core = lax.axis_index("c")
    per_half = half // ROWS
    blocks = 2 * per_half
    lane = lax.broadcasted_iota(jnp.int32, (ROWS, LANES), 1)
    first = lane < HEAD_DIM
    rows_at = lax.broadcasted_iota(jnp.int32, (ROWS, ROWS), 0)
    cols_at = lax.broadcasted_iota(jnp.int32, (ROWS, ROWS), 1)

    def place(i):
        start = jnp.where(core == i // per_half, 0, half) + (i % per_half) * ROWS
        return pl.ds(pl.multiple_of(start, ROWS), ROWS)

    for i in range(blocks):
        queries = q_ref[place(i), :].astype(FLOAT) * SCALE
        outs = []
        logs = []
        for head in range(2):
            mine = first if head == 0 else jnp.logical_not(first)
            masked = jnp.where(mine, queries, 0.0).astype(BRAIN)
            scores = []
            for j in range(i + 1):
                s = dot_nt(masked, k_ref[place(j), :])
                if j == i:
                    s = jnp.where(cols_at <= rows_at, s, NEGATIVE)
                elif j == per_half - 1:
                    s = jnp.where(cols_at < real - (per_half - 1) * ROWS, s, NEGATIVE)
                scores.append(s)
            top = scores[0]
            for s in scores[1:]:
                top = jnp.maximum(top, s)
            top = jnp.max(top, 1, keepdims=True)
            total = None
            out = None
            for j in range(i + 1):
                e = jnp.exp(scores[j] - top)
                total = e if total is None else total + e
                term = dot_nn(e.astype(BRAIN), v_ref[place(j), :])
                out = term if out is None else out + term
            total = jnp.sum(total, 1, keepdims=True)
            outs.append(out / total)
            logs.append(top + jnp.log(total))
        o_ref[place(i), :] = jnp.where(first, outs[0], outs[1]).astype(BRAIN)
        both = jnp.where(lane == 0, logs[0], logs[1])
        lse_ref[0, :, i * ROWS : (i + 1) * ROWS] = both.T[:8, :]


def attend_self(q, k, v, real):
    rows, width = q.shape
    pairs = width // LANES
    spec = pl.BlockSpec((rows, LANES), lambda p: (0, p))
    return pl.pallas_call(
        functools.partial(attend_kernel, rows // 2, real),
        grid=(pairs,),
        in_specs=[spec, spec, spec],
        out_specs=[spec, pl.BlockSpec((1, 8, rows), lambda p: (p, 0, 0))],
        out_shape=[
            jax.ShapeDtypeStruct((rows, width), BRAIN),
            jax.ShapeDtypeStruct((pairs, 8, rows), FLOAT),
        ],
        compiler_params=pltpu.CompilerParams(vmem_limit_bytes=48 * 2**20),
        cost_estimate=pl.CostEstimate(
            flops=10 * rows * rows * width, bytes_accessed=8 * rows * width, transcendentals=0
        ),
        name="attend",
    )(q, k, v)


def attend_back_kernel(
    half, real, q_ref, k_ref, v_ref, do_ref, o_ref, lse_ref, dq_ref, dk_ref, dv_ref,
    dq_sum, inner, q_two, do_two, hook=None,
):
    core = lax.axis_index("c")
    per_half = half // ROWS
    blocks = 2 * per_half
    first = lax.broadcasted_iota(jnp.int32, (ROWS, LANES), 1) < HEAD_DIM
    key_at = lax.broadcasted_iota(jnp.int32, (ROWS, 2 * ROWS), 0)
    query_at = lax.broadcasted_iota(jnp.int32, (ROWS, 2 * ROWS), 1) % ROWS
    pick = lax.broadcasted_iota(jnp.int32, (8, LANES), 1) // HEAD_DIM
    pick = (pick == lax.broadcasted_iota(jnp.int32, (8, LANES), 0)).astype(FLOAT)

    def place(i):
        start = jnp.where(core == i // per_half, 0, half) + (i % per_half) * ROWS
        return pl.ds(pl.multiple_of(start, ROWS), ROWS)

    def side_by_side(ref, i):
        return jnp.concatenate([ref[0:1, i * ROWS : (i + 1) * ROWS], ref[1:2, i * ROWS : (i + 1) * ROWS]], 1)

    for i in range(blocks):
        grads = do_ref[place(i), :].astype(FLOAT)
        queries = q_ref[place(i), :].astype(FLOAT) * SCALE
        product = grads * o_ref[place(i), :].astype(FLOAT)
        inner[:, i * ROWS : (i + 1) * ROWS] = dot_nt(pick, product, precision=lax.Precision.HIGHEST)
        q_two[i, :ROWS] = jnp.where(first, queries, 0.0).astype(BRAIN)
        q_two[i, ROWS:] = jnp.where(first, 0.0, queries).astype(BRAIN)
        do_two[i, :ROWS] = jnp.where(first, grads, 0.0).astype(BRAIN)
        do_two[i, ROWS:] = jnp.where(first, 0.0, grads).astype(BRAIN)
    dq_sum[...] = jnp.zeros_like(dq_sum)

    for j in range(blocks):
        if hook is not None:
            hook(j)
        keys = k_ref[place(j), :]
        values = v_ref[place(j), :]
        dk = dv = None
        for i in range(j, blocks):
            rows = pl.ds(i * ROWS, ROWS)
            q_m, do_m = q_two[i], do_two[i]
            s = dot_nt(keys, q_m) - side_by_side(lse_ref.at[0], i)
            if i == j:
                s = jnp.where(key_at <= query_at, s, NEGATIVE)
            elif j == per_half - 1:
                s = jnp.where(key_at < real - j * ROWS, s, NEGATIVE)
            p = jnp.exp(s)
            dp = dot_nt(values, do_m)
            ds = (p * (dp - side_by_side(inner, i))).astype(BRAIN)
            dv_term = dot_nn(p.astype(BRAIN), do_m)
            dk_term = dot_nn(ds, q_m)
            dk = dk_term if dk is None else dk + dk_term
            dv = dv_term if dv is None else dv + dv_term
            dq = dot_tn(ds, keys)
            dq_sum[rows, :] += jnp.where(first, dq[:ROWS], dq[ROWS:])
        dk_ref[place(j), :] = dk.astype(BRAIN)
        dv_ref[place(j), :] = dv.astype(BRAIN)

    for i in range(blocks):
        dq_ref[place(i), :] = (dq_sum[i * ROWS : (i + 1) * ROWS, :] * SCALE).astype(BRAIN)


def attend_self_back(q, k, v, do, o, lse, real):
    rows, width = q.shape
    pairs = width // LANES
    spec = pl.BlockSpec((rows, LANES), lambda p: (0, p))
    return pl.pallas_call(
        functools.partial(attend_back_kernel, rows // 2, real),
        grid=(pairs,),
        in_specs=[spec] * 5 + [pl.BlockSpec((1, 8, rows), lambda p: (p, 0, 0))],
        out_specs=[spec] * 3,
        scratch_shapes=[
            pltpu.VMEM((rows, LANES), FLOAT),
            pltpu.VMEM((8, rows), FLOAT),
            pltpu.VMEM((rows // ROWS, 2 * ROWS, LANES), BRAIN),
            pltpu.VMEM((rows // ROWS, 2 * ROWS, LANES), BRAIN),
        ],
        out_shape=[jax.ShapeDtypeStruct((rows, width), BRAIN)] * 3,
        compiler_params=pltpu.CompilerParams(vmem_limit_bytes=48 * 2**20),
        cost_estimate=pl.CostEstimate(
            flops=25 * rows * rows * width, bytes_accessed=16 * rows * width, transcendentals=0
        ),
        name="attend_back",
    )(q, k, v, do, o, lse)


ORDERS = ("zxy", "zyx", "xyz")
TICKS = 5
SUM_TIME = 2.2


def whereabouts():
    z, x, c, y = (lax.axis_index(name) for name in ("z", "x", "c", "y"))
    return z, x, c, y, lax.rem(z + 1, 4), lax.rem(z + 3, 4), lax.rem(z + 2, 4)


def greet(c, y, up, down, x, cores):
    barrier = pltpu.get_barrier_semaphore()
    partners = [{"z": up}, {"z": down}, {"x": 1 - x}, {"y": 1 - y}]
    if cores:
        partners.append({"c": 1 - c})
    for partner in partners:
        pl.semaphore_signal(barrier, inc=1, device_id=partner, device_id_type=MESH)

    @pl.when(c != y)
    def _():
        pl.semaphore_signal(barrier, inc=1, device_id={"c": y, "y": c}, device_id_type=MESH)
        pl.semaphore_wait(barrier, len(partners) + 1)

    @pl.when(c == y)
    def _():
        pl.semaphore_wait(barrier, len(partners))


def one(i):
    return pl.ds(i, 1)


class Crossing:
    def __init__(self, c, y, send, recv, local):
        self.c, self.y, self.send, self.recv, self.local = c, y, send, recv, local
        self.used = 0

    def begin(self, src, dst):
        start, finish = self.prepare(src, dst)
        start()
        return finish

    def prepare(self, src, dst):
        at = self.used
        self.used += 1
        far = pltpu.make_async_remote_copy(
            src_ref=src, dst_ref=dst, send_sem=self.send.at[at], recv_sem=self.recv.at[at],
            device_id={"c": self.y, "y": self.c}, device_id_type=MESH,
        )
        near = pltpu.make_async_copy(src, dst, self.local.at[at])

        def start():
            @pl.when(self.c != self.y)
            def _():
                far.start()

            @pl.when(self.c == self.y)
            def _():
                near.start()

        def finish():
            @pl.when(self.c != self.y)
            def _():
                far.wait()

            @pl.when(self.c == self.y)
            def _():
                near.wait()

        return start, finish


def gather_events(where, slots, weights, send, recv):
    z, x, c, y, up, down, across = where
    every = slice(None)
    chains = []
    for number, (which, start, sizes) in enumerate(slots):
        ref = weights[which]
        ticks = [[] for _ in range(TICKS)]
        for kind, order in enumerate(ORDERS):
            size = sizes[kind]
            if size == 0:
                continue
            columns = pl.ds(start, size)
            start += size

            def copy(at, region, partner, ref=ref, columns=columns, kind=kind, number=number):
                view = ref.at[(*region, every, columns)]
                return pltpu.make_async_remote_copy(
                    src_ref=view, dst_ref=view, send_sem=send.at[number, kind, at],
                    recv_sem=recv.at[number, kind, at], device_id=partner, device_id_type=MESH,
                )

            if order == "xyz":
                by_x = copy(0, (one(z), one(x), one(y)), {"x": 1 - x})
                by_y = copy(1, (one(z), every, one(y)), {"y": 1 - y})
                rest = (every, every)
            else:
                rest = (one(x), one(y))
            z_up = copy(2, (one(z), *rest), {"z": up})
            z_down = copy(3, (one(z), *rest), {"z": down})
            z_more = copy(4, (one(down), *rest), {"z": up})
            if order == "xyz":
                ticks[0] += [by_x.start]
                ticks[1] += [by_x.wait, by_y.start]
                ticks[2] += [by_y.wait, z_up.start, z_down.start]
                ticks[3] += [z_up.wait, z_more.start]
                ticks[4] += [z_down.wait, z_more.wait]
            else:
                if order == "zxy":
                    near = copy(0, (every, one(x), one(y)), {"x": 1 - x})
                    far = copy(1, (every, every, one(y)), {"y": 1 - y})
                else:
                    near = copy(0, (every, one(x), one(y)), {"y": 1 - y})
                    far = copy(1, (every, one(x), every), {"x": 1 - x})
                ticks[0] += [z_up.start, z_down.start]
                ticks[1] += [z_up.wait, z_more.start]
                ticks[2] += [z_down.wait, z_more.wait, near.start]
                ticks[3] += [near.wait, far.start]
                ticks[4] += [far.wait]
        chains.append(ticks)
    return chains


def run_tick(chains, at):
    for number, ticks in enumerate(chains):
        if 0 <= at - number < TICKS:
            for event in ticks[at - number]:
                event()


def total_ticks(slots):
    return len(slots) + TICKS - 1


def bring_own(crossing, where, slots, chains, blocks, weights):
    z, x, c = where[:3]
    for which, (block, weight) in enumerate(zip(blocks, weights)):
        start, finish = crossing.prepare(block, weight.at[z, x, c])
        number = [slot[0] for slot in slots].index(which)
        chains[number][0].insert(0, finish)
        yield start


ANY = pl.BlockSpec(memory_space=pl.ANY)
NEEDED_FIRST = 4


def gather_kernel(slots, count, real, *refs):
    blocks, (frames, text, target) = refs[:count], refs[count : count + 3]
    refs = refs[count + 3 :]
    weights, (own_out, text_out, target_out) = refs[:count], refs[count : count + 3]
    gains_ref, h_ref, q_ref, k_ref, v_ref, o_ref, lse_ref = refs[count + 3 : count + 10]
    send, recv, cross_send, cross_recv, cross_local, core_send, core_recv, loads, tiny, both, held = refs[count + 10 :]
    rows, width = h_ref.shape
    half = rows // 2
    pairs = q_ref.shape[1] // LANES
    where = whereabouts()
    z, x, c, y, up, down, across = where
    crossing = Crossing(c, y, cross_send, cross_recv, cross_local)
    chains = gather_events(where, slots, weights, send, recv)
    starts = list(bring_own(crossing, where, slots, chains, blocks, weights))
    frames_start, frames_finish = crossing.prepare(frames, both.at[0])
    moves = [crossing.prepare(*pair) for pair in ((text, text_out), (target, target_out))]
    sibling = pltpu.make_async_remote_copy(
        src_ref=both.at[0], dst_ref=both.at[1], send_sem=core_send, recv_sem=core_recv,
        device_id={"c": 1 - c}, device_id_type=MESH,
    )
    keep = pltpu.make_async_copy(both.at[0], own_out, loads.at[4])
    fetch = [pltpu.make_async_copy(weights[0], tiny, loads.at[0])]
    fetch += [pltpu.make_async_copy(weights[i + 1], held.at[i], loads.at[i + 1]) for i in range(3)]

    def tick(at):
        for number in reversed(range(len(slots))):
            stage = at - number
            last = TICKS if number < NEEDED_FIRST else TICKS - 1
            if 0 <= stage < last:
                run_events(chains[number][stage])

    greet(c, y, up, down, x, True)
    for start in starts[:NEEDED_FIRST]:
        start()
    frames_start()
    for start in starts[NEEDED_FIRST:]:
        start()
    for start, _ in moves:
        start()
    ready = NEEDED_FIRST + TICKS - 1
    for at in range(ready):
        tick(at)
        if at == 3:
            frames_finish()
            sibling.start()
            keep.start()
        if at == ready - 4:
            fetch[0].start()
    for copy in fetch[1:]:
        copy.start()
    sibling.wait()
    fetch[0].wait()
    gains_ref[...] = tiny[...].reshape(width, LANES).astype(FLOAT).T[:8, :]

    def norm_step(i, carry):
        here = pl.ds(pl.multiple_of(i * LANES, LANES), LANES)
        for side in range(2):
            there = pl.ds(pl.multiple_of(side * half + i * LANES, LANES), LANES)
            h_ref[there, :] = normalize(both[side, here, :].astype(FLOAT), gains_ref[0:1, :], gains_ref[1:2, :]).astype(BRAIN)
        return carry

    lax.fori_loop(0, half // LANES, norm_step, 0)
    later = list(range(ready, len(slots) + TICKS - 2))
    tick(later.pop(0))
    for i, out in enumerate((q_ref, k_ref, v_ref)):
        fetch[i + 1].wait()

        def project_step(r, carry, i=i, out=out):
            here = pl.ds(pl.multiple_of(r * ROWS, ROWS), ROWS)
            out[here, :] = dot_nn(h_ref[here, :], held[i].reshape(width, -1)).astype(BRAIN)
            return carry

        lax.fori_loop(0, rows // ROWS, project_step, 0)
        if later:
            tick(later.pop(0))

    def pair_step(p, carry):
        for turn in range(pairs):
            if turn < len(later):
                @pl.when(p == turn)
                def _(turn=turn):
                    tick(later[turn])

        lanes = pl.ds(pl.multiple_of(p * LANES, LANES), LANES)
        every = slice(None)
        q, k, v, o = (ref.at[every, lanes] for ref in (q_ref, k_ref, v_ref, o_ref))
        attend_kernel(half, real, q, k, v, o, lse_ref.at[pl.ds(p, 1)])
        return carry

    lax.fori_loop(0, pairs, pair_step, 0)
    for at in later[pairs:]:
        tick(at)
    for ticks in chains[NEEDED_FIRST:]:
        run_events(ticks[TICKS - 1])
    keep.wait()
    for _, finish in moves:
        finish()


def gather(blocks, frames, text, target, real, slots):
    count = len(blocks)
    rows, width = 2 * frames.shape[0], frames.shape[1]
    share = blocks[1].shape[1]
    pairs = share // LANES
    crossings = count + 3
    dma = pltpu.SemaphoreType.DMA
    vmem = pl.BlockSpec(memory_space=pltpu.VMEM)
    heads = jax.ShapeDtypeStruct((rows, share), BRAIN)
    gathered = [jax.ShapeDtypeStruct((4, 2, 2, *b.shape), BRAIN) for b in blocks]
    return pl.pallas_call(
        functools.partial(gather_kernel, slots, count, real),
        out_shape=[
            *gathered,
            *[jax.ShapeDtypeStruct(v.shape, v.dtype) for v in (frames, text, target)],
            jax.ShapeDtypeStruct((8, width), FLOAT), jax.ShapeDtypeStruct((rows, width), BRAIN),
            heads, heads, heads, heads, jax.ShapeDtypeStruct((pairs, 8, rows), FLOAT),
        ],
        in_specs=[ANY] * (count + 3),
        out_specs=[ANY] * (count + 3) + [vmem] * 7,
        scratch_shapes=[
            dma((len(slots), 3, 5)), dma((len(slots), 3, 5)),
            dma((crossings,)), dma((crossings,)), dma((crossings,)), dma, dma, dma((5,)),
            pltpu.VMEM(gathered[0].shape, BRAIN), pltpu.VMEM((2, *frames.shape), BRAIN),
            pltpu.VMEM((3, *gathered[1].shape), BRAIN),
        ],
        compiler_params=pltpu.CompilerParams(
            collective_id=1, has_side_effects=True, vmem_limit_bytes=56 * 2**20
        ),
        name="gather",
    )(*blocks, frames, text, target)


def plus(*terms):
    total = terms[0].astype(FLOAT)
    for term in terms[1:]:
        total = total + term.astype(FLOAT)
    return total.astype(BRAIN)


def sum_scratch(slots, rows):
    shapes = []
    for _, _, sizes in slots:
        for kind, order in enumerate(ORDERS):
            size = sizes[kind]
            if size == 0:
                continue
            if order == "xyz":
                leads = [(2, 2, 2), (2, 2), (2, 2), (2, 2), (2,), ()]
            else:
                leads = [(4,), (4,), (), (), (), ()]
            shapes += [pltpu.VMEM((*lead, rows, size), BRAIN) for lead in leads]
    return shapes


def sum_landings(slots, rows):
    return [
        jax.ShapeDtypeStruct((4, 2, rows, sizes[kind]), BRAIN)
        for _, _, sizes in slots
        for kind, order in enumerate(ORDERS)
        if sizes[kind] and order != "xyz"
    ]


def sum_events(where, slots, terms, outs, landings, buffers, pads, crossing, send, recv, local):
    z, x, c, y, up, down, across = where
    every = slice(None)
    chains = []
    taken = landed = 0
    for number, (which, start, sizes) in enumerate(slots):
        ref, out = terms[which], outs[which]
        ticks = [[] for _ in range(TICKS + 1)]
        after, later = [], []
        for kind, order in enumerate(ORDERS):
            size = sizes[kind]
            if size == 0:
                continue
            columns = pl.ds(start, size)
            start += size
            need = 6
            held = buffers[taken : taken + need]
            taken += need

            def copy(at, src, dst, partner, kind=kind, number=number):
                return pltpu.make_async_remote_copy(
                    src_ref=src, dst_ref=dst, send_sem=send.at[number, kind, at],
                    recv_sem=recv.at[number, kind, at], device_id=partner, device_id_type=MESH,
                )

            def view(*region, ref=ref, columns=columns):
                return ref.at[(*region, every, columns)]

            if order == "xyz":
                own, from_two, from_down, from_up, from_y, from_x = held
                load_a = pltpu.make_async_copy(view(z, every, every), own.at[0], local.at[number, kind, 0])
                load_b = pltpu.make_async_copy(view(down, every, every), own.at[1], local.at[number, kind, 1])
                s_three = copy(0, view(up, every, every), from_down, {"z": up})
                s_two = copy(1, view(across, every, every), from_two, {"z": down})
                s_one = copy(2, own.at[1], from_up, {"z": down})
                s_y = copy(3, own.at[0, every, 1 - y], from_y, {"y": 1 - y})
                s_x = copy(4, from_y.at[1 - x], from_x, {"x": 1 - x})

                def add_two(own=own, from_two=from_two):
                    for i in range(2):
                        for j in range(2):
                            own[1, i, j] = plus(own[1, i, j], from_two[i, j])

                def add_z(own=own, a=from_down, b=from_up):
                    for i in range(2):
                        for j in range(2):
                            own[0, i, j] = plus(own[0, i, j], a[i, j], b[i, j])

                def add_y(own=own, from_y=from_y):
                    for i in range(2):
                        from_y[i] = plus(own[0, i, y], from_y[i])

                def add_x(from_y=from_y, from_x=from_x):
                    from_x[...] = plus(from_y[x], from_x[...])

                ticks[0] += [load_a.start, load_b.start, s_three.start, s_two.start]
                ticks[1] += [s_two.wait, load_b.wait, add_two, s_one.start]
                ticks[2] += [s_three.wait, load_a.wait, s_one.wait, add_z, s_y.start]
                ticks[3] += [s_y.wait, add_y, s_x.start]
                ticks[4] += [s_x.wait, add_x]
                final = from_x
            else:
                from_second, far, from_two, from_down, from_up, total = held
                landing = landings[landed]
                landed += 1
                mine_at, got_at = (pad.at[every, every, pl.ds(0, size)] for pad in pads[kind])
                mine_pad, got_pad = pads[kind]
                if order == "zxy":
                    mine, theirs = view(every, 1 - x, y), view(every, every, 1 - y)
                    first, second = {"y": 1 - y}, {"x": 1 - x}
                    side = x
                else:
                    mine, theirs = view(every, x, 1 - y), view(every, 1 - x, every)
                    first, second = {"x": 1 - x}, {"y": 1 - y}
                    side = y
                load_mine = pltpu.make_async_copy(mine, mine_at, local.at[number, kind, 0])
                load_got = pltpu.make_async_copy(landing.at[every, 1 - side], got_at, local.at[number, kind, 1])
                load_near = pltpu.make_async_copy(view(every, x, y), mine_at, local.at[number, kind, 2])
                load_rest = pltpu.make_async_copy(landing.at[every, side], got_at, local.at[number, kind, 3])
                s_first = copy(0, theirs, landing, first)
                s_second = copy(1, far, from_second, second)
                s_three = copy(2, from_second.at[up], from_down, {"z": up})
                s_two = copy(3, from_second.at[across], from_two, {"z": down})
                s_one = copy(4, from_second.at[down], from_up, {"z": down})

                def add_first(mine=mine_pad, got=got_pad, size=size, far=far):
                    for i in range(4):
                        far[i] = plus(mine[i, :, :size], got[i, :, :size])

                def add_second(mine=mine_pad, got=got_pad, size=size, more=from_second):
                    for i in range(4):
                        more[i] = plus(mine[i, :, :size], got[i, :, :size], more[i])

                def add_two(more=from_second, two=from_two):
                    more[down] = plus(more[down], two[...])

                def add_z(more=from_second, a=from_down, b=from_up, total=total):
                    total[...] = plus(more[z], a[...], b[...])

                ticks[0] += [s_first.start]
                ticks[1] += [s_first.wait, load_mine.start, load_got.start]
                after += [load_mine.wait, load_got.wait, add_first, s_second.start]
                ticks[2] += [s_second.wait, load_near.start, load_rest.start]
                later += [load_near.wait, load_rest.wait, add_second, s_three.start, s_two.start]
                ticks[3] += [s_two.wait, add_two, s_one.start]
                ticks[4] += [s_three.wait, s_one.wait, add_z]
                final = total

            leave, left = crossing.prepare(final, out.at[every, columns])
            ticks[4] += [leave]
            ticks[5] += [left]
        ticks[1] += after
        ticks[2] += later
        chains.append(ticks)
    return chains


def sum_order(count):
    shares = ((1, 0.5), (2, 0.27), (3, 0.08), (4, 0.1), (5, 0.05))
    order = []
    passed = 0.0
    for tick, part in shares:
        order += [(n, tick, passed + part * (n + 1) / count) for n in range(count)]
        passed += part
    return order


def run_events(events):
    for event in events:
        event()


def sum_kernel(slots, count, real, *refs):
    terms, refs = refs[:count], refs[count:]
    home, q, k, v, do, o, h, w_q, w_k, w_v, x0, dx1, lse, gains, vectors = refs[:15]
    refs = refs[15:]
    outs, (home_out, frames_out, vectors_out) = refs[: count + 3], refs[count + 3 : count + 6]
    refs = refs[count + 6 :]
    lands = len([1 for _, _, sizes in slots for kind, order in enumerate(ORDERS) if sizes[kind] and order != "xyz"])
    landings, refs = refs[:lands], refs[lands:]
    send, recv, local, cross_send, cross_recv, cross_local, v_send, v_recv, h_send, h_recv, loads = refs[:11]
    four, ring, pad_a, pad_b, pad_c, pad_d, grads, grad_terms, far, got, near = refs[11:22]
    half, width = x0.shape
    rows, share = q.shape
    pairs = share // LANES
    tiles = rows // ROWS
    quarter = width // 4
    where = whereabouts()
    z, x, c, y, up, down, across = where
    every = slice(None)
    crossing = Crossing(c, y, cross_send, cross_recv, cross_local)
    all_terms = [*terms, *(grad_terms.at[i] for i in range(3))]
    pads = ((pad_a, pad_b), (pad_c, pad_d))
    chains = sum_events(where, slots, all_terms, outs, landings, refs[22:], pads, crossing, send, recv, local)
    early = [n for n, slot in enumerate(slots) if slot[0] < count]
    late = [n for n, slot in enumerate(slots) if slot[0] >= count]
    home_start, home_finish = crossing.prepare(home, home_out)
    frames_start, frames_finish = crossing.prepare(far, frames_out)
    greet(c, y, up, down, x, True)
    for n in early:
        run_events(chains[n][0])
    home_start()

    work = tiles * (tiles + 1) // 2
    times = [p + sum(tiles - i for i in range(j)) / work for p in range(pairs) for j in range(tiles)]
    times += [pairs + 0.9 * i for i in range(1, 5)]
    spots = {}
    for number, tick, part in sum_order(len(early)):
        due = part * SUM_TIME * pairs
        later = [i for i, time in enumerate(times) if time >= due]
        spots.setdefault(later[0] if later else len(times), []).append((early[number], tick))

    def at_spot(spot):
        for number, tick in spots.get(spot, []):
            run_events(chains[number][tick])

    def attention(pair_in, *held):
        def load(p, i):
            lanes = pl.ds(pl.multiple_of(p * LANES, LANES), LANES)
            slot = lax.rem(p, 2)
            source = (q, k, v, do, o)[i]
            return pltpu.make_async_copy(source.at[every, lanes], pair_in.at[slot, i], loads.at[slot, i])

        for i in range(5):
            load(0, i).start()

        def pair_step(p, carry):
            @pl.when(p + 1 < pairs)
            def _():
                for i in range(5):
                    load(p + 1, i).start()

            for i in range(5):
                load(p, i).wait()

            def hook(j):
                for turn in range(pairs):
                    if turn * tiles + j in spots:
                        @pl.when(p == turn)
                        def _(turn=turn):
                            at_spot(turn * tiles + j)

            lanes = pl.ds(pl.multiple_of(p * LANES, LANES), LANES)
            slot = lax.rem(p, 2)
            attend_back_kernel(
                half, real, *(pair_in.at[slot, i] for i in range(5)), lse.at[pl.ds(p, 1)],
                *(grads.at[i, every, lanes] for i in range(3)), *held, hook=hook,
            )
            return carry

        lax.fori_loop(0, pairs, pair_step, 0)

    pl.run_scoped(
        attention,
        pltpu.VMEM((2, 5, rows, LANES), BRAIN), pltpu.VMEM((rows, LANES), FLOAT), pltpu.VMEM((8, rows), FLOAT),
        pltpu.VMEM((tiles, 2 * ROWS, LANES), BRAIN), pltpu.VMEM((tiles, 2 * ROWS, LANES), BRAIN),
    )

    def exchange(part):
        columns = pl.ds(part * quarter, quarter)
        return pltpu.make_async_remote_copy(
            src_ref=far.at[every, columns], dst_ref=got.at[every, columns], send_sem=h_send.at[part],
            recv_sem=h_recv.at[part], device_id={"c": 1 - c}, device_id_type=MESH,
        )

    def projections(h_in, w_in):
        def load(part, i):
            slot = part % 2
            if i == 3:
                return pltpu.make_async_copy(h.at[every, pl.ds(part * quarter, quarter)], h_in.at[slot], loads.at[slot, 3])
            return pltpu.make_async_copy((w_q, w_k, w_v)[i].at[part], w_in.at[slot, i], loads.at[slot, i])

        for i in range(4):
            load(0, i).start()
        for part in range(4):
            if part < 3:
                for i in range(4):
                    load(part + 1, i).start()
            for i in range(4):
                load(part, i).wait()
            slot = part % 2
            columns = pl.ds(part * quarter, quarter)

            def grad_step(i, carry, part=part, slot=slot):
                product = dot_tn(h_in[slot], grads[i]).astype(BRAIN)
                grad_terms[i, part] = product.reshape(grad_terms.shape[2:])
                return carry

            def back_step(r, carry, slot=slot, columns=columns, out=None, base=0):
                here = pl.ds(pl.multiple_of(r * ROWS, ROWS), ROWS)
                there = pl.ds(pl.multiple_of(base + r * ROWS, ROWS), ROWS)
                total = dot_nt(grads[0, there, :], w_in[slot, 0].reshape(quarter, share))
                for i in (1, 2):
                    total = total + dot_nt(grads[i, there, :], w_in[slot, i].reshape(quarter, share))
                out[here, columns] = total.astype(out.dtype)
                return carry

            lax.fori_loop(0, half // ROWS, functools.partial(back_step, out=far, base=half), 0)
            exchange(part).start()
            lax.fori_loop(0, half // ROWS, functools.partial(back_step, out=near), 0)
            lax.fori_loop(0, 3, grad_step, 0)
            at_spot(pairs * tiles + part)

    pl.run_scoped(
        projections, pltpu.VMEM((2, rows, quarter), BRAIN), pltpu.VMEM((2, 3, *w_q.shape[1:]), BRAIN)
    )
    for n in late:
        run_events(chains[n][0])
    for part in range(4):
        exchange(part).wait()
    four[...] = vectors[...]

    def norm(x_in, dx_in):
        size = x_in.shape[1]

        def load(i):
            slot = lax.rem(i, 2)
            here = pl.ds(pl.multiple_of(i * size, size), size)
            return (
                pltpu.make_async_copy(x0.at[here], x_in.at[slot], loads.at[slot, 0]),
                pltpu.make_async_copy(dx1.at[here], dx_in.at[slot], loads.at[slot, 1]),
            )

        for copy in load(0):
            copy.start()

        def step(i, carry):
            @pl.when(i + 1 < half // size)
            def _():
                for copy in load(i + 1):
                    copy.start()

            for copy in load(i):
                copy.wait()
            slot = lax.rem(i, 2)
            here = pl.ds(pl.multiple_of(i * size, size), size)
            flow = near[here, :].astype(FLOAT) + got[here, :].astype(FLOAT)
            values, gain_sum, bias_sum = norm_back(x_in[slot].astype(FLOAT), gains[0:1, :], flow)
            far[here, :] = (dx_in[slot] + values).astype(BRAIN)
            four[0:1, :] += gain_sum[None, :]
            four[1:2, :] += bias_sum[None, :]
            return carry

        lax.fori_loop(0, half // size, step, 0)

    pl.run_scoped(norm, pltpu.VMEM((2, 96, width), BRAIN), pltpu.VMEM((2, 96, width), FLOAT))
    frames_start()

    def hop(at, src, dst, partner):
        return pltpu.make_async_remote_copy(
            src_ref=src, dst_ref=dst, send_sem=v_send.at[at], recv_sem=v_recv.at[at],
            device_id=partner, device_id_type=MESH,
        )

    held = ring
    held[0] = four[...]
    for at, partner in enumerate(({"c": 1 - c}, {"y": 1 - y}, {"x": 1 - x})):
        turn = hop(at, held.at[2 * at], held.at[2 * at + 1], partner)
        turn.start()
        turn.wait()
        total = held[2 * at] + held[2 * at + 1]
        if at < 2:
            held[2 * at + 2] = total
        else:
            held[6 + z] = total
    z_up = hop(3, held.at[6 + z], held.at[6 + z], {"z": up})
    z_down = hop(4, held.at[6 + z], held.at[6 + z], {"z": down})
    z_more = hop(5, held.at[6 + down], held.at[6 + down], {"z": up})
    z_up.start()
    z_down.start()
    z_up.wait()
    z_more.start()
    rest = spots.get(len(times), []) + [(n, tick) for n in late for tick in range(1, TICKS + 1)]
    for number, tick in sorted(rest, key=lambda event: (event[1], event[0])):
        run_events(chains[number][tick])
    z_down.wait()
    z_more.wait()
    vectors_out[...] = (held[6] + held[7]) + (held[8] + held[9])
    home_finish()
    frames_finish()


def sum_gradients(terms, home, attention, h, weights, x0, dx1, lse, gains, vectors, real, slots):
    count = len(terms)
    rows, share = attention[0].shape
    half, width = x0.shape
    size = terms[0].shape[3]
    crossings = 3 * len(slots) + 2
    dma = pltpu.SemaphoreType.DMA
    vmem = pl.BlockSpec(memory_space=pltpu.VMEM)
    landings = sum_landings(slots, size)
    widths = [t.shape[4] for t in terms] + [share] * 3
    most = [max(sizes[kind] for _, _, sizes in slots) for kind in range(2)]
    results = pl.pallas_call(
        functools.partial(sum_kernel, slots, count, real),
        in_specs=[ANY] * (count + 12) + [vmem] * 3,
        out_specs=[ANY] * (count + 5) + [vmem] + [ANY] * len(landings),
        out_shape=[jax.ShapeDtypeStruct((size, n), BRAIN) for n in widths]
        + [jax.ShapeDtypeStruct(home.shape, BRAIN), jax.ShapeDtypeStruct(x0.shape, BRAIN)]
        + [jax.ShapeDtypeStruct(vectors.shape, FLOAT)]
        + landings,
        scratch_shapes=[
            dma((len(slots), 3, 5)), dma((len(slots), 3, 5)), dma((len(slots), 3, 4)),
            dma((crossings,)), dma((crossings,)), dma((crossings,)), dma((6,)), dma((6,)),
            dma((4,)), dma((4,)), dma((2, 5)),
            pltpu.VMEM(vectors.shape, FLOAT), pltpu.VMEM((10, *vectors.shape), FLOAT),
            *[pltpu.VMEM((4, size, most[kind]), BRAIN) for kind in (0, 0, 1, 1)],
            pltpu.VMEM((3, rows, share), BRAIN), pltpu.VMEM((3, 4, 2, 2, size, share), BRAIN),
            pltpu.VMEM((half, width), BRAIN), pltpu.VMEM((half, width), BRAIN), pltpu.VMEM((half, width), BRAIN),
            *sum_scratch(slots, size),
        ],
        compiler_params=pltpu.CompilerParams(
            collective_id=3, has_side_effects=True, vmem_limit_bytes=58 * 2**20
        ),
        name="sum_gradients",
    )(*terms, home, *attention, h, *weights, x0, dx1, lse, gains, vectors)
    return results[: count + 6]


def slots_of(widths, six=((2, 3, 1), (2, 3, 1), (3, 2, 1)), eight=(3, 3, 2)):
    slots = []
    for which, width in enumerate(widths):
        tiles = width // LANES
        if tiles == 6:
            slots.append((which, 0, tuple(LANES * n for n in six[len(slots) % len(six)])))
        elif tiles % 8 == 0:
            for at in range(0, tiles, 8):
                slots.append((which, at * LANES, tuple(LANES * n for n in eight)))
        else:
            slots.append((which, 0, (width, 0, 0)))
    return tuple(slots)


def normalize(values, gain_vec, bias_vec):
    center = values - jnp.mean(values, -1, keepdims=True)
    spread = jnp.mean(center * center, -1, keepdims=True)
    return center * lax.rsqrt(spread + EPSILON) * gain_vec + bias_vec


def norm_back(values, gain_vec, grads):
    center = values - jnp.mean(values, -1, keepdims=True)
    scale_row = lax.rsqrt(jnp.mean(center * center, -1, keepdims=True) + EPSILON)
    normal = center * scale_row
    scaled = grads * gain_vec
    inner = jnp.mean(scaled * normal, -1, keepdims=True)
    grad_values = scale_row * (scaled - jnp.mean(scaled, -1, keepdims=True) - normal * inner)
    return grad_values, jnp.sum(grads * normal, 0), jnp.sum(grads, 0)


def gelu_pair(u):
    half_erf = 0.5 * (1.0 + lax.erf(u * (0.5**0.5)))
    density = jnp.exp(-0.5 * u * u) * ((2.0 * np.pi) ** -0.5)
    return (u * half_erf).astype(BRAIN), (half_erf + u * density).astype(BRAIN)


def cross_probs(queries, keys, first, head):
    mine = first if head == 0 else jnp.logical_not(first)
    masked = jnp.where(mine, queries, 0.0).astype(BRAIN)
    s = dot_nt(masked, keys)
    e = jnp.exp(s - jnp.max(s, 1, keepdims=True))
    return masked, mine, e / jnp.sum(e, 1, keepdims=True)


def cross_kernel(q_ref, k_ref, v_ref, o_ref):
    first = lax.broadcasted_iota(jnp.int32, (2 * ROWS, LANES), 1) < HEAD_DIM
    for start in range(0, q_ref.shape[0], 2 * ROWS):
        rows = pl.ds(start, 2 * ROWS)
        queries = q_ref[rows, :].astype(FLOAT) * SCALE
        outs = []
        for head in range(2):
            _, _, probs = cross_probs(queries, k_ref[...], first, head)
            outs.append(dot_nn(probs.astype(BRAIN), v_ref[...]))
        o_ref[rows, :] = jnp.where(first, outs[0], outs[1]).astype(BRAIN)


def cross_back_kernel(q_ref, k_ref, v_ref, do_ref, dq_ref, dk_ref, dv_ref):
    first = lax.broadcasted_iota(jnp.int32, (2 * ROWS, LANES), 1) < HEAD_DIM
    dk = jnp.zeros(k_ref.shape, FLOAT)
    dv = jnp.zeros(v_ref.shape, FLOAT)
    for start in range(0, q_ref.shape[0], 2 * ROWS):
        rows = pl.ds(start, 2 * ROWS)
        queries = q_ref[rows, :].astype(FLOAT) * SCALE
        grads = do_ref[rows, :].astype(FLOAT)
        dqs = []
        for head in range(2):
            q_m, mine, probs = cross_probs(queries, k_ref[...], first, head)
            do_m = jnp.where(mine, grads, 0.0).astype(BRAIN)
            dp = dot_nt(do_m, v_ref[...])
            ds = (probs * (dp - jnp.sum(probs * dp, 1, keepdims=True))).astype(BRAIN)
            dqs.append(dot_nn(ds, k_ref[...]))
            dk = dk + dot_tn(ds, q_m)
            dv = dv + dot_tn(probs.astype(BRAIN), do_m)
        dq_ref[rows, :] = (jnp.where(first, dqs[0], dqs[1]) * SCALE).astype(BRAIN)
    dk_ref[...] = dk.astype(BRAIN)
    dv_ref[...] = dv.astype(BRAIN)


def attend_cross(q, k, v):
    tall = pl.BlockSpec((q.shape[0], LANES), lambda p: (0, p))
    short = pl.BlockSpec((k.shape[0], LANES), lambda p: (0, p))
    return pl.pallas_call(
        cross_kernel,
        grid=(q.shape[1] // LANES,),
        in_specs=[tall, short, short],
        out_specs=tall,
        out_shape=jax.ShapeDtypeStruct(q.shape, BRAIN),
        compiler_params=pltpu.CompilerParams(vmem_limit_bytes=32 * 2**20),
        name="cross",
    )(q, k, v)


def attend_cross_back(q, k, v, do):
    tall = pl.BlockSpec((q.shape[0], LANES), lambda p: (0, p))
    short = pl.BlockSpec((k.shape[0], LANES), lambda p: (0, p))
    return pl.pallas_call(
        cross_back_kernel,
        grid=(q.shape[1] // LANES,),
        in_specs=[tall, short, short, tall],
        out_specs=[tall, short, short],
        out_shape=[jax.ShapeDtypeStruct(t.shape, BRAIN) for t in (q, k, v)],
        compiler_params=pltpu.CompilerParams(vmem_limit_bytes=32 * 2**20),
        name="cross_back",
    )(q, k, v, do)


def on_device(
    inputs, text_states, teacher, valid_frames,
    self_norm_gain, self_norm_bias, self_query, self_key, self_value, self_out,
    cross_norm_gain, cross_norm_bias, cross_query, cross_key, cross_value, cross_out,
    feed_norm_gain, feed_norm_bias, feed_in, feed_out,
):
    at_core, at_y = lax.axis_index("c"), lax.axis_index("y")
    real, width = inputs.shape[1], inputs.shape[2]
    half = -(-real // ROWS) * ROWS
    block, share = self_query.shape
    hidden = feed_in.shape[1]

    fits = ring_fit()

    tiny = [self_norm_gain, self_norm_bias, cross_norm_gain, cross_norm_bias, feed_norm_gain, feed_norm_bias]
    count = jnp.sum(valid_frames)
    digits = jnp.stack([count // 64, count % 64]).astype(BRAIN)
    digits = jnp.where((jnp.arange(block) == 0)[:, None], digits[None, :], jnp.zeros((), BRAIN))
    tiny = jnp.pad(jnp.concatenate([jnp.stack(tiny, 1), digits], 1), ((0, 0), (0, LANES - 8)))
    weights = [
        tiny, self_query, self_key, self_value, self_out.T, cross_query, cross_key, cross_value, cross_out.T
    ]
    wide = [swap_weight(v) for v in (feed_in, feed_out.T)]

    def both(own):
        return jnp.concatenate([own, swap_core(own)], 0)

    def summed(left, weight):
        far = dot_nt(left[half:], weight).astype(BRAIN)
        got = swap_core(far)
        return dot_nt(left[:half], weight) + got.astype(FLOAT)

    def padded(v):
        return jnp.pad(v, ((0, half - real), (0, 0)))

    frames = padded(inputs[0])
    flags = jnp.pad(valid_frames[0][:, None].astype(BRAIN), ((0, 0), (0, LANES - 1)))
    target = padded(jnp.concatenate([teacher[0], flags], 1))
    if fits:
        slots = slots_of([v.shape[1] for v in weights])
        frames, *wide = lax.optimization_barrier((frames, *wide))
        *weights, x_own, text, target, gains, h1, q1, k1, v1, o1, lse1 = gather(
            weights, frames, text_states[0], target, real, slots
        )
        weights = [joined(v) for v in weights]
    else:
        weights = [lax.all_gather(swap_clip(v), CHIPS, axis=0, tiled=True) for v in weights]
        x_own, text, target = (swap_clip(v) for v in (frames, text_states[0], target))
        gains = weights[0].T.astype(FLOAT)
        x_all = jnp.concatenate([x_own, swap_core(x_own)], 0)
        h1 = normalize(x_all.astype(FLOAT), gains[0], gains[1]).astype(BRAIN)
        q1, k1, v1 = (dot_nn(h1, w).astype(BRAIN) for w in weights[1:4])
        o1, lse1 = attend_self(q1, k1, v1, real)
    tiny, w_q, w_k, w_v, w_so, w_cq, w_ck, w_cv, w_co = weights
    w_fi, w_fo = (lax.all_gather(v, CHIPS, axis=0, tiled=True) for v in wide)
    counted = jnp.sum(tiny[:, 6:8].astype(FLOAT), 0)
    counted = counted[0] * 64.0 + counted[1]
    token_count = counted + swap_core(counted)
    valid = target[:, width : width + 1].astype(FLOAT)
    target = target[:, :width].astype(FLOAT)
    x0 = x_own.astype(FLOAT)
    x1 = x0 + summed(o1, w_so)
    h2 = both(normalize(x1, gains[2], gains[3]).astype(BRAIN))
    q2 = dot_nn(h2, w_cq).astype(BRAIN)
    k2 = dot_nn(text, w_ck).astype(BRAIN)
    v2 = dot_nn(text, w_cv).astype(BRAIN)
    o2 = attend_cross(q2, k2, v2)
    x2 = x1 + summed(o2, w_co)
    h3 = both(normalize(x2, gains[4], gains[5]).astype(BRAIN))
    g, slope = gelu_pair(dot_nn(h3, w_fi))
    y = x2 + summed(g, w_fo)
    home = y.astype(BRAIN)
    deviation = y - target
    error = jnp.sum(valid * deviation * deviation)
    tokens_all = real * lax.axis_size(("z", "x", "c", "y"))
    dy = (2.0 * tokens_all / token_count) * valid * deviation

    dyb = both(dy.astype(BRAIN))
    fo_grad = dot_tn(dyb, g).astype(BRAIN)
    dyb, fo_grad = lax.optimization_barrier((dyb, fo_grad))
    fo_grad = lax.psum_scatter(fo_grad, CHIPS, scatter_dimension=0, tiled=True)
    du = (slope.astype(FLOAT) * dot_nn(dyb, w_fo)).astype(BRAIN)
    fi_grad = dot_tn(h3, du).astype(BRAIN)
    fi_grad = lax.psum_scatter(fi_grad, CHIPS, scatter_dimension=0, tiled=True)
    term, gain3, bias3 = norm_back(x2, gains[4], summed(du, w_fi))
    dx2 = dy + term
    dx2b = both(dx2.astype(BRAIN))
    co_grad = dot_tn(dx2b, o2).astype(BRAIN)
    do2 = dot_nn(dx2b, w_co).astype(BRAIN)
    dq2, dk2, dv2 = attend_cross_back(q2, k2, v2, do2)
    cq_grad = dot_tn(h2, dq2).astype(BRAIN)
    ck_grad = dot_tn(text, dk2).astype(BRAIN)
    cv_grad = dot_tn(text, dv2).astype(BRAIN)
    text_part = (dot_nt(dk2, w_ck) + dot_nt(dv2, w_cv)).astype(BRAIN)
    text_mine = jnp.where(at_core == 0, text_part[:, : width // 2], text_part[:, width // 2 :])
    text_far = jnp.where(at_core == 0, text_part[:, width // 2 :], text_part[:, : width // 2])
    text_sum = text_mine.astype(FLOAT) + swap_core(text_far).astype(FLOAT)
    text_grad = swap_clip(text_sum.astype(BRAIN)).astype(FLOAT)[None]
    term, gain2, bias2 = norm_back(x1, gains[2], summed(dq2, w_cq))
    dx1 = dx2 + term
    dx1b = both(dx1.astype(BRAIN))
    so_grad = dot_tn(dx1b, o1).astype(BRAIN)
    do1 = dot_nn(dx1b, w_so).astype(BRAIN)
    zero = jnp.zeros((width,), FLOAT)
    vectors = jnp.stack([zero, zero, gain2, bias2, gain3, bias3])
    vectors = jnp.concatenate([vectors, jnp.full((2, width), error)], 0)
    grads = [co_grad, cq_grad, ck_grad, cv_grad, so_grad]
    if fits:
        slots = slots_of([v.shape[1] for v in grads] + [share] * 3, six=((2, 2, 2),))
        *grads, home, frames, vectors = sum_gradients(
            [by_chip(v) for v in grads], home, (q1, k1, v1, do1, o1), h1,
            [by_chip(v) for v in (w_q, w_k, w_v)], x_own, dx1, lse1, gains, vectors, real, slots,
        )
    else:
        dq1, dk1, dv1 = attend_self_back(q1, k1, v1, do1, o1, lse1, real)
        dh1 = dot_nt(dq1, w_q) + dot_nt(dk1, w_k) + dot_nt(dv1, w_v)
        dh1 = dh1[:half] + swap_core(dh1[half:].astype(BRAIN)).astype(FLOAT)
        term, gain1, bias1 = norm_back(x0, gains[0], dh1)
        frames = swap_clip((dx1 + term).astype(BRAIN))
        grads += [dot_tn(h1, d).astype(BRAIN) for d in (dq1, dk1, dv1)]
        grads = [swap_clip(lax.psum_scatter(v, CHIPS, scatter_dimension=0, tiled=True)) for v in grads]
        home = swap_clip(home)
        vectors = lax.psum(vectors.at[:2].set(jnp.stack([gain1, bias1])), ("z", "x", "c", "y"))
    layer_out = home[:real][None]
    inputs_grad = frames[None].astype(FLOAT)[:, :real]
    co_grad, cq_grad, ck_grad, cv_grad, so_grad, q_grad, k_grad, v_grad = (v.astype(FLOAT) for v in grads)
    fi_grad, fo_grad = swap_weight(fi_grad).astype(FLOAT), swap_weight(fo_grad).astype(FLOAT).T
    loss = vectors[6, 0] / (width * token_count)
    mine = block // 2
    place = (lax.axis_index(("z", "x", "c")) * 2 + at_y) * mine
    norms = lax.dynamic_slice(vectors, (0, place), (8, mine))
    return (
        loss, layer_out, inputs_grad, text_grad,
        norms[0], norms[1], q_grad, k_grad, v_grad, so_grad.T,
        norms[2], norms[3], cq_grad, ck_grad, cv_grad, co_grad.T,
        norms[4], norms[5], fi_grad, fo_grad,
    )


def solution(mesh):
    outer = mesh.shape["dp"] // 4
    fine = Mesh(np.array(mesh.devices).reshape(outer, 2, 2, 2), ("z", "x", "c", "y"))
    dp = ("z", "x", "c")
    frames = P(dp, "y", None)
    vector, wide, tall = P(dp), P(dp, "y"), P("y", dp)
    small = P(("z", "x", "c", "y"))
    attention = (vector, vector, wide, wide, wide, tall)
    return jax.shard_map(
        on_device,
        mesh=fine,
        in_specs=(frames, P(dp, None, None), frames, P(dp, "y"), *attention, *attention, vector, vector, wide, tall),
        out_specs=(
            P(), frames, frames, P(dp, None, "y"),
            small, small, wide, wide, wide, tall,
            small, small, wide, wide, wide, tall,
            small, small, wide, tall,
        ),
        check_vma=False,
    )
```
